32 devices in a mesh: tile: 16 (over z, x, core), mp: 2 (over y).
Axes of the slice: x: 2, y: 2, z: 4, core: 2. Of those that a mesh axis runs over, the one named last changes fastest.
Arguments:
- lo_in: bfloat16 [2, 384, 24, 1024], P(None, 'tile', None, 'mp'), may hold values from -6 to 6
- hi_in: bfloat16 [2, 768, 2, 36864], P(None, 'tile', 'mp'), may hold values from -6 to 6
- image_ids: int32 [2, 384], replicated, may hold values from 0 to 31, never falling along the last dimension, each value on 1 to 24 neighbouring positions
- cn_kernel: bfloat16 [49, 1536], P(None, 'mp'), may hold values from -0.875 to 0.875
- cn_gain: bfloat16 [1536], replicated, may hold values from 0.5 to 1.5
- cn_w1: bfloat16 [1536, 6144], P('tile', 'mp'), may hold values from -0.15625 to 0.15625
- cn_w2: bfloat16 [6144, 1536], P('mp', 'tile'), may hold values from -0.078125 to 0.078125
- cn_scale: bfloat16 [1536], P('mp'), may hold values from 0.29882812 to 1.5
- ad_proj: bfloat16 [1536, 1024], P('tile', 'mp'), may hold values from -0.15625 to 0.15625
- ad_kernel: bfloat16 [9, 1024], P(None, 'mp'), may hold values from -2 to 2
- gate_w1: bfloat16 [1536, 768], P('tile', 'mp'), may hold values from -0.15625 to 0.15625
- gate_w2: bfloat16 [768, 1024], P('mp', 'tile'), may hold values from -0.21875 to 0.21875
- ln1_gain: bfloat16 [1024], replicated, may hold values from 0.5 to 1.5
- qkv: bfloat16 [3, 1024, 1024], P(None, 'tile', 'mp'), may hold values from -0.1875 to 0.1875
- out_proj: bfloat16 [1024, 1024], P('mp', 'tile'), may hold values from -0.75 to 0.75
- ln2_gain: bfloat16 [1024], replicated, may hold values from 0.5 to 1.5
- fc1: bfloat16 [1024, 4096], P('tile', 'mp'), may hold values from -0.1875 to 0.1875
- fc2: bfloat16 [4096, 1024], P('mp', 'tile'), may hold values from -0.09375 to 0.09375
- d_lo_out: bfloat16 [2, 384, 24, 1024], P(None, 'tile', None, 'mp'), may hold values from -6 to 6
- d_hi_out: bfloat16 [2, 768, 2, 36864], P(None, 'tile', 'mp'), may hold values from -6 to 6
Outputs:
- lo_out: bfloat16 [2, 384, 24, 1024], P(None, 'tile', None, 'mp')
- hi_out: bfloat16 [2, 768, 2, 36864], P(None, 'tile', 'mp')
- grad_lo: float32 [2, 384, 24, 1024], P(None, 'tile', None, 'mp')
- grad_hi: float32 [2, 768, 2, 36864], P(None, 'tile', 'mp')
- g_cn_kernel: float32 [49, 1536], P(None, 'mp')
- g_cn_gain: float32 [1536], replicated
- g_cn_w1: float32 [1536, 6144], P('tile', 'mp')
- g_cn_w2: float32 [6144, 1536], P('mp', 'tile')
- g_cn_scale: float32 [1536], P('mp')
- g_ad_proj: float32 [1536, 1024], P('tile', 'mp')
- g_ad_kernel: float32 [9, 1024], P(None, 'mp')
- g_gate_w1: float32 [1536, 768], P('tile', 'mp')
- g_gate_w2: float32 [768, 1024], P('mp', 'tile')
- g_ln1_gain: float32 [1024], replicated
- g_qkv: float32 [3, 1024, 1024], P(None, 'tile', 'mp')
- g_out_proj: float32 [1024, 1024], P('mp', 'tile')
- g_ln2_gain: float32 [1024], replicated
- g_fc1: float32 [1024, 4096], P('tile', 'mp')
- g_fc2: float32 [4096, 1024], P('mp', 'tile')
The draws below stay inside these ranges and needn't reach their ends.
Inputs may be any that keep to these rules, and one draw needn't show every extreme that they name: `image_ids`: image numbers never fall along a canvas; each image covers 1 to 24 whole consecutive rows, and some image covers exactly 24.
All inputs are finite; a program needn't handle non-finite values.
Results may differ from the reference program's by a relative error of at most 0.03.
Values may be sent and summed in bfloat16 or wider, within the bound.
No kernel may reach another device: no remote copies, remote signals or barrier semaphores. Data moves between devices by JAX's collectives and lax.ppermute only.
A program may use at most 832 MiB of HBM per device.

```python
import math
import jax
import jax.numpy as jnp
import numpy as np
from jax import lax

D = 1024
HEADS = 16
HDIM = 64
FF = 4096
CH = 1536
CHID = 6144
GH = 768
IMG_ROWS = 24
LCOLS = 24
ROWS_DEV = 24
MICRO = 2
LROWS = 384
HROWS = 768
HCOLS = 48
IMAGES = 32
GROUPS = 2
CGRP = 768


def steps_of(own_key, shape, shards, low, high):
    factor_of, own = 1.0, jax.random.fold_in(own_key, 6)
    for position, parts in shards:
        steps = jnp.exp(jax.random.uniform(jax.random.fold_in(own, position), (parts,), jnp.float32, low / len(shards), high / len(shards)))
        factor_of = factor_of * jnp.repeat(steps, shape[position] // parts).reshape([-1 if axis == position else 1 for axis in range(len(shape))])
    return factor_of


def profile(count, total, reach, slope):
    loads = [(1 << 20) // math.isqrt(grade ** slope) + 1 for grade in range(2, count + 1)]
    rest, holding = total - reach - (count - 1), [1] * (count - 1)
    while rest > 0:
        free = [i for i in range(count - 1) if holding[i] < reach]
        pool, remaining = sum([loads[i] for i in free]), rest
        for i in free:
            addition = min(reach - holding[i], max(1, remaining * loads[i] // pool), rest)
            holding[i] = holding[i] + addition
            rest = rest - addition
    return np.array([reach] + holding)


def ragged_sizes(own_key, number_of, total, bound, slope):
    if number_of == 2:
        one = jax.random.randint(own_key, (), max(1, total - bound), min(bound, total - 1) + 1)
        return jnp.stack([one, total - one])
    lengths = jnp.asarray(profile(number_of, total, bound, slope), jnp.int32)
    couples = (number_of - 1) // 2
    source_of, receiver = lengths[1:1 + 2 * couples:2], lengths[2:2 + 2 * couples:2]
    room = jnp.minimum(source_of - 1, bound - receiver)
    moved = jax.random.randint(jax.random.fold_in(own_key, 1), (couples,), 0, 1 << 20) % (room + 1)
    lengths = lengths.at[1:1 + 2 * couples:2].set(source_of - moved).at[2:2 + 2 * couples:2].set(receiver + moved)
    return lengths[jax.random.permutation(jax.random.fold_in(own_key, 2), number_of)]


def bell_draw(key, shape, spread, most, split=(), kind=jnp.bfloat16):
    array = spread * jax.random.normal(key, shape, jnp.float32)
    if split:
        array = array * steps_of(key, shape, split, -0.22, 0.18)
    return jnp.clip(array, -most, most).astype(kind)


def setup_inputs(seed: int = 0) -> dict:
    key_of = jax.random.split(jax.random.key(seed), 21)
    return {
        "lo_in": bell_draw(key_of[0], (MICRO, LROWS, LCOLS, D), 1.0, 6.0, ((1, 16), (3, 2))),
        "hi_in": bell_draw(key_of[1], (MICRO, HROWS, GROUPS, HCOLS * CGRP), 1.0, 6.0, ((1, 16), (2, 2))),
        "image_ids": jax.vmap(lambda own: jnp.searchsorted(jnp.cumsum(ragged_sizes(own, IMAGES, LROWS, IMG_ROWS, 2)), jnp.arange(LROWS), side="right"))(jax.random.split(key_of[2], MICRO)).reshape((MICRO, LROWS)).astype(jnp.int32),
        "cn_kernel": bell_draw(key_of[3], (49, CH), 49 ** -0.5, 0.875, ((1, 2),)),
        "cn_gain": jnp.clip(1.0 + 0.1 * jax.random.normal(key_of[4], (CH,), jnp.float32), 0.5, 1.5).astype(jnp.bfloat16),
        "cn_w1": bell_draw(key_of[5], (CH, CHID), CH ** -0.5, 0.15625, ((0, 16), (1, 2))),
        "cn_w2": bell_draw(key_of[6], (CHID, CH), CHID ** -0.5, 0.078125, ((0, 2), (1, 16))),
        "cn_scale": jnp.clip(jnp.exp(math.log(1.5) - 1.6133518 * jax.random.uniform(key_of[7], (CH,), jnp.float32) ** steps_of(key_of[7], (CH,), ((0, 2),), -0.2, 0.2)), 0.29882812, 1.5).astype(jnp.bfloat16),
        "ad_proj": bell_draw(key_of[8], (CH, D), CH ** -0.5, 0.15625, ((0, 16), (1, 2))),
        "ad_kernel": bell_draw(key_of[9], (9, D), 9 ** -0.5, 2.0, ((1, 2),)),
        "gate_w1": bell_draw(key_of[10], (CH, GH), CH ** -0.5, 0.15625, ((0, 16), (1, 2))),
        "gate_w2": bell_draw(key_of[11], (GH, D), GH ** -0.5, 0.21875, ((0, 2), (1, 16))),
        "ln1_gain": jnp.clip(1.0 + 0.1 * jax.random.normal(key_of[12], (D,), jnp.float32), 0.5, 1.5).astype(jnp.bfloat16),
        "qkv": bell_draw(key_of[13], (3, D, D), D ** -0.5, 0.1875, ((1, 16), (2, 2))),
        "out_proj": bell_draw(key_of[14], (D, D), (D // 16) ** -0.5, 0.75, ((0, 2), (1, 16))),
        "ln2_gain": jnp.clip(1.0 + 0.1 * jax.random.normal(key_of[15], (D,), jnp.float32), 0.5, 1.5).astype(jnp.bfloat16),
        "fc1": bell_draw(key_of[16], (D, FF), D ** -0.5, 0.1875, ((0, 16), (1, 2))),
        "fc2": bell_draw(key_of[17], (FF, D), FF ** -0.5, 0.09375, ((0, 2), (1, 16))),
        "d_lo_out": bell_draw(key_of[18], (MICRO, LROWS, LCOLS, D), 1.0, 6.0, ((1, 16), (3, 2))),
        "d_hi_out": bell_draw(key_of[19], (MICRO, HROWS, GROUPS, HCOLS * CGRP), 1.0, 6.0, ((1, 16), (2, 2))),
    }


EPS = 1e-06
HIGH = lax.Precision.HIGHEST

@jax.custom_vjp
def low(v):
    return lax.optimization_barrier(v.astype(jnp.bfloat16)).astype(jnp.float32)

@jax.custom_vjp
def low_back(v):
    return v

def low_keep(v):
    return (low(v), None)

def low_pass(kept, grad):
    return (grad,)

def back_keep(v):
    return (v, None)

def back_low(kept, grad):
    return (low(grad),)
low.defvjp(low_keep, low_pass)
low_back.defvjp(back_keep, back_low)

def matmul(left, right):
    return jnp.dot(left, right, precision=HIGH, preferred_element_type=jnp.float32)

def layer_norm(values, gain_vec):
    average = lax.optimization_barrier(jnp.mean(values, axis=-1, keepdims=True))
    centered = values - average
    variance = lax.optimization_barrier(jnp.mean(centered * centered, axis=-1, keepdims=True))
    return centered * lax.rsqrt(variance + EPS) * gain_vec

def gelu_exact(values):
    return jax.nn.gelu(values, approximate=False)

def to_channels(grouped):
    return grouped.reshape(MICRO, HROWS, GROUPS, HCOLS, CGRP).transpose(0, 1, 3, 2, 4).reshape(MICRO, HROWS, HCOLS, CH)

def to_groups(plain):
    return plain.reshape(MICRO, HROWS, HCOLS, GROUPS, CGRP).transpose(0, 1, 3, 2, 4).reshape(MICRO, HROWS, GROUPS, HCOLS * CGRP)

def depthwise(field, kernel, labels, tap_size):
    margin = tap_size // 2
    row_count, col_count = (field.shape[0], field.shape[1])
    padded = jnp.pad(field, ((margin, margin), (margin, margin), (0, 0)))
    label_pad = jnp.pad(labels, (margin, margin), constant_values=-1)
    summed = jnp.zeros(field.shape, field.dtype)
    for a in range(tap_size):
        same_img = (label_pad[a:a + row_count] == labels)[:, None, None]
        shifted = jnp.where(same_img, padded[a:a + row_count], 0.0)
        for b in range(tap_size):
            summed = summed + kernel[a * tap_size + b] * shifted[:, b:b + col_count]
    return summed

def depthwise_window(window, kernel, label_win, tap_size):
    margin = tap_size // 2
    row_count = window.shape[0] - 2 * margin
    col_count = window.shape[1]
    widened = jnp.pad(window, ((0, 0), (margin, margin), (0, 0)))
    labels_mid = label_win[margin:margin + row_count]
    summed = jnp.zeros((row_count, col_count, window.shape[2]), window.dtype)
    for a in range(tap_size):
        same_img = (label_win[a:a + row_count] == labels_mid)[:, None, None]
        shifted = jnp.where(same_img, widened[a:a + row_count], 0.0)
        for b in range(tap_size):
            summed = summed + kernel[a * tap_size + b] * shifted[:, b:b + col_count]
    return summed

def hi_block(window, label_win, cn_kernel, cn_gain, cn_w1, cn_w2, cn_scale):
    row_count = window.shape[0] - 6
    conv_out = low_back(low(depthwise_window(window, cn_kernel, label_win, 7)))
    normed = low(low_back(layer_norm(conv_out, cn_gain)))
    flat = normed.reshape(-1, normed.shape[-1])
    inner_act = low(gelu_exact(low_back(matmul(flat, cn_w1))))
    branch = low_back(matmul(inner_act, cn_w2)).reshape(conv_out.shape)
    return window[3:3 + row_count] + cn_scale * branch

def attention(query_grid, key_grid, value_grid, labels):
    row_count, col_count, width = query_grid.shape
    margin = IMG_ROWS - 1
    key_span = ROWS_DEV + 2 * margin
    key_pad = jnp.pad(key_grid, ((margin, margin), (0, 0), (0, 0)))
    value_pad = jnp.pad(value_grid, ((margin, margin), (0, 0), (0, 0)))
    label_pad = jnp.pad(labels, (margin, margin), constant_values=-1)
    attn_scale = HDIM ** (-0.5)

    def one_block(block_idx):
        first_row = block_idx * ROWS_DEV
        query_blk = lax.dynamic_slice_in_dim(query_grid, first_row, ROWS_DEV, 0).reshape(ROWS_DEV * col_count, HEADS, HDIM)
        key_blk = lax.dynamic_slice_in_dim(key_pad, first_row, key_span, 0).reshape(key_span * col_count, HEADS, HDIM)
        value_blk = lax.dynamic_slice_in_dim(value_pad, first_row, key_span, 0).reshape(key_span * col_count, HEADS, HDIM)
        query_lab = jnp.repeat(lax.dynamic_slice_in_dim(labels, first_row, ROWS_DEV, 0), col_count)
        key_lab = jnp.repeat(lax.dynamic_slice_in_dim(label_pad, first_row, key_span, 0), col_count)
        scores = low_back(jnp.einsum('qhd,khd->hqk', query_blk, key_blk, precision=HIGH) * attn_scale)
        allowed = (query_lab[:, None] == key_lab[None, :])[None]
        weights = low(jax.nn.softmax(jnp.where(allowed, scores, -1e+30), axis=-1))
        result = jnp.einsum('hqk,khd->qhd', weights, value_blk, precision=HIGH)
        return result.reshape(ROWS_DEV, col_count, width)
    blocks = lax.map(jax.checkpoint(one_block), jnp.arange(row_count // ROWS_DEV, dtype=jnp.int32))
    return blocks.reshape(row_count, col_count, width)

def forward(lo_field, hi_field, labels, cn_kernel, cn_gain, cn_w1, cn_w2, cn_scale, ad_proj, ad_kernel, gate_w1, gate_w2, ln1_gain, qkv, out_proj, ln2_gain, fc1, fc2):
    hi_rows, hi_cols, channels = hi_field.shape
    lo_rows, lo_cols, width = lo_field.shape
    hi_labels = jnp.repeat(labels, 2)
    block_rows = math.gcd(hi_rows, 16)
    block_count = hi_rows // block_rows
    hi_pad = jnp.pad(hi_field, ((3, 3), (0, 0), (0, 0)))
    label_pad = jnp.pad(hi_labels, (3, 3), constant_values=-1)
    window_idx = jnp.arange(block_count, dtype=jnp.int32)[:, None] * block_rows + jnp.arange(block_rows + 6, dtype=jnp.int32)[None, :]
    windows = hi_pad[window_idx]
    label_wins = label_pad[window_idx]

    def run_block(items):
        return hi_block(items[0], items[1], cn_kernel, cn_gain, cn_w1, cn_w2, cn_scale)
    hi_sum = lax.map(jax.checkpoint(run_block), (windows, label_wins)).reshape(hi_field.shape)
    pooled = low(lax.optimization_barrier(jnp.mean(hi_sum.reshape(lo_rows, 2, lo_cols, 2, channels), axis=(1, 3))))
    flat_pool = pooled.reshape(lo_rows * lo_cols, channels)
    proj_low = low(low_back(matmul(flat_pool, ad_proj))).reshape(lo_rows, lo_cols, width)
    local_conv = low_back(depthwise(proj_low, ad_kernel, labels, 3))
    gate_hidden = low(gelu_exact(low_back(matmul(flat_pool, gate_w1))))
    gate_val = jnp.tanh(low_back(matmul(gate_hidden, gate_w2))).reshape(lo_field.shape)
    mixed_one = (lo_field + gate_val * local_conv).reshape(lo_rows * lo_cols, width)
    norm_one = low(low_back(layer_norm(low(mixed_one), ln1_gain)))
    query_grid = low(low_back(matmul(norm_one, qkv[0]))).reshape(lo_field.shape)
    key_grid = low(low_back(matmul(norm_one, qkv[1]))).reshape(lo_field.shape)
    value_grid = low(low_back(matmul(norm_one, qkv[2]))).reshape(lo_field.shape)
    attended = low(low_back(attention(query_grid, key_grid, value_grid, labels))).reshape(lo_rows * lo_cols, width)
    mixed_two = mixed_one + low_back(matmul(attended, out_proj))
    norm_two = low(low_back(layer_norm(low(mixed_two), ln2_gain)))
    ff_hidden = low(gelu_exact(low_back(matmul(norm_two, fc1))))
    lo_result = mixed_two + low_back(matmul(ff_hidden, fc2))
    return (lo_result.reshape(lo_field.shape), hi_sum)

def reference(lo_in, hi_in, image_ids, cn_kernel, cn_gain, cn_w1, cn_w2, cn_scale, ad_proj, ad_kernel, gate_w1, gate_w2, ln1_gain, qkv, out_proj, ln2_gain, fc1, fc2, d_lo_out, d_hi_out):
    hi_map = to_channels(hi_in)
    hi_cot = to_channels(d_hi_out)
    params = tuple((item.astype(jnp.float32) for item in (cn_kernel, cn_gain, cn_w1, cn_w2, cn_scale, ad_proj, ad_kernel, gate_w1, gate_w2, ln1_gain, qkv, out_proj, ln2_gain, fc1, fc2)))
    totals = tuple((jnp.zeros(item.shape, jnp.float32) for item in params))
    lo_list, hi_list, glo_list, ghi_list = ([], [], [], [])
    for micro_idx in range(MICRO):
        labels = image_ids[micro_idx]

        def run_layer(lo_field, hi_field, *weights):
            return forward(lo_field, hi_field, labels, *weights)
        outputs, pull_back = jax.vjp(run_layer, lo_in[micro_idx].astype(jnp.float32), hi_map[micro_idx].astype(jnp.float32), *params)
        grads = pull_back((d_lo_out[micro_idx].astype(jnp.float32), hi_cot[micro_idx].astype(jnp.float32)))
        lo_list.append(outputs[0].astype(jnp.bfloat16))
        hi_list.append(outputs[1].astype(jnp.bfloat16))
        glo_list.append(grads[0])
        ghi_list.append(grads[1])
        totals = tuple((acc + part for acc, part in zip(totals, grads[2:])))
    return (jnp.stack(lo_list), to_groups(jnp.stack(hi_list)), jnp.stack(glo_list), to_groups(jnp.stack(ghi_list)), totals[0], totals[1], totals[2], totals[3], totals[4], totals[5], totals[6], totals[7], totals[8], totals[9], totals[10], totals[11], totals[12], totals[13], totals[14])
```

```python
import jax
import jax.numpy as jnp
import numpy as np
from jax import lax
from jax.experimental import pallas as pl
from jax.experimental.pallas import tpu as pltpu
from jax.sharding import Mesh
from jax.sharding import PartitionSpec as P

HDIM = 64
IMG_ROWS = 24
HCOLS = 48

EPS = 1e-06
NEG = -1e30
BF = jnp.bfloat16
F32 = jnp.float32
ALL = ("mb", "tile")


def rim_pair(value, width, axis):
    devices, length = lax.axis_size("tile"), value.shape[axis]
    up = [(i, (i + 1) % devices) for i in range(devices - 1)]
    down = [(j, i) for i, j in up]
    before = lax.ppermute(lax.slice_in_dim(value, length - width, length, axis=axis), "tile", up)
    after = lax.ppermute(lax.slice_in_dim(value, 0, width, axis=axis), "tile", down)
    return before, after


def rim_rows(value, width):
    devices, length = lax.axis_size("tile"), value.shape[0]
    up = [(i, (i + 1) % devices) for i in range(devices - 1)]
    down = [(j, i) for i, j in up]
    before = lax.ppermute(value[length - width :], "tile", up)
    after = lax.ppermute(value[:width], "tile", down)
    return jnp.concatenate([before, value, after], axis=0)


def matmul(left, right):
    return jnp.dot(left, right, preferred_element_type=F32)


def matmul_tn(left, right):
    return lax.dot_general(left, right, (((0,), (0,)), ((), ())), preferred_element_type=F32)


def matmul_nt(left, right):
    return lax.dot_general(left, right, (((1,), (1,)), ((), ())), preferred_element_type=F32)


def layer_norm(values, gain_vec):
    average = jnp.mean(values, axis=-1, keepdims=True)
    centered = values - average
    variance = jnp.mean(centered * centered, axis=-1, keepdims=True)
    return centered * lax.rsqrt(variance + EPS) * gain_vec


def gelu_pair(values):
    cdf = 0.5 + 0.5 * lax.erf(values * 0.7071067811865476)
    slope = cdf + values * (0.3989422804014327 * jnp.exp(-0.5 * values * values))
    return (values * cdf).astype(BF), slope.astype(BF)


def features(values):
    parts = lax.axis_size("tp")
    if parts == 1:
        return values
    rows, width = values.shape
    full = lax.all_gather(values.reshape(rows, 2, width // 2), "tp", axis=2)
    return full.reshape(rows, parts * width)


def partial_sums(values):
    parts = lax.axis_size("tp")
    if parts == 1:
        return values
    rows, width = values.shape
    split = values.reshape(rows, 2, parts, width // (2 * parts))
    return lax.psum_scatter(split, "tp", scatter_dimension=2).reshape(rows, width // parts)


def own_slice(values):
    parts = lax.axis_size("tp")
    if parts == 1:
        return values
    rows, width = values.shape
    split = values.reshape(rows, 2, parts, width // (2 * parts))
    own = lax.dynamic_index_in_dim(split, lax.axis_index("tp"), 2, keepdims=False)
    return own.reshape(rows, width // parts)


SWAP = [(0, 1), (1, 0)]


def swap_micro(values):
    mine = lax.axis_index("mb")
    own = lax.dynamic_index_in_dim(values, mine, 0, keepdims=False)
    sent = lax.dynamic_index_in_dim(values, 1 - mine, 0, keepdims=False)
    return own, lax.ppermute(sent, "mb", SWAP)


def in_order(own, other, axis):
    first = lax.axis_index("mb") == 0
    return jnp.concatenate(
        [jnp.where(first, own, other), jnp.where(first, other, own)], axis=axis
    )


def both_micro(own, other):
    first = lax.axis_index("mb") == 0
    return jnp.stack([jnp.where(first, own, other), jnp.where(first, other, own)])


def halves(values):
    width = values.shape[-1] // 2
    mine = lax.axis_index("mb")
    own = lax.dynamic_slice_in_dim(values, mine * width, width, values.ndim - 1)
    sent = lax.dynamic_slice_in_dim(values, (1 - mine) * width, width, values.ndim - 1)
    return own, sent


def row_labels(labels, first_row, count_rows, margin):
    padded = jnp.pad(labels, (margin, margin), constant_values=-1)
    return lax.dynamic_slice_in_dim(padded, first_row, count_rows + 2 * margin, 0)


def depthwise(padded, kernel, ids_pad, ids_mid, tap_size, flipped):
    margin = tap_size // 2
    row_count = ids_mid.shape[0]
    col_count = padded.shape[1]
    widened = jnp.pad(padded, ((0, 0), (margin, margin), (0, 0)))
    summed = jnp.zeros((row_count, col_count, padded.shape[2]), F32)
    for a in range(tap_size):
        same_img = (ids_pad[a : a + row_count] == ids_mid)[:, None, None]
        shifted = jnp.where(same_img, widened[a : a + row_count].astype(F32), 0.0)
        for b in range(tap_size):
            tap_index = (
                (tap_size - 1 - a) * tap_size + (tap_size - 1 - b) if flipped else a * tap_size + b
            )
            summed = summed + kernel[tap_index].astype(F32) * shifted[:, b : b + col_count]
    return summed


def tap_grads(padded, grad_low, ids_pad, ids_mid, tap_size):
    margin = tap_size // 2
    row_count = ids_mid.shape[0]
    col_count = padded.shape[1]
    widened = jnp.pad(padded, ((0, 0), (margin, margin), (0, 0)))
    grad_vals = grad_low.astype(F32)
    results = []
    for a in range(tap_size):
        same_img = (ids_pad[a : a + row_count] == ids_mid)[:, None, None]
        shifted = jnp.where(same_img, widened[a : a + row_count].astype(F32), 0.0)
        for b in range(tap_size):
            results.append(jnp.sum(shifted[:, b : b + col_count] * grad_vals, axis=(0, 1)))
    return jnp.stack(results)


def gather_all(shard):
    full = lax.all_gather(shard, ALL, axis=0)
    return full.reshape(2, -1, shard.shape[1])


def reduce_all(first, second):
    both = jnp.concatenate([first.astype(BF), second.astype(BF)], axis=0)
    return lax.psum_scatter(both, ALL, scatter_dimension=0, tiled=True).astype(F32)


LANES = 128
RIM = 16
VMEM_LIMIT = 60 * 1024 * 1024


def conv_params(flops=0, moved=0):
    return dict(
        compiler_params=pltpu.CompilerParams(vmem_limit_bytes=VMEM_LIMIT),
        cost_estimate=pl.CostEstimate(flops=flops, bytes_accessed=moved, transcendentals=0),
    )


def masked_taps(taps_ref, mask_ref, km_ref, sub, flip):
    for a in range(7):
        seen = mask_ref[a, pl.ds(sub * 8, 8), :]
        for b in range(7):
            tap = 48 - (a * 7 + b) if flip else a * 7 + b
            km_ref[a * 7 + b] = taps_ref[tap : tap + 1, :] * seen


def conv_kernel(place_ref, x_ref, top_ref, bot_ref, taps_ref, mask_ref, out_ref, xs_ref, km_ref):
    rows, width = 48, x_ref.shape[1] // 48
    cb = pl.program_id(0)

    @pl.when(cb == 0)
    def _():
        for w in (0, 1, 2, 51, 52, 53):
            xs_ref[w] = jnp.zeros_like(xs_ref[w])

    def fill(w, carry):
        at = pl.ds(pl.multiple_of(w * width + cb * LANES, LANES), LANES)
        xs_ref[w + 3, 0:RIM, :] = top_ref[:, at].astype(F32)
        xs_ref[w + 3, RIM : RIM + rows, :] = x_ref[:, at].astype(F32)
        xs_ref[w + 3, RIM + rows :, :] = bot_ref[:, at].astype(F32)
        return carry

    lax.fori_loop(0, 48, fill, 0)

    def band(t, carry):
        for s in range(2):
            masked_taps(taps_ref, mask_ref, km_ref.at[s], t * 2 + s, False)

        def block(i, carry):
            w0 = i * 8
            accs = []
            for s in range(2):
                acc = [jnp.zeros((8, LANES), F32) for _ in range(8)]
                for a in range(7):
                    start = t * 16 + (s * 8 + RIM - 3 + a)
                    x = [xs_ref[w0 + j, pl.ds(start, 8), :] for j in range(14)]
                    for b in range(7):
                        k = km_ref[s, a * 7 + b]
                        for j in range(8):
                            acc[j] = acc[j] + k * x[j + b]
                accs.append(acc)
            for j in range(8):
                both = jnp.concatenate([accs[0][j], accs[1][j]], axis=0).astype(BF)
                out_ref[pl.ds(pl.multiple_of((w0 + j) * rows + t * 16, 16), 16), :] = both
            return carry

        lax.fori_loop(0, 6, block, 0)
        return carry

    lax.fori_loop(0, 3, band, 0)


def conv_forward(x, top, bot, taps, mask, place, into=None):
    width = x.shape[1] // 48
    blocks = width // LANES
    whole = lambda cb, place: (0, 0)
    half = lambda cb, place: (0, place[0] * blocks + cb)
    extra = [] if into is None else [into]
    kernel = conv_kernel if into is None else conv_kernel_into
    return pl.pallas_call(
        kernel,
        out_shape=jax.ShapeDtypeStruct((48 * 48, 2 * width), BF),
        grid_spec=pltpu.PrefetchScalarGridSpec(
            num_scalar_prefetch=1,
            grid=(blocks,),
            in_specs=[
                pl.BlockSpec(x.shape, whole),
                pl.BlockSpec(top.shape, whole),
                pl.BlockSpec(bot.shape, whole),
                pl.BlockSpec((49, LANES), half),
                pl.BlockSpec(mask.shape, lambda cb, place: (0, 0, 0)),
            ]
            + [pl.BlockSpec(memory_space=pl.ANY)] * len(extra),
            out_specs=pl.BlockSpec((48 * 48, LANES), half),
            scratch_shapes=[
                pltpu.VMEM((54, 80, LANES), F32),
                pltpu.VMEM((2, 49, 8, LANES), F32),
            ],
        ),
        input_output_aliases={} if into is None else {6: 0},
        **conv_params(2 * 49 * 48 * 48 * width * 8, 12_000_000),
    )(place, x, top, bot, taps, mask, *extra)


def conv_kernel_into(place_ref, x_ref, top_ref, bot_ref, taps_ref, mask_ref, into_ref, *rest):
    conv_kernel(place_ref, x_ref, top_ref, bot_ref, taps_ref, mask_ref, *rest)


def back_kernel(place_ref, g_ref, top_ref, bot_ref, x_ref, cot_ref, pool_ref, taps_ref, mask_ref,
                out_ref, tap_out_ref, gs_ref, km_ref, tacc_ref, sp_ref):
    rows, width = 48, x_ref.shape[1] // 48
    cb = pl.program_id(0)

    @pl.when(cb == 0)
    def _():
        for w in (0, 1, 2, 51, 52, 53):
            gs_ref[w] = jnp.zeros_like(gs_ref[w])

    tacc_ref[...] = jnp.zeros_like(tacc_ref)

    def fill(w, carry):
        gs_ref[w + 3, 0:RIM, :] = top_ref[pl.ds(pl.multiple_of(w * RIM, RIM), RIM), :].astype(F32)
        own = pl.ds(pl.multiple_of(w * rows, rows), rows)
        gs_ref[w + 3, RIM : RIM + rows, :] = g_ref[own, :].astype(F32)
        gs_ref[w + 3, RIM + rows :, :] = bot_ref[pl.ds(pl.multiple_of(w * RIM, RIM), RIM), :].astype(F32)
        return carry

    lax.fori_loop(0, 48, fill, 0)

    def spread(q, carry):
        quarter = pool_ref[q] * 0.25
        sp_ref[q, pl.ds(0, 24, stride=2), :] = quarter
        sp_ref[q, pl.ds(1, 24, stride=2), :] = quarter
        return carry

    lax.fori_loop(0, 24, spread, 0)

    def band(t, carry):
        for s in range(2):
            masked_taps(taps_ref, mask_ref, km_ref.at[s], t * 2 + s, True)

        def block(i, carry):
            w0 = i * 8
            ats = [
                pl.ds(pl.multiple_of((w0 + j) * width + cb * LANES, LANES), LANES) for j in range(8)
            ]
            band_rows = pl.ds(pl.multiple_of(t * 16, 16), 16)
            vals = [x_ref[band_rows, at].astype(F32) for at in ats]
            accs = []
            for s in range(2):
                acc = [jnp.zeros((8, LANES), F32) for _ in range(8)]
                v = [val[s * 8 : s * 8 + 8] for val in vals]
                for a in range(7):
                    start = t * 16 + (s * 8 + RIM - 3 + a)
                    g = [gs_ref[w0 + j, pl.ds(start, 8), :] for j in range(14)]
                    seen = mask_ref[a, pl.ds(t * 16 + s * 8, 8), :]
                    vm = [item * seen for item in v]
                    for b in range(7):
                        k = km_ref[s, a * 7 + b]
                        tap = None
                        for j in range(8):
                            acc[j] = acc[j] + k * g[j + b]
                            term = vm[j] * g[j + b]
                            tap = term if tap is None else tap + term
                        tacc_ref[48 - (a * 7 + b)] += tap
                accs.append(acc)
            for j in range(8):
                both = jnp.concatenate([accs[0][j], accs[1][j]], axis=0)
                total = both + cot_ref[band_rows, ats[j]].astype(F32)
                total = total + sp_ref[i * 4 + j // 2, band_rows, :]
                out_ref[0, band_rows, ats[j]] = total.astype(out_ref.dtype)
            return carry

        lax.fori_loop(0, 6, block, 0)
        return carry

    lax.fori_loop(0, 3, band, 0)
    tap_out_ref[0:49, :] = jnp.sum(tacc_ref[...], axis=1)


def conv_backward(grad, top, bot, x, cot, pool, taps, mask, place, slots, kind):
    width = x.shape[1] // 48
    blocks = width // LANES
    whole = lambda cb, place: (0, 0)
    half = lambda cb, place: (0, place[0] * blocks + cb)
    return pl.pallas_call(
        back_kernel,
        out_shape=(
            jax.ShapeDtypeStruct((slots, *x.shape), kind),
            jax.ShapeDtypeStruct((56, width), F32),
        ),
        grid_spec=pltpu.PrefetchScalarGridSpec(
            num_scalar_prefetch=1,
            grid=(blocks,),
            in_specs=[
                pl.BlockSpec((48 * 48, LANES), half),
                pl.BlockSpec((48 * RIM, LANES), half),
                pl.BlockSpec((48 * RIM, LANES), half),
                pl.BlockSpec(x.shape, whole),
                pl.BlockSpec(cot.shape, whole),
                pl.BlockSpec((24, 24, LANES), lambda cb, place: (0, 0, place[0] * blocks + cb)),
                pl.BlockSpec((49, LANES), half),
                pl.BlockSpec(mask.shape, lambda cb, place: (0, 0, 0)),
            ],
            out_specs=(
                pl.BlockSpec((1, *x.shape), lambda cb, place: (place[0] if slots == 2 else 0, 0, 0)),
                pl.BlockSpec((56, LANES), lambda cb, place: (0, cb)),
            ),
            scratch_shapes=[
                pltpu.VMEM((54, 80, LANES), F32),
                pltpu.VMEM((2, 49, 8, LANES), F32),
                pltpu.VMEM((49, 8, LANES), F32),
                pltpu.VMEM((24, 48, LANES), F32),
            ],
        ),
        **conv_params(4 * 49 * 48 * 48 * width * 8, 25_000_000),
    )(place, grad, top, bot, x, cot, pool, taps, mask)


def join_kernel(place_ref, branch_ref, scale_ref, own_ref, other_ref, own_out, other_out, pool_out, pair_ref):
    rows, width = 48, own_ref.shape[1] // 4
    for g, (src, dst) in enumerate(((own_ref, own_out), (other_ref, other_out))):
        side = place_ref[0] if g == 0 else 1 - place_ref[0]
        at = pl.ds(pl.multiple_of(side * width, LANES), width)
        scale = scale_ref[:, at]
        for q in range(2):
            total = None
            for w in (2 * q, 2 * q + 1):
                field = src[:, w * width : (w + 1) * width].astype(F32)
                field = field + scale * branch_ref[w * rows : (w + 1) * rows, at]
                dst[0, :, w * width : (w + 1) * width] = field.astype(BF)
                total = field if total is None else total + field
            for n in range(width // LANES):
                pair_ref[q, n] = total[:, n * LANES : (n + 1) * LANES]
                even = pair_ref[q, n, pl.ds(0, 24, stride=2), :]
                odd = pair_ref[q, n, pl.ds(1, 24, stride=2), :]
                lane = pl.ds(pl.multiple_of(side * width + n * LANES, LANES), LANES)
                pool_out[q, :, lane] = (even + odd) * 0.25


def join_branch(branch, scale, own, other, place):
    width = own.shape[1] // 48
    raw = pl.BlockSpec((48, 4 * width), lambda i, place: (0, i))
    return pl.pallas_call(
        join_kernel,
        out_shape=(
            jax.ShapeDtypeStruct((2, *own.shape), BF),
            jax.ShapeDtypeStruct((1, *own.shape), BF),
            jax.ShapeDtypeStruct((24, 24, 2 * width), F32),
        ),
        grid_spec=pltpu.PrefetchScalarGridSpec(
            num_scalar_prefetch=1,
            grid=(12,),
            in_specs=[
                pl.BlockSpec((4 * 48, 2 * width), lambda i, place: (i, 0)),
                pl.BlockSpec((1, 2 * width), lambda i, place: (0, 0)),
                raw,
                raw,
            ],
            out_specs=(
                pl.BlockSpec((1, 48, 4 * width), lambda i, place: (place[0], 0, i)),
                pl.BlockSpec((1, 48, 4 * width), lambda i, place: (0, 0, i)),
                pl.BlockSpec((2, 24, 2 * width), lambda i, place: (i, 0, 0)),
            ),
            scratch_shapes=[pltpu.VMEM((2, width // LANES, 48, LANES), F32)],
        ),
        **conv_params(10_000_000, 40_000_000),
    )(place, branch, scale, own, other)


def scaled_kernel(place_ref, pool_ref, branch_ref, scale_ref, own_ref, other_ref, out_ref, sum_ref, pair_ref):
    rows, width = 48, own_ref.shape[1] // 4

    @pl.when(pl.program_id(0) == 0)
    def _():
        sum_ref[...] = jnp.zeros_like(sum_ref)

    for g, src in enumerate((own_ref, other_ref)):
        side = place_ref[0] if g == 0 else 1 - place_ref[0]
        at = pl.ds(pl.multiple_of(side * width, LANES), width)
        scale = scale_ref[:, at]
        for q in range(2):
            quarter = pool_ref[q, :, at] * 0.25
            for n in range(width // LANES):
                part = quarter[:, n * LANES : (n + 1) * LANES]
                pair_ref[q, n, pl.ds(0, 24, stride=2), :] = part
                pair_ref[q, n, pl.ds(1, 24, stride=2), :] = part
            spread = jnp.concatenate([pair_ref[q, n] for n in range(width // LANES)], axis=1)
            for w in (2 * q, 2 * q + 1):
                here = slice(w * rows, (w + 1) * rows)
                grad = src[:, w * width : (w + 1) * width].astype(F32) + spread
                part = grad * branch_ref[here, at]
                sum_ref[:, at] += jnp.sum(part.reshape(6, 8, width), axis=0)
                out_ref[here, at] = (grad * scale).astype(BF)


def scaled_grads(pool, branch, scale, own, other, place):
    width = own.shape[1] // 48
    raw = pl.BlockSpec((48, 4 * width), lambda i, place: (0, i))
    return pl.pallas_call(
        scaled_kernel,
        out_shape=(
            jax.ShapeDtypeStruct(branch.shape, BF),
            jax.ShapeDtypeStruct((8, 2 * width), F32),
        ),
        grid_spec=pltpu.PrefetchScalarGridSpec(
            num_scalar_prefetch=1,
            grid=(12,),
            in_specs=[
                pl.BlockSpec((2, 24, 2 * width), lambda i, place: (i, 0, 0)),
                pl.BlockSpec((4 * 48, 2 * width), lambda i, place: (i, 0)),
                pl.BlockSpec((1, 2 * width), lambda i, place: (0, 0)),
                raw,
                raw,
            ],
            out_specs=(
                pl.BlockSpec((4 * 48, 2 * width), lambda i, place: (i, 0)),
                pl.BlockSpec((8, 2 * width), lambda i, place: (0, 0)),
            ),
            scratch_shapes=[pltpu.VMEM((2, width // LANES, 48, LANES), F32)],
        ),
        **conv_params(10_000_000, 40_000_000),
    )(place, pool, branch, scale, own, other)


CHUNK = 256
NT = (((1,), (1,)), ((), ()))
TN = (((0,), (0,)), ((), ()))


def dot(left, right, dims):
    return lax.dot_general(left, right, dims, preferred_element_type=F32)


NN = (((1,), (0,)), ((), ()))


def lane_half(shape, side):
    lanes = lax.broadcasted_iota(jnp.int32, shape, len(shape) - 1)
    return (lanes < 64) if side == 0 else (lanes >= 64)


def fill_window(win_ref, before, own, after):
    count = own.shape[0]
    win_ref[0:count] = before[...]
    win_ref[count : 2 * count] = own[...]
    win_ref[2 * count : 3 * count] = after[...]
    win_ref[3 * count :] = jnp.zeros_like(win_ref[3 * count :])


def attend_kernel(first_ref, last_ref, q_ref, kb_ref, k_ref, ka_ref, vb_ref, v_ref, va_ref,
                  klab_ref, qlab_ref, out_ref, total_ref, kw_ref, vw_ref):
    fill_window(kw_ref, kb_ref, k_ref, ka_ref)
    fill_window(vw_ref, vb_ref, v_ref, va_ref)
    for n in range(3):
        rows = slice(n * 192, (n + 1) * 192)
        q = q_ref[rows, :] * jnp.asarray(0.125, BF)
        q_half = [jnp.where(lane_half(q.shape, side), q, jnp.zeros_like(q)) for side in range(2)]
        q_lab = qlab_ref[n, 0:1, :]

        def chunk(c, carry):
            at = pl.ds(pl.multiple_of(c * CHUNK, CHUNK), CHUNK)
            kc, vc = kw_ref[at, :], vw_ref[at, :]
            same = klab_ref[at, 0:1] == q_lab
            new = []
            for side in range(2):
                top, total, acc = carry[side]
                s = jnp.where(same, dot(kc, q_half[side], NT), NEG)
                best = jnp.maximum(top, jnp.max(s, axis=0, keepdims=True))
                p = jnp.exp(s - best)
                shrink = jnp.exp(top - best)
                total = total * shrink + jnp.sum(p, axis=0, keepdims=True)
                new.append((best, total, acc * shrink + dot(vc, p.astype(BF), TN)))
            return tuple(new)

        start = (jnp.full((1, 192), NEG, F32), jnp.zeros((1, 192), F32), jnp.zeros((LANES, 192), F32))
        done = lax.fori_loop(first_ref[n], last_ref[n], chunk, (start, start))
        outs = []
        for side in range(2):
            top, total, acc = done[side]
            outs.append(acc * (1.0 / total))
            total_ref[0, n, side : side + 1, :] = top + jnp.log(total)
        both = jnp.concatenate([outs[0][:64], outs[1][64:]], axis=0)
        out_ref[rows, :] = both.T.astype(BF)


def attend(q, k, v, around, qlab, klab, first, last):
    count, width = q.shape
    window = -(-3 * count // CHUNK) * CHUNK
    block = pl.BlockSpec((count, LANES), lambda p, *_: (0, p))
    stats = pl.BlockSpec((1, 3, 2, 192), lambda p, *_: (p, 0, 0, 0))
    return pl.pallas_call(
        attend_kernel,
        out_shape=(
            jax.ShapeDtypeStruct(q.shape, BF),
            jax.ShapeDtypeStruct((width // LANES, 3, 2, 192), F32),
        ),
        grid_spec=pltpu.PrefetchScalarGridSpec(
            num_scalar_prefetch=2,
            grid=(width // LANES,),
            in_specs=[block] * 7
            + [
                pl.BlockSpec(klab.shape, lambda p, *_: (0, 0)),
                pl.BlockSpec(qlab.shape, lambda p, *_: (0, 0, 0)),
            ],
            out_specs=(block, stats),
            scratch_shapes=[pltpu.VMEM((window, LANES), BF), pltpu.VMEM((window, LANES), BF)],
        ),
        **conv_params(20_000_000_000, 20_000_000),
    )(first, last, q, around[0], k, around[1], around[2], v, around[3], klab, qlab)


def attend_back_kernel(first_ref, last_ref, q_ref, kb_ref, k_ref, ka_ref, vb_ref, v_ref, va_ref,
                       do_ref, total_ref, delta_ref, klab_ref, qlab_ref,
                       dq_ref, dk_ref, dv_ref, before_ref, after_ref,
                       kw_ref, vw_ref, dkw_ref, dvw_ref):
    count = q_ref.shape[0]
    fill_window(kw_ref, kb_ref, k_ref, ka_ref)
    fill_window(vw_ref, vb_ref, v_ref, va_ref)
    dkw_ref[...] = jnp.zeros_like(dkw_ref)
    dvw_ref[...] = jnp.zeros_like(dvw_ref)
    for n in range(3):
        rows = slice(n * 192, (n + 1) * 192)
        q = q_ref[rows, :] * jnp.asarray(0.125, BF)
        do = do_ref[rows, :]
        masks = [lane_half((192, LANES), side) for side in range(2)]
        q_half = [jnp.where(m, q, jnp.zeros_like(q)) for m in masks]
        do_half = [jnp.where(m, do, jnp.zeros_like(do)) for m in masks]
        q_lab = qlab_ref[n, 0:1, :]

        def chunk(c, dq):
            at = pl.ds(pl.multiple_of(c * CHUNK, CHUNK), CHUNK)
            kc, vc = kw_ref[at, :], vw_ref[at, :]
            same = klab_ref[at, 0:1] == q_lab
            ks = [jnp.where(lane_half((CHUNK, LANES), side), kc, jnp.zeros_like(kc)) for side in range(2)]
            dk, dv = dkw_ref[at, :], dvw_ref[at, :]
            for side in range(2):
                s = dot(kc, q_half[side], NT)
                p = jnp.exp(jnp.where(same, s - total_ref[0, n, side : side + 1, :], NEG))
                dp = dot(vc, do_half[side], NT)
                ds = (p * (dp - delta_ref[0, n, side : side + 1, :])).astype(BF)
                dv = dv + dot(p.astype(BF), do_half[side], NN)
                dk = dk + dot(ds, q_half[side], NN)
                dq = dq + dot(ds, ks[side], TN)
            dkw_ref[at, :] = dk
            dvw_ref[at, :] = dv
            return dq

        dq = lax.fori_loop(first_ref[n], last_ref[n], chunk, jnp.zeros((192, LANES), F32))
        dq_ref[rows, :] = (dq * 0.125).astype(BF)
    dk_ref[...] = dkw_ref[count : 2 * count, :]
    dv_ref[...] = dvw_ref[count : 2 * count, :]
    before_ref[0] = dkw_ref[0:count, :].astype(BF)
    before_ref[1] = dvw_ref[0:count, :].astype(BF)
    after_ref[0] = dkw_ref[2 * count : 3 * count, :].astype(BF)
    after_ref[1] = dvw_ref[2 * count : 3 * count, :].astype(BF)


def attend_back(q, k, v, around, grad, total, delta, qlab, klab, first, last):
    count, width = q.shape
    window = -(-3 * count // CHUNK) * CHUNK
    block = pl.BlockSpec((count, LANES), lambda p, *_: (0, p))
    stats = pl.BlockSpec((1, 3, 2, 192), lambda p, *_: (p, 0, 0, 0))
    pair = pl.BlockSpec((2, count, LANES), lambda p, *_: (0, 0, p))
    return pl.pallas_call(
        attend_back_kernel,
        out_shape=(
            jax.ShapeDtypeStruct(q.shape, BF),
            jax.ShapeDtypeStruct(q.shape, F32),
            jax.ShapeDtypeStruct(q.shape, F32),
            jax.ShapeDtypeStruct((2, count, width), BF),
            jax.ShapeDtypeStruct((2, count, width), BF),
        ),
        grid_spec=pltpu.PrefetchScalarGridSpec(
            num_scalar_prefetch=2,
            grid=(width // LANES,),
            in_specs=[block] * 8
            + [
                stats,
                stats,
                pl.BlockSpec(klab.shape, lambda p, *_: (0, 0)),
                pl.BlockSpec(qlab.shape, lambda p, *_: (0, 0, 0)),
            ],
            out_specs=(block, block, block, pair, pair),
            scratch_shapes=[
                pltpu.VMEM((window, LANES), BF),
                pltpu.VMEM((window, LANES), BF),
                pltpu.VMEM((window, LANES), F32),
                pltpu.VMEM((window, LANES), F32),
            ],
        ),
        **conv_params(20_000_000_000, 20_000_000),
    )(first, last, q, around[0], k, around[1], around[2], v, around[3], grad, total, delta, klab, qlab)


def on_device(
    lo_in,
    hi_in,
    image_ids,
    cn_kernel,
    cn_gain,
    cn_w1,
    cn_w2,
    cn_scale,
    ad_proj,
    ad_kernel,
    gate_w1,
    gate_w2,
    ln1_gain,
    qkv,
    out_proj,
    ln2_gain,
    fc1,
    fc2,
    d_lo_out,
    d_hi_out,
):
    micro_count, row_count, col_count, d_shard = lo_in.shape
    hi_rows = hi_in.shape[1]
    hi_cols = HCOLS
    c_shard = hi_in.shape[3] // hi_cols
    d_own, c_own = 2 * d_shard, 2 * c_shard
    tok_count = row_count * col_count
    pix_count = hi_rows * hi_cols
    mine = lax.axis_index("mb")
    row_start = lax.axis_index("tile") * row_count
    head_count = d_own // HDIM

    fast = c_shard % LANES == 0 and lax.axis_size("tp") == 1
    hi_raw = hi_in.reshape(2, hi_rows, hi_cols * c_shard)
    hi_own, hi_other = swap_micro(hi_raw)
    up, down = rim_pair(hi_raw, 3, 1)
    own_rims, other_rims = swap_micro(jnp.stack([up, down], axis=1))
    cot_own, cot_other = swap_micro(d_hi_out.reshape(2, hi_rows, hi_cols * c_shard))
    lo_low = in_order(*swap_micro(lo_in.reshape(2, tok_count, d_shard)), 1)
    lo_field = lo_low.astype(F32)

    mlp_in = gather_all(cn_w1)
    mlp_out = gather_all(cn_w2.T)
    ad_gate = gather_all(jnp.concatenate([ad_proj, gate_w1], axis=1))
    ad_matrix = [ad_gate[g, :, :d_shard] for g in range(2)]
    gate_in = [ad_gate[g, :, d_shard:] for g in range(2)]
    gh_shard = gate_w1.shape[1]
    ff_shard = fc1.shape[1]
    vit = gather_all(
        jnp.concatenate([gate_w2.T, qkv[0], qkv[1], qkv[2], out_proj.T, fc1, fc2.T], axis=1)
    )
    cuts = np.cumsum([0, gh_shard, d_shard, d_shard, d_shard, d_shard, ff_shard, ff_shard])
    gate_out, q_w, k_w, v_w, out_w, ff_in, ff_out = [
        [vit[g, :, int(cuts[i]) : int(cuts[i + 1])] for g in range(2)] for i in range(7)
    ]

    def apply(left, pair):
        return jnp.concatenate([matmul(left, pair[0]), matmul(left, pair[1])], axis=1)

    def apply_t(left, pair):
        width = pair[0].shape[1]
        return matmul_nt(left[:, :width], pair[0]) + matmul_nt(left[:, width:], pair[1])

    def cols(values):
        width = values.shape[1] // 2
        return [values[:, :width], values[:, width:]]

    canvas_ids = lax.dynamic_index_in_dim(image_ids, mine, 0, keepdims=False)
    small_ids = row_labels(canvas_ids, row_start, row_count, 1)
    lo_mid = small_ids[1 : 1 + row_count]
    hi_ids = row_labels(jnp.repeat(canvas_ids, 2), 2 * row_start, hi_rows, 3)
    hi_mid = hi_ids[3 : 3 + hi_rows]

    def both_shards(shard, axis):
        return in_order(shard, lax.ppermute(shard, "mb", SWAP), axis)

    conv_taps = both_shards(cn_kernel, 1)
    ad_taps = both_shards(ad_kernel, 1)
    hi_scale = both_shards(cn_scale, 0).astype(F32)

    own_place = mine.reshape(1).astype(jnp.int32)
    other_place = 1 - own_place
    own_rims, other_rims = [
        (jnp.pad(rims[0], ((RIM - 3, 0), (0, 0))), jnp.pad(rims[1], ((0, RIM - 3), (0, 0))))
        for rims in (own_rims, other_rims)
    ]
    seen = jnp.stack([(hi_ids[a : a + hi_rows] == hi_mid).astype(F32) for a in range(7)])
    mask = jnp.broadcast_to(seen[:, :, None], (7, hi_rows, LANES))
    wide_taps = conv_taps.astype(F32)

    def natural(own, other):
        shape = (-1, hi_cols, c_shard)
        return in_order(own.reshape(shape), other.reshape(shape), 2)

    if fast:
        conv_flat = conv_forward(hi_own, *own_rims, wide_taps, mask, own_place)
        conv_flat = conv_forward(hi_other, *other_rims, wide_taps, mask, other_place, conv_flat)
    else:
        hi_field = natural(hi_own, hi_other)
        hi_pad = jnp.concatenate(
            [
                natural(own_rims[0], other_rims[0])[-3:],
                hi_field,
                natural(own_rims[1], other_rims[1])[:3],
            ]
        )
        conv_low = depthwise(hi_pad, conv_taps, hi_ids, hi_mid, 7, False).astype(BF)
        conv_flat = conv_low.transpose(1, 0, 2).reshape(pix_count, c_own)
    conv_full = features(conv_flat)
    normed, norm_pull = jax.vjp(layer_norm, conv_full.astype(F32), cn_gain.astype(F32))
    normed_low = lax.optimization_barrier(normed.astype(BF))
    inner_act, inner_slope = zip(*[gelu_pair(matmul(normed_low, mlp_in[g])) for g in range(2)])
    branch = partial_sums(
        matmul_nt(inner_act[0], mlp_out[0]) + matmul_nt(inner_act[1], mlp_out[1])
    )
    if fast:
        hi_mine, hi_sent, pooled = join_branch(branch, hi_scale[None], hi_own, hi_other, own_place)
        pooled = pooled.transpose(1, 0, 2)
    else:
        branch_rows = branch.reshape(hi_cols, hi_rows, c_own).transpose(1, 0, 2)
        hi_sum = hi_field.astype(F32) + hi_scale * branch_rows
        pooled = jnp.mean(hi_sum.reshape(row_count, 2, col_count, 2, c_own), axis=(1, 3))
    pooled_full = features(pooled.reshape(tok_count, c_own).astype(BF))
    proj_low = apply(pooled_full, ad_matrix).astype(BF)
    proj_pad = rim_rows(proj_low.reshape(row_count, col_count, d_own), 1)
    local_conv = depthwise(proj_pad, ad_taps, small_ids, lo_mid, 3, False).reshape(
        tok_count, d_own
    )
    gate_hidden, gate_slope = gelu_pair(apply(pooled_full, gate_in))
    gate_val = jnp.tanh(partial_sums(apply_t(gate_hidden, gate_out)))
    mixed_one = lo_field + gate_val * local_conv
    mixed_full = features(mixed_one.astype(BF))
    norm_one, first_pull = jax.vjp(layer_norm, mixed_full.astype(F32), ln1_gain.astype(F32))
    norm_low = norm_one.astype(BF)
    queries = apply(norm_low, q_w).astype(BF)
    key_rows = apply(norm_low, k_w).astype(BF)
    value_rows = apply(norm_low, v_w).astype(BF)
    key_value = jnp.concatenate([key_rows, value_rows], axis=1)
    kv_before, kv_after = rim_pair(key_value, tok_count, 0)
    around = (kv_before[:, :d_own], kv_after[:, :d_own], kv_before[:, d_own:], kv_after[:, d_own:])
    near = row_labels(canvas_ids, row_start, row_count, row_count)
    key_tok = jnp.repeat(near, col_count)
    window = -(-3 * tok_count // CHUNK) * CHUNK
    key_tok = jnp.pad(key_tok, (0, window - 3 * tok_count), constant_values=-2)
    key_lab = jnp.broadcast_to(key_tok[:, None], (window, LANES))
    query_lab = jnp.broadcast_to(jnp.repeat(lo_mid, col_count).reshape(3, 1, 192), (3, 8, 192))
    edge = jnp.arange(3 * row_count)
    first_row = jnp.min(jnp.where(near[None] == lo_mid[::8][:, None], edge, 3 * row_count), axis=1)
    last_row = jnp.max(jnp.where(near[None] == lo_mid[7::8][:, None], edge, -1), axis=1) + 1
    first = (first_row * col_count // CHUNK).astype(jnp.int32)
    last = ((last_row * col_count + CHUNK - 1) // CHUNK).astype(jnp.int32)
    attended, log_total = attend(
        queries, key_rows, value_rows, around, query_lab, key_lab, first, last
    )
    mixed_two = mixed_one + partial_sums(apply_t(attended, out_w))
    mixed2_full = features(mixed_two.astype(BF))
    norm_two, second_pull = jax.vjp(layer_norm, mixed2_full.astype(F32), ln2_gain.astype(F32))
    norm2_low = norm_two.astype(BF)
    ff_hidden, ff_slope = gelu_pair(apply(norm2_low, ff_in))
    lo_result = (mixed_two + partial_sums(apply_t(ff_hidden, ff_out))).astype(BF)

    grad_low = in_order(*swap_micro(d_lo_out.reshape(2, tok_count, d_shard)), 1)
    grad_out = grad_low.astype(F32)
    ff_grad_full = features(grad_low)
    ff_pre_grad = (apply(ff_grad_full, ff_out) * ff_slope.astype(F32)).astype(BF)
    second_grad = partial_sums(apply_t(ff_pre_grad, ff_in)).astype(BF)
    g_ff = reduce_all(
        *[
            jnp.concatenate([matmul_tn(norm2_low, i), matmul_tn(ff_grad_full, o)], axis=1)
            for i, o in zip(cols(ff_pre_grad), cols(ff_hidden))
        ]
    )
    back_two, grad_ln2 = second_pull(features(second_grad).astype(F32))
    grad_two = grad_out + own_slice(back_two)
    att_grad_full = features(grad_two.astype(BF))
    att_grad = apply(att_grad_full, out_w).astype(BF)
    inner = (att_grad.astype(F32) * attended.astype(F32)).reshape(3, 192, head_count // 2, 2, HDIM)
    delta = jnp.sum(inner, axis=-1).transpose(2, 0, 3, 1)
    query_grad, key_own, value_own, to_before, to_after = attend_back(
        queries, key_rows, value_rows, around, att_grad, log_total, delta, query_lab, key_lab, first, last
    )
    devices = lax.axis_size("tile")
    steps = [(i, i + 1) for i in range(devices - 1)]
    from_before = lax.ppermute(to_after, "tile", steps)
    from_after = lax.ppermute(to_before, "tile", [(j, i) for i, j in steps])
    key_grad, value_grad = [
        (own + from_before[i].astype(F32) + from_after[i].astype(F32)).astype(BF)
        for i, own in enumerate((key_own, value_own))
    ]
    first_grad = partial_sums(
        apply_t(query_grad, q_w) + apply_t(key_grad, k_w) + apply_t(value_grad, v_w)
    ).astype(BF)
    back_one, grad_ln1 = first_pull(features(first_grad).astype(F32))
    grad_one = grad_two + own_slice(back_one)
    gate_pre_grad = (grad_one * local_conv * (1.0 - gate_val * gate_val)).astype(BF)
    gate_grad_full = features(gate_pre_grad)
    g_att = reduce_all(
        *[
            jnp.concatenate(
                [
                    matmul_tn(gate_grad_full, h),
                    matmul_tn(norm_low, q),
                    matmul_tn(norm_low, k),
                    matmul_tn(norm_low, v),
                    matmul_tn(att_grad_full, o),
                ],
                axis=1,
            )
            for h, q, k, v, o in zip(
                cols(gate_hidden), cols(query_grad), cols(key_grad), cols(value_grad), cols(attended)
            )
        ]
    )
    hidden_grad = (apply(gate_grad_full, gate_out) * gate_slope.astype(F32)).astype(BF)
    local_grad = (grad_one * gate_val).astype(BF).reshape(row_count, col_count, d_own)
    local_pad = rim_rows(local_grad, 1)
    proj_grad = (
        depthwise(local_pad, ad_taps, small_ids, lo_mid, 3, True)
        .reshape(tok_count, d_own)
        .astype(BF)
    )
    grad_ad_kernel = tap_grads(proj_pad, local_grad, small_ids, lo_mid, 3)
    g_ad = reduce_all(
        *[
            jnp.concatenate([matmul_tn(pooled_full, p), matmul_tn(pooled_full, h)], axis=1)
            for p, h in zip(cols(proj_grad), cols(hidden_grad))
        ]
    )
    pooled_grad = partial_sums(apply_t(hidden_grad, gate_in) + apply_t(proj_grad, ad_matrix))
    pool_cols = pooled_grad.reshape(row_count, col_count, c_own).transpose(1, 0, 2)
    if fast:
        scaled_grad, scale_parts = scaled_grads(
            pool_cols, branch, hi_scale[None], cot_own, cot_other, own_place
        )
        grad_scale = jnp.sum(scale_parts, axis=0)
    else:
        spread_grad = jnp.repeat(jnp.repeat(pool_cols.transpose(1, 0, 2) * 0.25, 2, 0), 2, 1)
        hi_grad = natural(cot_own, cot_other).astype(F32) + spread_grad
        grad_cols = hi_grad.transpose(1, 0, 2).reshape(pix_count, c_own)
        grad_scale = jnp.sum(grad_cols * branch, axis=0)
        scaled_grad = (grad_cols * hi_scale).astype(BF)
    branch_full = lax.optimization_barrier(features(scaled_grad))
    g_w2 = reduce_all(*[matmul_tn(branch_full, act) for act in inner_act])
    inner_grad = [
        (matmul(branch_full, mlp_out[g]) * inner_slope[g].astype(F32)).astype(BF) for g in range(2)
    ]
    g_w1 = reduce_all(*[matmul_tn(normed_low, grad) for grad in inner_grad])
    normed_grad = partial_sums(
        matmul_nt(inner_grad[0], mlp_in[0]) + matmul_nt(inner_grad[1], mlp_in[1])
    ).astype(BF)
    back_conv, grad_cn_gain = norm_pull(features(normed_grad).astype(F32))
    conv_grad = own_slice(back_conv).astype(BF)
    conv_cols = conv_grad.reshape(hi_cols, hi_rows, c_own)
    grad_up, grad_down = rim_pair(conv_cols, 3, 1)
    if fast:
        grad_rims = [
            jnp.pad(rim, ((0, 0), side, (0, 0))).reshape(hi_cols * RIM, c_own)
            for rim, side in ((grad_up, (RIM - 3, 0)), (grad_down, (0, RIM - 3)))
        ]
        ghi_sent, taps_other = conv_backward(
            conv_grad, *grad_rims, hi_other, cot_other, pool_cols, wide_taps, mask, other_place, 1, BF
        )
        ghi_mine, taps_own = conv_backward(
            conv_grad, *grad_rims, hi_own, cot_own, pool_cols, wide_taps, mask, own_place, 2, F32
        )
        grad_cn_kernel = in_order(taps_own[:49], taps_other[:49], 1)
    else:
        conv_grad = conv_cols.transpose(1, 0, 2)
        conv_pad = jnp.concatenate(
            [grad_up.transpose(1, 0, 2), conv_grad, grad_down.transpose(1, 0, 2)]
        )
        hi_back = hi_grad + depthwise(conv_pad, conv_taps, hi_ids, hi_mid, 7, True)
        grad_cn_kernel = tap_grads(hi_pad, conv_grad, hi_ids, hi_mid, 7)

    def leave(values, kind):
        own, sent = halves(values)
        other = lax.ppermute(sent.astype(BF), "mb", SWAP)
        return both_micro(own.astype(kind), other.astype(kind))

    lo_stack = leave(lo_result.reshape(row_count, col_count, d_own), BF)
    if fast:
        hi_stack, ghi_stack = [
            lax.dynamic_update_slice_in_dim(
                stack, lax.ppermute(sent, "mb", SWAP).astype(stack.dtype), 1 - mine, 0
            )
            for stack, sent in ((hi_mine, hi_sent), (ghi_mine, ghi_sent))
        ]
    else:
        hi_stack = leave(hi_sum, BF)
        ghi_stack = leave(hi_back, F32)
    glo_stack = leave(grad_one.reshape(row_count, col_count, d_own), F32)

    flat_terms = [grad_cn_kernel, grad_scale, grad_ad_kernel, grad_cn_gain, grad_ln1, grad_ln2]
    sizes = np.cumsum([0] + [item.size for item in flat_terms])
    total = lax.psum(
        jnp.concatenate([item.reshape(-1).astype(BF) for item in flat_terms]), ALL
    ).astype(F32)
    sums = [
        total[int(sizes[i]) : int(sizes[i + 1])].reshape(item.shape)
        for i, item in enumerate(flat_terms)
    ]
    g_kernel, g_scale, g_taps = [halves(item)[0] for item in sums[:3]]
    gain_sums = sums[3:]

    g_gate_w1 = g_ad[:, d_shard:]
    g_gate_w2 = g_att[:, :gh_shard].T
    g_qkv = jnp.stack([g_att[:, gh_shard + j * d_shard : gh_shard + (j + 1) * d_shard] for j in range(3)])
    g_out = g_att[:, gh_shard + 3 * d_shard :].T
    return (
        lo_stack,
        hi_stack.reshape(2, hi_rows, 1, hi_cols * c_shard),
        glo_stack,
        ghi_stack.reshape(2, hi_rows, 1, hi_cols * c_shard),
        g_kernel,
        gain_sums[0],
        g_w1,
        g_w2.T,
        g_scale,
        g_ad[:, :d_shard],
        g_taps,
        g_gate_w1,
        g_gate_w2,
        gain_sums[1],
        g_qkv,
        g_out,
        gain_sums[2],
        g_ff[:, :ff_shard],
        g_ff[:, ff_shard:].T,
    )


def solution(mesh):
    tiles, mps = mesh.shape["tile"], mesh.shape["mp"]
    fine = Mesh(mesh.devices.reshape(tiles, 2, mps // 2), ("tile", "mb", "tp"))
    mp = ("mb", "tp")
    in_specs = (
        P(None, "tile", None, mp),
        P(None, "tile", mp, None),
        P(),
        P(None, mp),
        P(),
        P("tile", mp),
        P(mp, "tile"),
        P(mp),
        P("tile", mp),
        P(None, mp),
        P("tile", mp),
        P(mp, "tile"),
        P(),
        P(None, "tile", mp),
        P(mp, "tile"),
        P(),
        P("tile", mp),
        P(mp, "tile"),
        P(None, "tile", None, mp),
        P(None, "tile", mp, None),
    )
    out_specs = (
        P(None, "tile", None, mp),
        P(None, "tile", mp, None),
        P(None, "tile", None, mp),
        P(None, "tile", mp, None),
        P(None, mp),
        P(),
        P("tile", mp),
        P(mp, "tile"),
        P(mp),
        P("tile", mp),
        P(None, mp),
        P("tile", mp),
        P(mp, "tile"),
        P(),
        P(None, "tile", mp),
        P(mp, "tile"),
        P(),
        P("tile", mp),
        P(mp, "tile"),
    )
    return jax.shard_map(
        on_device, mesh=fine, in_specs=in_specs, out_specs=out_specs, check_vma=False
    )
```

```python
import functools

import jax
import jax.numpy as jnp
import numpy as np
from jax import lax
from jax.experimental import pallas as pl
from jax.experimental.pallas import tpu as pltpu
from jax.sharding import Mesh
from jax.sharding import PartitionSpec as P

HDIM = 64
IMG_ROWS = 24
HCOLS = 48

EPS = 1e-06
NEG = -1e30
BF = jnp.bfloat16
F32 = jnp.float32
ALL = ("mb", "tile")


def rim_pair(value, width, axis):
    devices, length = lax.axis_size("tile"), value.shape[axis]
    up = [(i, (i + 1) % devices) for i in range(devices - 1)]
    down = [(j, i) for i, j in up]
    before = lax.ppermute(lax.slice_in_dim(value, length - width, length, axis=axis), "tile", up)
    after = lax.ppermute(lax.slice_in_dim(value, 0, width, axis=axis), "tile", down)
    return before, after


def rim_rows(value, width):
    devices, length = lax.axis_size("tile"), value.shape[0]
    up = [(i, (i + 1) % devices) for i in range(devices - 1)]
    down = [(j, i) for i, j in up]
    before = lax.ppermute(value[length - width :], "tile", up)
    after = lax.ppermute(value[:width], "tile", down)
    return jnp.concatenate([before, value, after], axis=0)


def matmul(left, right):
    return jnp.dot(left, right, preferred_element_type=F32)


def matmul_tn(left, right):
    return lax.dot_general(left, right, (((0,), (0,)), ((), ())), preferred_element_type=F32)


def matmul_nt(left, right):
    return lax.dot_general(left, right, (((1,), (1,)), ((), ())), preferred_element_type=F32)


def layer_norm(values, gain_vec):
    average = jnp.mean(values, axis=-1, keepdims=True)
    centered = values - average
    variance = jnp.mean(centered * centered, axis=-1, keepdims=True)
    return centered * lax.rsqrt(variance + EPS) * gain_vec


def gelu_pair(values):
    cdf = 0.5 + 0.5 * lax.erf(values * 0.7071067811865476)
    slope = cdf + values * (0.3989422804014327 * jnp.exp(-0.5 * values * values))
    return (values * cdf).astype(BF), slope.astype(BF)


def features(values):
    parts = lax.axis_size("tp")
    if parts == 1:
        return values
    rows, width = values.shape
    full = lax.all_gather(values.reshape(rows, 2, width // 2), "tp", axis=2)
    return full.reshape(rows, parts * width)


def partial_sums(values):
    parts = lax.axis_size("tp")
    if parts == 1:
        return values
    rows, width = values.shape
    split = values.reshape(rows, 2, parts, width // (2 * parts))
    return lax.psum_scatter(split, "tp", scatter_dimension=2).reshape(rows, width // parts)


def own_slice(values):
    parts = lax.axis_size("tp")
    if parts == 1:
        return values
    rows, width = values.shape
    split = values.reshape(rows, 2, parts, width // (2 * parts))
    own = lax.dynamic_index_in_dim(split, lax.axis_index("tp"), 2, keepdims=False)
    return own.reshape(rows, width // parts)


SWAP = [(0, 1), (1, 0)]


def swap_micro(values):
    mine = lax.axis_index("mb")
    own = lax.dynamic_index_in_dim(values, mine, 0, keepdims=False)
    sent = lax.dynamic_index_in_dim(values, 1 - mine, 0, keepdims=False)
    return own, lax.ppermute(sent, "mb", SWAP)


def in_order(own, other, axis):
    first = lax.axis_index("mb") == 0
    return jnp.concatenate(
        [jnp.where(first, own, other), jnp.where(first, other, own)], axis=axis
    )


def both_micro(own, other):
    first = lax.axis_index("mb") == 0
    return jnp.stack([jnp.where(first, own, other), jnp.where(first, other, own)])


def halves(values):
    width = values.shape[-1] // 2
    mine = lax.axis_index("mb")
    own = lax.dynamic_slice_in_dim(values, mine * width, width, values.ndim - 1)
    sent = lax.dynamic_slice_in_dim(values, (1 - mine) * width, width, values.ndim - 1)
    return own, sent


def row_labels(labels, first_row, count_rows, margin):
    padded = jnp.pad(labels, (margin, margin), constant_values=-1)
    return lax.dynamic_slice_in_dim(padded, first_row, count_rows + 2 * margin, 0)


def depthwise(padded, kernel, ids_pad, ids_mid, tap_size, flipped):
    margin = tap_size // 2
    row_count = ids_mid.shape[0]
    col_count = padded.shape[1]
    widened = jnp.pad(padded, ((0, 0), (margin, margin), (0, 0)))
    summed = jnp.zeros((row_count, col_count, padded.shape[2]), F32)
    for a in range(tap_size):
        same_img = (ids_pad[a : a + row_count] == ids_mid)[:, None, None]
        shifted = jnp.where(same_img, widened[a : a + row_count].astype(F32), 0.0)
        for b in range(tap_size):
            tap_index = (
                (tap_size - 1 - a) * tap_size + (tap_size - 1 - b) if flipped else a * tap_size + b
            )
            summed = summed + kernel[tap_index].astype(F32) * shifted[:, b : b + col_count]
    return summed


def tap_grads(padded, grad_low, ids_pad, ids_mid, tap_size):
    margin = tap_size // 2
    row_count = ids_mid.shape[0]
    col_count = padded.shape[1]
    widened = jnp.pad(padded, ((0, 0), (margin, margin), (0, 0)))
    grad_vals = grad_low.astype(F32)
    results = []
    for a in range(tap_size):
        same_img = (ids_pad[a : a + row_count] == ids_mid)[:, None, None]
        shifted = jnp.where(same_img, widened[a : a + row_count].astype(F32), 0.0)
        for b in range(tap_size):
            results.append(jnp.sum(shifted[:, b : b + col_count] * grad_vals, axis=(0, 1)))
    return jnp.stack(results)


def stacked_kernel(cuts, *refs):
    count = len(cuts) - 1
    step = pl.program_id(0)
    for i in range(count):

        @pl.when((step >= cuts[i]) & (step < cuts[i + 1]))
        def _(i=i):
            refs[-1][...] = dot(refs[i][...], refs[count + i][...], NN).astype(BF)


def stacked_grads(lefts, rights):
    widths = [item.shape[1] for item in rights]
    if any(width % CHUNK for width in widths):
        return jnp.concatenate(
            [matmul_tn(left, right).astype(BF) for left, right in zip(lefts, rights)], axis=1
        )
    tokens, rows = lefts[0].shape
    cuts = [int(item) for item in np.cumsum([0] + [width // CHUNK for width in widths])]

    def column(i):
        return lambda step: (0, jnp.clip(step - cuts[i], 0, cuts[i + 1] - cuts[i] - 1))

    return pl.pallas_call(
        functools.partial(stacked_kernel, cuts),
        out_shape=jax.ShapeDtypeStruct((rows, sum(widths)), BF),
        grid=(cuts[-1],),
        in_specs=[pl.BlockSpec((rows, tokens), lambda step: (0, 0)) for _ in lefts]
        + [pl.BlockSpec((tokens, CHUNK), column(i)) for i in range(len(rights))],
        out_specs=pl.BlockSpec((rows, CHUNK), lambda step: (0, step)),
        **conv_params(2 * tokens * rows * sum(widths), 2 * rows * sum(widths)),
    )(*[left.T for left in lefts], *rights)


def gather_all(shard):
    full = lax.all_gather(shard, ALL, axis=0)
    return full.reshape(2, -1, shard.shape[1])


def reduce_tiles(terms):
    return lax.psum_scatter(terms, "tile", scatter_dimension=0, tiled=True)


def settle(summed, widths):
    own, sent, start = [], [], 0
    for width in widths:
        mine, other = halves(summed[:, start : start + 2 * width])
        own.append(mine)
        sent.append(other)
        start += 2 * width
    got = lax.ppermute(jnp.concatenate(sent, axis=1), "mb", SWAP)
    cuts = [int(item) for item in np.cumsum([0] + list(widths))]
    return [
        item.astype(F32) + got[:, cuts[i] : cuts[i + 1]].astype(F32) for i, item in enumerate(own)
    ]


def sum_everywhere(flat):
    devices = lax.axis_size("tile")
    if devices & (devices - 1):
        return lax.psum(flat, "tile")
    bit = 1
    while bit < devices:
        flat = flat + lax.ppermute(flat, "tile", [(i, i ^ bit) for i in range(devices)])
        bit *= 2
    return flat


def together(*values):
    return lax.optimization_barrier(values)


LANES = 128
RIM = 8
VMEM_LIMIT = 60 * 1024 * 1024


def conv_params(flops=0, moved=0):
    return dict(
        compiler_params=pltpu.CompilerParams(vmem_limit_bytes=VMEM_LIMIT),
        cost_estimate=pl.CostEstimate(flops=flops, bytes_accessed=moved, transcendentals=0),
    )


def masked_taps(taps_ref, mask_ref, km_ref, sub, flip):
    for a in range(7):
        seen = mask_ref[a, pl.ds(sub * 8, 8), :]
        for b in range(7):
            tap = 48 - (a * 7 + b) if flip else a * 7 + b
            km_ref[a * 7 + b] = taps_ref[tap : tap + 1, :] * seen


def conv_kernel(place_ref, x_ref, top_ref, bot_ref, taps_ref, mask_ref, out_ref, xs_ref, km_ref):
    rows, width = 48, x_ref.shape[1] // 48
    cb = pl.program_id(0)

    @pl.when(cb == 0)
    def _():
        for w in (0, 1, 2, 51, 52, 53):
            xs_ref[w] = jnp.zeros_like(xs_ref[w])

    def fill(w, carry):
        at = pl.ds(pl.multiple_of(w * width + cb * LANES, LANES), LANES)
        xs_ref[w + 3, 0:RIM, :] = top_ref[:, at].astype(F32)
        xs_ref[w + 3, RIM : RIM + rows, :] = x_ref[:, at].astype(F32)
        xs_ref[w + 3, RIM + rows :, :] = bot_ref[:, at].astype(F32)
        return carry

    lax.fori_loop(0, 48, fill, 0)

    def band(t, carry):
        for s in range(2):
            masked_taps(taps_ref, mask_ref, km_ref.at[s], t * 2 + s, False)

        def block(i, carry):
            w0 = i * 8
            accs = []
            for s in range(2):
                acc = [jnp.zeros((8, LANES), F32) for _ in range(8)]
                for a in range(7):
                    start = t * 16 + (s * 8 + RIM - 3 + a)
                    x = [xs_ref[w0 + j, pl.ds(start, 8), :] for j in range(14)]
                    for b in range(7):
                        k = km_ref[s, a * 7 + b]
                        for j in range(8):
                            acc[j] = acc[j] + k * x[j + b]
                accs.append(acc)
            for j in range(8):
                both = jnp.concatenate([accs[0][j], accs[1][j]], axis=0).astype(BF)
                out_ref[pl.ds(pl.multiple_of((w0 + j) * rows + t * 16, 16), 16), :] = both
            return carry

        lax.fori_loop(0, 6, block, 0)
        return carry

    lax.fori_loop(0, 3, band, 0)


def conv_forward(x, top, bot, taps, mask, place, into=None):
    width = x.shape[1] // 48
    blocks = width // LANES
    whole = lambda cb, place: (0, 0)
    half = lambda cb, place: (0, place[0] * blocks + cb)
    extra = [] if into is None else [into]
    kernel = conv_kernel if into is None else conv_kernel_into
    return pl.pallas_call(
        kernel,
        out_shape=jax.ShapeDtypeStruct((48 * 48, 2 * width), BF),
        grid_spec=pltpu.PrefetchScalarGridSpec(
            num_scalar_prefetch=1,
            grid=(blocks,),
            in_specs=[
                pl.BlockSpec(x.shape, whole),
                pl.BlockSpec(top.shape, whole),
                pl.BlockSpec(bot.shape, whole),
                pl.BlockSpec((49, LANES), lambda cb, place: (0, cb)),
                pl.BlockSpec(mask.shape, lambda cb, place: (0, 0, 0)),
            ]
            + [pl.BlockSpec(memory_space=pl.ANY)] * len(extra),
            out_specs=pl.BlockSpec((48 * 48, LANES), half),
            scratch_shapes=[
                pltpu.VMEM((54, 64, LANES), F32),
                pltpu.VMEM((2, 49, 8, LANES), F32),
            ],
        ),
        input_output_aliases={} if into is None else {6: 0},
        **conv_params(2 * 49 * 48 * 48 * width * 8, 12_000_000),
    )(place, x, top, bot, taps, mask, *extra)


def conv_kernel_into(place_ref, x_ref, top_ref, bot_ref, taps_ref, mask_ref, into_ref, *rest):
    conv_kernel(place_ref, x_ref, top_ref, bot_ref, taps_ref, mask_ref, *rest)


def back_kernel(place_ref, g_ref, top_ref, bot_ref, x_ref, cot_ref, pool_ref, taps_ref, mask_ref,
                out_ref, tap_out_ref, gs_ref, km_ref, tacc_ref, sp_ref):
    rows, width = 48, x_ref.shape[1] // 48
    cb = pl.program_id(0)

    @pl.when(cb == 0)
    def _():
        for w in (0, 1, 2, 51, 52, 53):
            gs_ref[w] = jnp.zeros_like(gs_ref[w])

    tacc_ref[...] = jnp.zeros_like(tacc_ref)

    def fill(w, carry):
        gs_ref[w + 3, 0:RIM, :] = top_ref[w].astype(F32)
        own = pl.ds(pl.multiple_of(w * rows, rows), rows)
        gs_ref[w + 3, RIM : RIM + rows, :] = g_ref[own, :].astype(F32)
        gs_ref[w + 3, RIM + rows :, :] = bot_ref[w].astype(F32)
        return carry

    lax.fori_loop(0, 48, fill, 0)

    def spread(q, carry):
        quarter = pool_ref[q] * 0.25
        sp_ref[q, pl.ds(0, 24, stride=2), :] = quarter
        sp_ref[q, pl.ds(1, 24, stride=2), :] = quarter
        return carry

    lax.fori_loop(0, 24, spread, 0)

    def band(t, carry):
        for s in range(2):
            masked_taps(taps_ref, mask_ref, km_ref.at[s], t * 2 + s, True)

        def block(i, carry):
            w0 = i * 8
            ats = [
                pl.ds(pl.multiple_of((w0 + j) * width + cb * LANES, LANES), LANES) for j in range(8)
            ]
            band_rows = pl.ds(pl.multiple_of(t * 16, 16), 16)
            vals = [x_ref[band_rows, at].astype(F32) for at in ats]
            accs = []
            for s in range(2):
                acc = [jnp.zeros((8, LANES), F32) for _ in range(8)]
                v = [val[s * 8 : s * 8 + 8] for val in vals]
                for a in range(7):
                    start = t * 16 + (s * 8 + RIM - 3 + a)
                    g = [gs_ref[w0 + j, pl.ds(start, 8), :] for j in range(14)]
                    seen = mask_ref[a, pl.ds(t * 16 + s * 8, 8), :]
                    vm = [item * seen for item in v]
                    for b in range(7):
                        k = km_ref[s, a * 7 + b]
                        tap = None
                        for j in range(8):
                            acc[j] = acc[j] + k * g[j + b]
                            term = vm[j] * g[j + b]
                            tap = term if tap is None else tap + term
                        tacc_ref[48 - (a * 7 + b)] += tap
                accs.append(acc)
            for j in range(8):
                both = jnp.concatenate([accs[0][j], accs[1][j]], axis=0)
                total = both + cot_ref[band_rows, ats[j]].astype(F32)
                total = total + sp_ref[i * 4 + j // 2, band_rows, :]
                out_ref[0, band_rows, ats[j]] = total.astype(out_ref.dtype)
            return carry

        lax.fori_loop(0, 6, block, 0)
        return carry

    lax.fori_loop(0, 3, band, 0)
    tap_out_ref[0:49, :] = jnp.sum(tacc_ref[...], axis=1)


def conv_backward(grad, top, bot, x, cot, pool, taps, mask, place, slots, kind):
    width = x.shape[1] // 48
    blocks = width // LANES
    whole = lambda cb, place: (0, 0)
    half = lambda cb, place: (0, place[0] * blocks + cb)
    return pl.pallas_call(
        back_kernel,
        out_shape=(
            jax.ShapeDtypeStruct((slots, *x.shape), kind),
            jax.ShapeDtypeStruct((56, width), F32),
        ),
        grid_spec=pltpu.PrefetchScalarGridSpec(
            num_scalar_prefetch=1,
            grid=(blocks,),
            in_specs=[
                pl.BlockSpec((48 * 48, LANES), half),
                pl.BlockSpec((48, RIM, LANES), lambda cb, place: (0, 0, place[0] * blocks + cb)),
                pl.BlockSpec((48, RIM, LANES), lambda cb, place: (0, 0, place[0] * blocks + cb)),
                pl.BlockSpec(x.shape, whole),
                pl.BlockSpec(cot.shape, whole),
                pl.BlockSpec((24, 24, LANES), lambda cb, place: (0, 0, place[0] * blocks + cb)),
                pl.BlockSpec((49, LANES), lambda cb, place: (0, cb)),
                pl.BlockSpec(mask.shape, lambda cb, place: (0, 0, 0)),
            ],
            out_specs=(
                pl.BlockSpec((1, *x.shape), lambda cb, place: (place[0] if slots == 2 else 0, 0, 0)),
                pl.BlockSpec((56, LANES), lambda cb, place: (0, cb)),
            ),
            scratch_shapes=[
                pltpu.VMEM((54, 64, LANES), F32),
                pltpu.VMEM((2, 49, 8, LANES), F32),
                pltpu.VMEM((49, 8, LANES), F32),
                pltpu.VMEM((24, 48, LANES), F32),
            ],
        ),
        **conv_params(4 * 49 * 48 * 48 * width * 8, 25_000_000),
    )(place, grad, top, bot, x, cot, pool, taps, mask)


def join_kernel(place_ref, branch_ref, scale_ref, own_ref, other_ref, own_out, other_out, pool_out, pair_ref):
    rows, width = 48, own_ref.shape[1] // 4
    for g, (src, dst) in enumerate(((own_ref, own_out), (other_ref, other_out))):
        side = place_ref[0] if g == 0 else 1 - place_ref[0]
        at = pl.ds(pl.multiple_of(side * width, LANES), width)
        scale = scale_ref[:, at]
        for q in range(2):
            total = None
            for w in (2 * q, 2 * q + 1):
                field = src[:, w * width : (w + 1) * width].astype(F32)
                field = field + scale * branch_ref[w * rows : (w + 1) * rows, at]
                dst[0, :, w * width : (w + 1) * width] = field.astype(BF)
                total = field if total is None else total + field
            for n in range(width // LANES):
                pair_ref[q, n] = total[:, n * LANES : (n + 1) * LANES]
                even = pair_ref[q, n, pl.ds(0, 24, stride=2), :]
                odd = pair_ref[q, n, pl.ds(1, 24, stride=2), :]
                lane = pl.ds(pl.multiple_of(side * width + n * LANES, LANES), LANES)
                pool_out[q, :, lane] = (even + odd) * 0.25


def join_branch(branch, scale, own, other, place):
    width = own.shape[1] // 48
    raw = pl.BlockSpec((48, 4 * width), lambda i, place: (0, i))
    return pl.pallas_call(
        join_kernel,
        out_shape=(
            jax.ShapeDtypeStruct((2, *own.shape), BF),
            jax.ShapeDtypeStruct((1, *own.shape), BF),
            jax.ShapeDtypeStruct((24, 24, 2 * width), F32),
        ),
        grid_spec=pltpu.PrefetchScalarGridSpec(
            num_scalar_prefetch=1,
            grid=(12,),
            in_specs=[
                pl.BlockSpec((4 * 48, 2 * width), lambda i, place: (i, 0)),
                pl.BlockSpec((1, 2 * width), lambda i, place: (0, 0)),
                raw,
                raw,
            ],
            out_specs=(
                pl.BlockSpec((1, 48, 4 * width), lambda i, place: (place[0], 0, i)),
                pl.BlockSpec((1, 48, 4 * width), lambda i, place: (0, 0, i)),
                pl.BlockSpec((2, 24, 2 * width), lambda i, place: (i, 0, 0)),
            ),
            scratch_shapes=[pltpu.VMEM((2, width // LANES, 48, LANES), F32)],
        ),
        **conv_params(10_000_000, 40_000_000),
    )(place, branch, scale, own, other)


def scaled_kernel(place_ref, pool_ref, branch_ref, scale_ref, own_ref, other_ref, out_ref, sum_ref, pair_ref):
    rows, width = 48, own_ref.shape[1] // 4

    @pl.when(pl.program_id(0) == 0)
    def _():
        sum_ref[...] = jnp.zeros_like(sum_ref)

    for g, src in enumerate((own_ref, other_ref)):
        side = place_ref[0] if g == 0 else 1 - place_ref[0]
        at = pl.ds(pl.multiple_of(side * width, LANES), width)
        scale = scale_ref[:, at]
        for q in range(2):
            quarter = pool_ref[q, :, at] * 0.25
            for n in range(width // LANES):
                part = quarter[:, n * LANES : (n + 1) * LANES]
                pair_ref[q, n, pl.ds(0, 24, stride=2), :] = part
                pair_ref[q, n, pl.ds(1, 24, stride=2), :] = part
            spread = jnp.concatenate([pair_ref[q, n] for n in range(width // LANES)], axis=1)
            for w in (2 * q, 2 * q + 1):
                here = slice(w * rows, (w + 1) * rows)
                grad = src[:, w * width : (w + 1) * width].astype(F32) + spread
                part = grad * branch_ref[here, at]
                sum_ref[:, at] += jnp.sum(part.reshape(6, 8, width), axis=0)
                out_ref[here, at] = (grad * scale).astype(BF)


def scaled_grads(pool, branch, scale, own, other, place):
    width = own.shape[1] // 48
    raw = pl.BlockSpec((48, 4 * width), lambda i, place: (0, i))
    return pl.pallas_call(
        scaled_kernel,
        out_shape=(
            jax.ShapeDtypeStruct(branch.shape, BF),
            jax.ShapeDtypeStruct((8, 2 * width), F32),
        ),
        grid_spec=pltpu.PrefetchScalarGridSpec(
            num_scalar_prefetch=1,
            grid=(12,),
            in_specs=[
                pl.BlockSpec((2, 24, 2 * width), lambda i, place: (i, 0, 0)),
                pl.BlockSpec((4 * 48, 2 * width), lambda i, place: (i, 0)),
                pl.BlockSpec((1, 2 * width), lambda i, place: (0, 0)),
                raw,
                raw,
            ],
            out_specs=(
                pl.BlockSpec((4 * 48, 2 * width), lambda i, place: (i, 0)),
                pl.BlockSpec((8, 2 * width), lambda i, place: (0, 0)),
            ),
            scratch_shapes=[pltpu.VMEM((2, width // LANES, 48, LANES), F32)],
        ),
        **conv_params(10_000_000, 40_000_000),
    )(place, pool, branch, scale, own, other)


CHUNK = 256
PAIRS = 2
WIDE = PAIRS * LANES
NT = (((1,), (1,)), ((), ()))
TN = (((0,), (0,)), ((), ()))


def dot(left, right, dims):
    return lax.dot_general(left, right, dims, preferred_element_type=F32)


NN = (((1,), (0,)), ((), ()))


def lane_half(shape, side):
    lanes = lax.broadcasted_iota(jnp.int32, shape, len(shape) - 1)
    return (lanes < 64) if side == 0 else (lanes >= 64)


def fill_window(win_ref, before, own, after):
    count = own.shape[0]
    win_ref[0:count] = before[...]
    win_ref[count : 2 * count] = own[...]
    win_ref[2 * count : 3 * count] = after[...]
    win_ref[3 * count :] = jnp.zeros_like(win_ref[3 * count :])


def attend_kernel(first_ref, last_ref, q_ref, kb_ref, k_ref, ka_ref, vb_ref, v_ref, va_ref,
                  klab_ref, qlab_ref, out_ref, total_ref, kw_ref, vw_ref):
    fill_window(kw_ref, kb_ref, k_ref, ka_ref)
    fill_window(vw_ref, vb_ref, v_ref, va_ref)
    heads = [(pair, side) for pair in range(PAIRS) for side in range(2)]
    lanes = [slice(pair * LANES, (pair + 1) * LANES) for pair in range(PAIRS)]
    for n in range(3):
        rows = slice(n * 192, (n + 1) * 192)
        q = q_ref[rows, :] * jnp.asarray(0.125, BF)
        q_half = []
        for pair, side in heads:
            own = q[:, lanes[pair]]
            q_half.append(jnp.where(lane_half(own.shape, side), own, jnp.zeros_like(own)))
        q_lab = qlab_ref[n, 0:1, :]

        def chunk(c, carry):
            at = pl.ds(pl.multiple_of(c * CHUNK, CHUNK), CHUNK)
            same = klab_ref[at, 0:1] == q_lab
            new = []
            scores = [
                jnp.where(same, dot(kw_ref[at, lanes[pair]], q_half[i], NT), NEG)
                for i, (pair, side) in enumerate(heads)
            ]
            for i, (pair, side) in enumerate(heads):
                top, total, acc = carry[i]
                best = jnp.maximum(top, jnp.max(scores[i], axis=0, keepdims=True))
                p = jnp.exp(scores[i] - best)
                shrink = jnp.exp(top - best)
                total = total * shrink + jnp.sum(p, axis=0, keepdims=True)
                acc = acc * shrink + dot(vw_ref[at, lanes[pair]], p.astype(BF), TN)
                new.append((best, total, acc))
            return tuple(new)

        start = (jnp.full((1, 192), NEG, F32), jnp.zeros((1, 192), F32), jnp.zeros((LANES, 192), F32))
        done = lax.fori_loop(first_ref[n], last_ref[n], chunk, (start,) * len(heads))
        for pair in range(PAIRS):
            outs = []
            for side in range(2):
                top, total, acc = done[2 * pair + side]
                outs.append(acc * (1.0 / total))
                total_ref[pair, n, side : side + 1, :] = top + jnp.log(total)
            both = jnp.concatenate([outs[0][:64], outs[1][64:]], axis=0)
            out_ref[rows, lanes[pair]] = both.T.astype(BF)


def attend(q, k, v, around, qlab, klab, first, last):
    count, width = q.shape
    window = -(-3 * count // CHUNK) * CHUNK
    block = pl.BlockSpec((count, WIDE), lambda p, *_: (0, p))
    stats = pl.BlockSpec((PAIRS, 3, 2, 192), lambda p, *_: (p, 0, 0, 0))
    return pl.pallas_call(
        attend_kernel,
        out_shape=(
            jax.ShapeDtypeStruct(q.shape, BF),
            jax.ShapeDtypeStruct((width // LANES, 3, 2, 192), F32),
        ),
        grid_spec=pltpu.PrefetchScalarGridSpec(
            num_scalar_prefetch=2,
            grid=(width // WIDE,),
            in_specs=[block] * 7
            + [
                pl.BlockSpec(klab.shape, lambda p, *_: (0, 0)),
                pl.BlockSpec(qlab.shape, lambda p, *_: (0, 0, 0)),
            ],
            out_specs=(block, stats),
            scratch_shapes=[pltpu.VMEM((window, WIDE), BF), pltpu.VMEM((window, WIDE), BF)],
        ),
        **conv_params(20_000_000_000, 20_000_000),
    )(first, last, q, around[0], k, around[1], around[2], v, around[3], klab, qlab)


def attend_back_kernel(first_ref, last_ref, q_ref, kb_ref, k_ref, ka_ref, vb_ref, v_ref, va_ref,
                       do_ref, o_ref, total_ref, klab_ref, qlab_ref,
                       dq_ref, dk_ref, dv_ref, before_ref, after_ref,
                       kw_ref, vw_ref, dkw_ref, dvw_ref):
    count = q_ref.shape[0]
    fill_window(kw_ref, kb_ref, k_ref, ka_ref)
    fill_window(vw_ref, vb_ref, v_ref, va_ref)
    dkw_ref[...] = jnp.zeros_like(dkw_ref)
    dvw_ref[...] = jnp.zeros_like(dvw_ref)
    heads = [(pair, side) for pair in range(PAIRS) for side in range(2)]
    lanes = [slice(pair * LANES, (pair + 1) * LANES) for pair in range(PAIRS)]
    for n in range(3):
        rows = slice(n * 192, (n + 1) * 192)
        q = q_ref[rows, :] * jnp.asarray(0.125, BF)
        do = do_ref[rows, :]
        halves = [lane_half((192, LANES), side) for side in range(2)]
        q_half = [jnp.where(halves[s], q[:, lanes[p]], jnp.zeros((), BF)) for p, s in heads]
        do_half = [jnp.where(halves[s], do[:, lanes[p]], jnp.zeros((), BF)) for p, s in heads]
        q_lab = qlab_ref[n, 0:1, :]
        flow = do.astype(F32) * o_ref[rows, :].astype(F32)
        delta = []
        for p in range(PAIRS):
            turned = flow[:, lanes[p]].T
            delta += [jnp.sum(turned[s * 64 : s * 64 + 64], axis=0, keepdims=True) for s in range(2)]

        def chunk(c, carry):
            at = pl.ds(pl.multiple_of(c * CHUNK, CHUNK), CHUNK)
            same = klab_ref[at, 0:1] == q_lab
            kcs = [kw_ref[at, lanes[pair]] for pair in range(PAIRS)]
            vcs = [vw_ref[at, lanes[pair]] for pair in range(PAIRS)]
            scores = [dot(kcs[p], q_half[i], NT) for i, (p, s) in enumerate(heads)]
            dps = [dot(vcs[p], do_half[i], NT) for i, (p, s) in enumerate(heads)]
            ps, dss = [], []
            for i, (p, s) in enumerate(heads):
                raised = jnp.where(same, scores[i] - total_ref[p, n, s : s + 1, :], NEG)
                ps.append(jnp.exp(raised))
            for i, (p, s) in enumerate(heads):
                dss.append((ps[i] * (dps[i] - delta[i])).astype(BF))
            low = [item.astype(BF) for item in ps]
            dqs = []
            for p in range(PAIRS):
                e, o = 2 * p, 2 * p + 1
                dvw_ref[at, lanes[p]] += dot(low[e], do_half[e], NN) + dot(low[o], do_half[o], NN)
                dkw_ref[at, lanes[p]] += dot(dss[e], q_half[e], NN) + dot(dss[o], q_half[o], NN)
                two = [dot(dss[e], kcs[p], TN), dot(dss[o], kcs[p], TN)]
                dqs.append(carry[p] + jnp.where(lane_half((192, LANES), 0), two[0], two[1]))
            return tuple(dqs)

        dqs = lax.fori_loop(
            first_ref[n], last_ref[n], chunk, tuple(jnp.zeros((192, LANES), F32) for _ in range(PAIRS))
        )
        for pair in range(PAIRS):
            dq_ref[rows, lanes[pair]] = (dqs[pair] * 0.125).astype(BF)
    dk_ref[...] = dkw_ref[count : 2 * count, :]
    dv_ref[...] = dvw_ref[count : 2 * count, :]
    before_ref[0] = dkw_ref[0:count, :].astype(BF)
    before_ref[1] = dvw_ref[0:count, :].astype(BF)
    after_ref[0] = dkw_ref[2 * count : 3 * count, :].astype(BF)
    after_ref[1] = dvw_ref[2 * count : 3 * count, :].astype(BF)


def attend_back(q, k, v, around, grad, out, total, qlab, klab, first, last):
    count, width = q.shape
    window = -(-3 * count // CHUNK) * CHUNK
    block = pl.BlockSpec((count, WIDE), lambda p, *_: (0, p))
    stats = pl.BlockSpec((PAIRS, 3, 2, 192), lambda p, *_: (p, 0, 0, 0))
    pair = pl.BlockSpec((2, count, WIDE), lambda p, *_: (0, 0, p))
    return pl.pallas_call(
        attend_back_kernel,
        out_shape=(
            jax.ShapeDtypeStruct(q.shape, BF),
            jax.ShapeDtypeStruct(q.shape, F32),
            jax.ShapeDtypeStruct(q.shape, F32),
            jax.ShapeDtypeStruct((2, count, width), BF),
            jax.ShapeDtypeStruct((2, count, width), BF),
        ),
        grid_spec=pltpu.PrefetchScalarGridSpec(
            num_scalar_prefetch=2,
            grid=(width // WIDE,),
            in_specs=[block] * 9
            + [
                stats,
                pl.BlockSpec(klab.shape, lambda p, *_: (0, 0)),
                pl.BlockSpec(qlab.shape, lambda p, *_: (0, 0, 0)),
            ],
            out_specs=(block, block, block, pair, pair),
            scratch_shapes=[
                pltpu.VMEM((window, WIDE), BF),
                pltpu.VMEM((window, WIDE), BF),
                pltpu.VMEM((window, WIDE), F32),
                pltpu.VMEM((window, WIDE), F32),
            ],
        ),
        **conv_params(20_000_000_000, 20_000_000),
    )(first, last, q, around[0], k, around[1], around[2], v, around[3], grad, out, total, klab, qlab)


def on_device(
    lo_in,
    hi_in,
    image_ids,
    cn_kernel,
    cn_gain,
    cn_w1,
    cn_w2,
    cn_scale,
    ad_proj,
    ad_kernel,
    gate_w1,
    gate_w2,
    ln1_gain,
    qkv,
    out_proj,
    ln2_gain,
    fc1,
    fc2,
    d_lo_out,
    d_hi_out,
):
    micro_count, row_count, col_count, d_shard = lo_in.shape
    hi_rows = hi_in.shape[1]
    hi_cols = HCOLS
    c_shard = hi_in.shape[3] // hi_cols
    d_own, c_own = 2 * d_shard, 2 * c_shard
    tok_count = row_count * col_count
    pix_count = hi_rows * hi_cols
    mine = lax.axis_index("mb")
    row_start = lax.axis_index("tile") * row_count
    head_count = d_own // HDIM

    fast = c_shard % LANES == 0 and lax.axis_size("tp") == 1
    hi_raw = hi_in.reshape(2, hi_rows, hi_cols * c_shard)
    hi_own, hi_other = swap_micro(hi_raw)
    up, down = rim_pair(hi_raw, RIM, 1)
    own_rims, other_rims = swap_micro(jnp.stack([up, down], axis=1))
    lo_in, d_lo_out, cn_scale, ad_kernel, hi_other = together(
        lo_in, d_lo_out, cn_scale, ad_kernel, hi_other
    )
    lo_low = in_order(*swap_micro(lo_in.reshape(2, tok_count, d_shard)), 1)
    lo_field = lo_low.astype(F32)

    hid_shard, gh_shard, ff_shard = cn_w1.shape[1], gate_w1.shape[1], fc1.shape[1]
    mlp = gather_all(jnp.concatenate([cn_w1, cn_w2.T], axis=1))
    def apply(left, pair):
        return jnp.concatenate([matmul(left, pair[0]), matmul(left, pair[1])], axis=1)

    def apply_t(left, pair):
        width = pair[0].shape[1]
        return matmul_nt(left[:, :width], pair[0]) + matmul_nt(left[:, width:], pair[1])

    def cols(values):
        width = values.shape[1] // 2
        return [values[:, :width], values[:, width:]]

    canvas_ids = lax.dynamic_index_in_dim(image_ids, mine, 0, keepdims=False)
    small_ids = row_labels(canvas_ids, row_start, row_count, 1)
    lo_mid = small_ids[1 : 1 + row_count]
    hi_ids = row_labels(jnp.repeat(canvas_ids, 2), 2 * row_start, hi_rows, 3)
    hi_mid = hi_ids[3 : 3 + hi_rows]

    def both_shards(shard, axis):
        return in_order(shard, lax.ppermute(shard, "mb", SWAP), axis)

    other_kernel = lax.ppermute(cn_kernel, "mb", SWAP)
    conv_taps = in_order(cn_kernel, other_kernel, 1)
    ad_taps = both_shards(ad_kernel, 1)
    hi_scale = both_shards(cn_scale, 0).astype(F32)

    own_place = mine.reshape(1).astype(jnp.int32)
    other_place = 1 - own_place
    seen = jnp.stack([(hi_ids[a : a + hi_rows] == hi_mid).astype(F32) for a in range(7)])
    mask = jnp.broadcast_to(seen[:, :, None], (7, hi_rows, LANES))
    own_taps, other_taps = cn_kernel.astype(F32), other_kernel.astype(F32)

    def natural(own, other):
        shape = (-1, hi_cols, c_shard)
        return in_order(own.reshape(shape), other.reshape(shape), 2)

    if fast:
        conv_flat = conv_forward(hi_own, *own_rims, own_taps, mask, own_place)
        conv_flat = conv_forward(hi_other, *other_rims, other_taps, mask, other_place, conv_flat)
    else:
        hi_field = natural(hi_own, hi_other)
        hi_pad = jnp.concatenate(
            [
                natural(own_rims[0], other_rims[0])[-3:],
                hi_field,
                natural(own_rims[1], other_rims[1])[:3],
            ]
        )
        conv_low = depthwise(hi_pad, conv_taps, hi_ids, hi_mid, 7, False).astype(BF)
        conv_flat = conv_low.transpose(1, 0, 2).reshape(pix_count, c_own)
    conv_full = features(conv_flat)
    normed, norm_pull = jax.vjp(layer_norm, conv_full.astype(F32), cn_gain.astype(F32))
    normed_low, mlp, gate_w2 = together(normed.astype(BF), mlp, gate_w2)
    mlp_in = [mlp[g, :, :hid_shard] for g in range(2)]
    mlp_out = [mlp[g, :, hid_shard:] for g in range(2)]
    ad_shard = jnp.concatenate([ad_proj, gate_w1], axis=1)
    narrow = gate_w2.shape[1]
    vit = gather_all(
        jnp.concatenate(
            [
                gate_w2.T,
                qkv[0],
                qkv[1],
                qkv[2],
                out_proj.T,
                fc1,
                fc2.T,
                ad_shard.reshape(narrow, -1),
            ],
            axis=1,
        )
    )
    cuts = np.cumsum([0, gh_shard, d_shard, d_shard, d_shard, d_shard, ff_shard, ff_shard])
    gate_out, q_w, k_w, v_w, out_w, ff_in, ff_out = [
        [vit[g, :, int(cuts[i]) : int(cuts[i + 1])] for g in range(2)] for i in range(7)
    ]
    ad_gate = vit[:, :, int(cuts[7]) :].reshape(2, -1, ad_shard.shape[1])
    ad_matrix = [ad_gate[g, :, :d_shard] for g in range(2)]
    gate_in = [ad_gate[g, :, d_shard:] for g in range(2)]

    inner_act, inner_slope = zip(*[gelu_pair(matmul(normed_low, mlp_in[g])) for g in range(2)])
    branch = partial_sums(
        matmul_nt(inner_act[0], mlp_out[0]) + matmul_nt(inner_act[1], mlp_out[1])
    )
    if fast:
        hi_mine, hi_sent, pooled = join_branch(branch, hi_scale[None], hi_own, hi_other, own_place)
        pooled = pooled.transpose(1, 0, 2)
    else:
        branch_rows = branch.reshape(hi_cols, hi_rows, c_own).transpose(1, 0, 2)
        hi_sum = hi_field.astype(F32) + hi_scale * branch_rows
        pooled = jnp.mean(hi_sum.reshape(row_count, 2, col_count, 2, c_own), axis=(1, 3))
    pooled_full = features(pooled.reshape(tok_count, c_own).astype(BF))
    pooled_full, d_hi_out = together(pooled_full, d_hi_out)
    cot_own, cot_other = swap_micro(d_hi_out.reshape(2, hi_rows, hi_cols * c_shard))
    proj_low = apply(pooled_full, ad_matrix).astype(BF)
    proj_pad = rim_rows(proj_low.reshape(row_count, col_count, d_own), 1)
    local_conv = depthwise(proj_pad, ad_taps, small_ids, lo_mid, 3, False).reshape(
        tok_count, d_own
    )
    gate_hidden, gate_slope = gelu_pair(apply(pooled_full, gate_in))
    gate_val = jnp.tanh(partial_sums(apply_t(gate_hidden, gate_out)))
    mixed_one = lo_field + gate_val * local_conv
    mixed_full = features(mixed_one.astype(BF))
    norm_one, first_pull = jax.vjp(layer_norm, mixed_full.astype(F32), ln1_gain.astype(F32))
    norm_low = norm_one.astype(BF)
    queries = apply(norm_low, q_w).astype(BF)
    key_rows = apply(norm_low, k_w).astype(BF)
    value_rows = apply(norm_low, v_w).astype(BF)
    around = rim_pair(key_rows, tok_count, 0) + rim_pair(value_rows, tok_count, 0)
    near = row_labels(canvas_ids, row_start, row_count, row_count)
    key_tok = jnp.repeat(near, col_count)
    window = -(-3 * tok_count // CHUNK) * CHUNK
    key_tok = jnp.pad(key_tok, (0, window - 3 * tok_count), constant_values=-2)
    key_lab = jnp.broadcast_to(key_tok[:, None], (window, LANES))
    query_lab = jnp.broadcast_to(jnp.repeat(lo_mid, col_count).reshape(3, 1, 192), (3, 8, 192))
    edge = jnp.arange(3 * row_count)
    first_row = jnp.min(jnp.where(near[None] == lo_mid[::8][:, None], edge, 3 * row_count), axis=1)
    last_row = jnp.max(jnp.where(near[None] == lo_mid[7::8][:, None], edge, -1), axis=1) + 1
    first = (first_row * col_count // CHUNK).astype(jnp.int32)
    last = ((last_row * col_count + CHUNK - 1) // CHUNK).astype(jnp.int32)
    attended, log_total = attend(
        queries, key_rows, value_rows, around, query_lab, key_lab, first, last
    )
    mixed_two = mixed_one + partial_sums(apply_t(attended, out_w))
    if fast:
        hi_got = lax.ppermute(hi_sent, "mb", SWAP)
        mixed_two, hi_got, cot_other = together(mixed_two, hi_got, cot_other)
    mixed2_full = features(mixed_two.astype(BF))
    norm_two, second_pull = jax.vjp(layer_norm, mixed2_full.astype(F32), ln2_gain.astype(F32))
    norm2_low = norm_two.astype(BF)
    ff_hidden, ff_slope = gelu_pair(apply(norm2_low, ff_in))
    lo_result = (mixed_two + partial_sums(apply_t(ff_hidden, ff_out))).astype(BF)

    grad_low = in_order(*swap_micro(d_lo_out.reshape(2, tok_count, d_shard)), 1)
    grad_out = grad_low.astype(F32)
    ff_grad_full = features(grad_low)
    ff_pre_grad = (apply(ff_grad_full, ff_out) * ff_slope.astype(F32)).astype(BF)
    second_grad = partial_sums(apply_t(ff_pre_grad, ff_in)).astype(BF)
    back_two, grad_ln2 = second_pull(features(second_grad).astype(F32))
    p_ff = stacked_grads([norm2_low, ff_grad_full], [ff_pre_grad, ff_hidden])
    grad_two, p_ff = together(grad_out + own_slice(back_two), p_ff)
    s_ff = reduce_tiles(p_ff)
    att_grad_full = features(grad_two.astype(BF))
    att_grad = apply(att_grad_full, out_w).astype(BF)
    query_grad, key_own, value_own, to_before, to_after = attend_back(
        queries, key_rows, value_rows, around, att_grad, attended, log_total, query_lab, key_lab, first, last
    )
    devices = lax.axis_size("tile")
    steps = [(i, i + 1) for i in range(devices - 1)]
    from_before = lax.ppermute(to_after, "tile", steps)
    from_after = lax.ppermute(to_before, "tile", [(j, i) for i, j in steps])
    key_grad, value_grad = [
        (own + from_before[i].astype(F32) + from_after[i].astype(F32)).astype(BF)
        for i, own in enumerate((key_own, value_own))
    ]
    first_grad = partial_sums(
        apply_t(query_grad, q_w) + apply_t(key_grad, k_w) + apply_t(value_grad, v_w)
    ).astype(BF)
    back_one, grad_ln1 = first_pull(features(first_grad).astype(F32))
    grad_one = grad_two + own_slice(back_one)
    gate_pre_grad = (grad_one * local_conv * (1.0 - gate_val * gate_val)).astype(BF)
    gate_grad_full = features(gate_pre_grad)
    p_att = stacked_grads(
        [gate_grad_full, norm_low, att_grad_full],
        [gate_hidden, jnp.concatenate([query_grad, key_grad, value_grad], axis=1), attended],
    )
    hidden_grad = (apply(gate_grad_full, gate_out) * gate_slope.astype(F32)).astype(BF)
    local_grad = (grad_one * gate_val).astype(BF).reshape(row_count, col_count, d_own)
    local_pad = rim_rows(local_grad, 1)
    proj_grad = (
        depthwise(local_pad, ad_taps, small_ids, lo_mid, 3, True)
        .reshape(tok_count, d_own)
        .astype(BF)
    )
    grad_ad_kernel = tap_grads(proj_pad, local_grad, small_ids, lo_mid, 3)
    p_ad = matmul_tn(pooled_full, jnp.concatenate([proj_grad, hidden_grad], axis=1)).astype(BF)
    pooled_grad = partial_sums(apply_t(hidden_grad, gate_in) + apply_t(proj_grad, ad_matrix))
    pooled_grad, p_att, p_ad, s_ff = together(pooled_grad, p_att, p_ad, s_ff)
    s_att, s_ad = reduce_tiles(p_att), reduce_tiles(p_ad)
    pool_cols = pooled_grad.reshape(row_count, col_count, c_own).transpose(1, 0, 2)
    if fast:
        scaled_grad, scale_parts = scaled_grads(
            pool_cols, branch, hi_scale[None], cot_own, cot_other, own_place
        )
        grad_scale = jnp.sum(scale_parts, axis=0)
    else:
        spread_grad = jnp.repeat(jnp.repeat(pool_cols.transpose(1, 0, 2) * 0.25, 2, 0), 2, 1)
        hi_grad = natural(cot_own, cot_other).astype(F32) + spread_grad
        grad_cols = hi_grad.transpose(1, 0, 2).reshape(pix_count, c_own)
        grad_scale = jnp.sum(grad_cols * branch, axis=0)
        scaled_grad = (grad_cols * hi_scale).astype(BF)
    branch_full = lax.optimization_barrier(features(scaled_grad))
    p_w2 = [matmul_tn(branch_full, act).astype(BF) for act in inner_act]
    branch_full, *p_w2 = together(branch_full, *p_w2)
    s_w2 = [reduce_tiles(item) for item in p_w2]
    grad_first = (matmul(branch_full, mlp_out[0]) * inner_slope[0].astype(F32)).astype(BF)
    w1_first = matmul_tn(normed_low, grad_first).astype(BF)
    branch_full, w1_first = together(branch_full, w1_first)
    grad_second = (matmul(branch_full, mlp_out[1]) * inner_slope[1].astype(F32)).astype(BF)
    w1_second = matmul_tn(normed_low, grad_second).astype(BF)
    w1_sent = jnp.where(mine == 0, w1_second, w1_first)
    w1_own = jnp.where(mine == 0, w1_first, w1_second)
    grad_second, w1_sent = together(grad_second, w1_sent)
    w1_got = lax.ppermute(w1_sent, "mb", SWAP)
    normed_grad = partial_sums(
        matmul_nt(grad_first, mlp_in[0]) + matmul_nt(grad_second, mlp_in[1])
    ).astype(BF)
    back_conv, grad_cn_gain = norm_pull(features(normed_grad).astype(F32))
    conv_grad = own_slice(back_conv).astype(BF)
    conv_cols = conv_grad.reshape(hi_cols, hi_rows, c_own)
    grad_up, grad_down = rim_pair(conv_cols, RIM, 1)
    if fast:
        ghi_sent, taps_other = conv_backward(
            conv_grad, grad_up, grad_down, hi_other, cot_other, pool_cols, other_taps, mask, other_place, 1, BF
        )
        w1_sum = (w1_own.astype(F32) + w1_got.astype(F32)).astype(BF)
        conv_grad, w1_sum, ghi_sent = together(conv_grad, w1_sum, ghi_sent)
        ghi_mine, taps_own = conv_backward(
            conv_grad, grad_up, grad_down, hi_own, cot_own, pool_cols, own_taps, mask, own_place, 2, F32
        )
        grad_cn_kernel = in_order(taps_own[:49], taps_other[:49], 1)
    else:
        conv_grad = conv_cols.transpose(1, 0, 2)
        conv_pad = jnp.concatenate(
            [grad_up.transpose(1, 0, 2)[-3:], conv_grad, grad_down.transpose(1, 0, 2)[:3]]
        )
        hi_back = hi_grad + depthwise(conv_pad, conv_taps, hi_ids, hi_mid, 7, True)
        grad_cn_kernel = tap_grads(hi_pad, conv_grad, hi_ids, hi_mid, 7)
        w1_sum = (w1_own.astype(F32) + w1_got.astype(F32)).astype(BF)
    g_w1 = reduce_tiles(w1_sum).astype(F32)

    def leave(values, kind):
        own, sent = halves(values)
        other = lax.ppermute(sent.astype(BF), "mb", SWAP)
        return both_micro(own.astype(kind), other.astype(kind))

    lo_stack = leave(lo_result.reshape(row_count, col_count, d_own), BF)
    if fast:
        ghi_got = lax.ppermute(ghi_sent, "mb", SWAP)
        hi_stack, ghi_stack = [
            lax.dynamic_update_slice_in_dim(stack, got.astype(stack.dtype), 1 - mine, 0)
            for stack, got in ((hi_mine, hi_got), (ghi_mine, ghi_got))
        ]
    else:
        hi_stack = leave(hi_sum, BF)
        ghi_stack = leave(hi_back, F32)
    glo_stack = leave(grad_one.reshape(row_count, col_count, d_own), F32)

    (g_w2,) = settle(jnp.concatenate(s_w2, axis=1), (hid_shard,))
    g_fc1, g_fc2 = settle(s_ff, (ff_shard, ff_shard))
    g_gate_w2, g_q, g_k, g_v, g_out = settle(s_att, (gh_shard, d_shard, d_shard, d_shard, d_shard))
    g_ad, g_gate_w1 = settle(s_ad, (d_shard, gh_shard))

    own_terms, sent_terms = zip(*[halves(item) for item in (grad_cn_kernel, grad_scale, grad_ad_kernel)])
    gains = [grad_cn_gain, grad_ln1, grad_ln2]
    flat, sent = [
        jnp.concatenate([item.reshape(-1) for item in (*terms, *gains)])
        for terms in (own_terms, sent_terms)
    ]
    flat = sum_everywhere(flat + lax.ppermute(sent, "mb", SWAP))
    sizes = np.cumsum([0] + [item.size for item in (*own_terms, *gains)])
    g_kernel, g_scale, g_taps, *gain_sums = [
        flat[int(sizes[i]) : int(sizes[i + 1])].reshape(item.shape)
        for i, item in enumerate((*own_terms, *gains))
    ]

    return (
        lo_stack,
        hi_stack.reshape(2, hi_rows, 1, hi_cols * c_shard),
        glo_stack,
        ghi_stack.reshape(2, hi_rows, 1, hi_cols * c_shard),
        g_kernel,
        gain_sums[0],
        g_w1,
        g_w2.T,
        g_scale,
        g_ad,
        g_taps,
        g_gate_w1,
        g_gate_w2.T,
        gain_sums[1],
        jnp.stack([g_q, g_k, g_v]),
        g_out.T,
        gain_sums[2],
        g_fc1,
        g_fc2.T,
    )


def solution(mesh):
    tiles, mps = mesh.shape["tile"], mesh.shape["mp"]
    fine = Mesh(mesh.devices.reshape(tiles, 2, mps // 2), ("tile", "mb", "tp"))
    mp = ("mb", "tp")
    in_specs = (
        P(None, "tile", None, mp),
        P(None, "tile", mp, None),
        P(),
        P(None, mp),
        P(),
        P("tile", mp),
        P(mp, "tile"),
        P(mp),
        P("tile", mp),
        P(None, mp),
        P("tile", mp),
        P(mp, "tile"),
        P(),
        P(None, "tile", mp),
        P(mp, "tile"),
        P(),
        P("tile", mp),
        P(mp, "tile"),
        P(None, "tile", None, mp),
        P(None, "tile", mp, None),
    )
    out_specs = (
        P(None, "tile", None, mp),
        P(None, "tile", mp, None),
        P(None, "tile", None, mp),
        P(None, "tile", mp, None),
        P(None, mp),
        P(),
        P("tile", mp),
        P(mp, "tile"),
        P(mp),
        P("tile", mp),
        P(None, mp),
        P("tile", mp),
        P(mp, "tile"),
        P(),
        P(None, "tile", mp),
        P(mp, "tile"),
        P(),
        P("tile", mp),
        P(mp, "tile"),
    )
    return jax.shard_map(
        on_device, mesh=fine, in_specs=in_specs, out_specs=out_specs, check_vma=False
    )
```

```python
import functools

import jax
import jax.numpy as jnp
import numpy as np
from jax import lax
from jax.experimental import pallas as pl
from jax.experimental.pallas import tpu as pltpu
from jax.sharding import Mesh
from jax.sharding import PartitionSpec as P

HDIM = 64
IMG_ROWS = 24
HCOLS = 48

EPS = 1e-06
NEG = -1e30
BF = jnp.bfloat16
F32 = jnp.float32
TILE = ("chip", "core")
ALL = ("mb", *TILE)


def tile_count():
    return lax.axis_size("chip") * lax.axis_size("core")


def rim_pair(value, width, axis):
    devices, length = tile_count(), value.shape[axis]
    up = [(i, (i + 1) % devices) for i in range(devices - 1)]
    down = [(j, i) for i, j in up]
    before = lax.ppermute(lax.slice_in_dim(value, length - width, length, axis=axis), TILE, up)
    after = lax.ppermute(lax.slice_in_dim(value, 0, width, axis=axis), TILE, down)
    return before, after


def rim_rows(value, width):
    devices, length = tile_count(), value.shape[0]
    up = [(i, (i + 1) % devices) for i in range(devices - 1)]
    down = [(j, i) for i, j in up]
    before = lax.ppermute(value[length - width :], TILE, up)
    after = lax.ppermute(value[:width], TILE, down)
    return jnp.concatenate([before, value, after], axis=0)


def matmul(left, right):
    return jnp.dot(left, right, preferred_element_type=F32)


def matmul_tn(left, right):
    return lax.dot_general(left, right, (((0,), (0,)), ((), ())), preferred_element_type=F32)


def matmul_nt(left, right):
    return lax.dot_general(left, right, (((1,), (1,)), ((), ())), preferred_element_type=F32)


def layer_norm(values, gain_vec):
    average = jnp.mean(values, axis=-1, keepdims=True)
    centered = values - average
    variance = jnp.mean(centered * centered, axis=-1, keepdims=True)
    return centered * lax.rsqrt(variance + EPS) * gain_vec


def gelu_pair(values):
    cdf = 0.5 + 0.5 * lax.erf(values * 0.7071067811865476)
    slope = cdf + values * (0.3989422804014327 * jnp.exp(-0.5 * values * values))
    return (values * cdf).astype(BF), slope.astype(BF)


def features(values):
    parts = lax.axis_size("tp")
    if parts == 1:
        return values
    rows, width = values.shape
    full = lax.all_gather(values.reshape(rows, 2, width // 2), "tp", axis=2)
    return full.reshape(rows, parts * width)


def partial_sums(values):
    parts = lax.axis_size("tp")
    if parts == 1:
        return values
    rows, width = values.shape
    split = values.reshape(rows, 2, parts, width // (2 * parts))
    return lax.psum_scatter(split, "tp", scatter_dimension=2).reshape(rows, width // parts)


def own_slice(values):
    parts = lax.axis_size("tp")
    if parts == 1:
        return values
    rows, width = values.shape
    split = values.reshape(rows, 2, parts, width // (2 * parts))
    own = lax.dynamic_index_in_dim(split, lax.axis_index("tp"), 2, keepdims=False)
    return own.reshape(rows, width // parts)


SWAP = [(0, 1), (1, 0)]


def swap_micro(values):
    mine = lax.axis_index("mb")
    own = lax.dynamic_index_in_dim(values, mine, 0, keepdims=False)
    sent = lax.dynamic_index_in_dim(values, 1 - mine, 0, keepdims=False)
    return own, lax.ppermute(sent, "mb", SWAP)


def in_order(own, other, axis):
    first = lax.axis_index("mb") == 0
    return jnp.concatenate(
        [jnp.where(first, own, other), jnp.where(first, other, own)], axis=axis
    )


def both_micro(own, other):
    first = lax.axis_index("mb") == 0
    return jnp.stack([jnp.where(first, own, other), jnp.where(first, other, own)])


def halves(values):
    width = values.shape[-1] // 2
    mine = lax.axis_index("mb")
    own = lax.dynamic_slice_in_dim(values, mine * width, width, values.ndim - 1)
    sent = lax.dynamic_slice_in_dim(values, (1 - mine) * width, width, values.ndim - 1)
    return own, sent


def row_labels(labels, first_row, count_rows, margin):
    padded = jnp.pad(labels, (margin, margin), constant_values=-1)
    return lax.dynamic_slice_in_dim(padded, first_row, count_rows + 2 * margin, 0)


def depthwise(padded, kernel, ids_pad, ids_mid, tap_size, flipped):
    margin = tap_size // 2
    row_count = ids_mid.shape[0]
    col_count = padded.shape[1]
    widened = jnp.pad(padded, ((0, 0), (margin, margin), (0, 0)))
    summed = jnp.zeros((row_count, col_count, padded.shape[2]), F32)
    for a in range(tap_size):
        same_img = (ids_pad[a : a + row_count] == ids_mid)[:, None, None]
        shifted = jnp.where(same_img, widened[a : a + row_count].astype(F32), 0.0)
        for b in range(tap_size):
            tap_index = (
                (tap_size - 1 - a) * tap_size + (tap_size - 1 - b) if flipped else a * tap_size + b
            )
            summed = summed + kernel[tap_index].astype(F32) * shifted[:, b : b + col_count]
    return summed


def tap_grads(padded, grad_low, ids_pad, ids_mid, tap_size):
    margin = tap_size // 2
    row_count = ids_mid.shape[0]
    col_count = padded.shape[1]
    widened = jnp.pad(padded, ((0, 0), (margin, margin), (0, 0)))
    grad_vals = grad_low.astype(F32)
    results = []
    for a in range(tap_size):
        same_img = (ids_pad[a : a + row_count] == ids_mid)[:, None, None]
        shifted = jnp.where(same_img, widened[a : a + row_count].astype(F32), 0.0)
        for b in range(tap_size):
            results.append(jnp.sum(shifted[:, b : b + col_count] * grad_vals, axis=(0, 1)))
    return jnp.stack(results)


def stacked_kernel(cuts, *refs):
    count = len(cuts) - 1
    step = pl.program_id(0)
    for i in range(count):

        @pl.when((step >= cuts[i]) & (step < cuts[i + 1]))
        def _(i=i):
            refs[-1][...] = dot(refs[i][...], refs[count + i][...], NN).astype(BF)


def stacked_grads(lefts, rights):
    widths = [item.shape[1] for item in rights]
    step_width = next((size for size in (512, 256) if not any(width % size for width in widths)), 0)
    if not step_width:
        return jnp.concatenate(
            [matmul_tn(left, right).astype(BF) for left, right in zip(lefts, rights)], axis=1
        )
    tokens, rows = lefts[0].shape
    cuts = [int(item) for item in np.cumsum([0] + [width // step_width for width in widths])]

    def column(i):
        return lambda step: (0, jnp.clip(step - cuts[i], 0, cuts[i + 1] - cuts[i] - 1))

    return pl.pallas_call(
        functools.partial(stacked_kernel, cuts),
        out_shape=jax.ShapeDtypeStruct((rows, sum(widths)), BF),
        grid=(cuts[-1],),
        in_specs=[pl.BlockSpec((rows, tokens), lambda step: (0, 0)) for _ in lefts]
        + [pl.BlockSpec((tokens, step_width), column(i)) for i in range(len(rights))],
        out_specs=pl.BlockSpec((rows, step_width), lambda step: (0, step)),
        **conv_params(5 * tokens * rows * sum(widths), 2 * rows * sum(widths)),
    )(*[left.T for left in lefts], *rights)


def gather_all(shard):
    full = lax.all_gather(shard, ALL, axis=0)
    return full.reshape(2, -1, shard.shape[1])


def reduce_tiles(terms):
    return lax.psum_scatter(terms, TILE, scatter_dimension=0, tiled=True)


def core_sum(terms):
    width = terms.shape[1] // 2
    core = lax.axis_index("core")
    own = lax.dynamic_slice_in_dim(terms, core * width, width, 1)
    sent = lax.dynamic_slice_in_dim(terms, (1 - core) * width, width, 1)
    got = lax.ppermute(sent, "core", SWAP)
    return (own.astype(F32) + got.astype(F32)).astype(BF)


def reduce_chips(terms):
    both = lax.psum_scatter(terms, "chip", scatter_dimension=0, tiled=True)
    rows = both.shape[0] // 2
    core = lax.axis_index("core")
    own = lax.dynamic_slice_in_dim(both, core * rows, rows, 0)
    sent = lax.dynamic_slice_in_dim(both, (1 - core) * rows, rows, 0)
    got = lax.ppermute(sent, "core", SWAP)
    first = core == 0
    return jnp.concatenate([jnp.where(first, own, got), jnp.where(first, got, own)], axis=1)


def settle(summed, widths):
    own, sent, start = [], [], 0
    for width in widths:
        mine, other = halves(summed[:, start : start + 2 * width])
        own.append(mine)
        sent.append(other)
        start += 2 * width
    got = lax.ppermute(jnp.concatenate(sent, axis=1), "mb", SWAP)
    cuts = [int(item) for item in np.cumsum([0] + list(widths))]
    return [
        item.astype(F32) + got[:, cuts[i] : cuts[i + 1]].astype(F32) for i, item in enumerate(own)
    ]


def sum_everywhere(flat):
    devices = tile_count()
    if devices & (devices - 1):
        return lax.psum(flat, TILE)
    bit = 1
    while bit < devices:
        flat = flat + lax.ppermute(flat, TILE, [(i, i ^ bit) for i in range(devices)])
        bit *= 2
    return flat


def together(*values):
    return lax.optimization_barrier(values)


LANES = 128
RIM = 8
VMEM_LIMIT = 60 * 1024 * 1024


def conv_params(flops=0, moved=0):
    return dict(
        compiler_params=pltpu.CompilerParams(vmem_limit_bytes=VMEM_LIMIT),
        cost_estimate=pl.CostEstimate(flops=flops, bytes_accessed=moved, transcendentals=0),
    )


def masked_taps(taps_ref, mask_ref, km_ref, sub, flip):
    for a in range(7):
        seen = mask_ref[a, pl.ds(sub * 8, 8), :]
        for b in range(7):
            tap = 48 - (a * 7 + b) if flip else a * 7 + b
            km_ref[a * 7 + b] = taps_ref[tap : tap + 1, :] * seen


def conv_kernel(place_ref, x_ref, top_ref, bot_ref, taps_ref, mask_ref, out_ref, xs_ref, km_ref):
    rows, width = 48, x_ref.shape[1] // 48
    cb = pl.program_id(0)

    @pl.when(cb == 0)
    def _():
        for w in (0, 1, 2, 51, 52, 53):
            xs_ref[w] = jnp.zeros_like(xs_ref[w])

    def fill(w, carry):
        at = pl.ds(pl.multiple_of(w * width + cb * LANES, LANES), LANES)
        xs_ref[w + 3, 0:RIM, :] = top_ref[:, at].astype(F32)
        xs_ref[w + 3, RIM : RIM + rows, :] = x_ref[:, at].astype(F32)
        xs_ref[w + 3, RIM + rows :, :] = bot_ref[:, at].astype(F32)
        return carry

    lax.fori_loop(0, 48, fill, 0)

    def band(t, carry):
        for s in range(2):
            masked_taps(taps_ref, mask_ref, km_ref.at[s], t * 2 + s, False)

        def block(i, carry):
            w0 = i * 8
            accs = []
            for s in range(2):
                acc = [jnp.zeros((8, LANES), F32) for _ in range(8)]
                for a in range(7):
                    start = t * 16 + (s * 8 + RIM - 3 + a)
                    x = [xs_ref[w0 + j, pl.ds(start, 8), :] for j in range(14)]
                    for b in range(7):
                        k = km_ref[s, a * 7 + b]
                        for j in range(8):
                            acc[j] = acc[j] + k * x[j + b]
                accs.append(acc)
            for j in range(8):
                both = jnp.concatenate([accs[0][j], accs[1][j]], axis=0).astype(BF)
                out_ref[pl.ds(pl.multiple_of((w0 + j) * rows + t * 16, 16), 16), :] = both
            return carry

        lax.fori_loop(0, 6, block, 0)
        return carry

    lax.fori_loop(0, 3, band, 0)


def conv_forward(x, top, bot, taps, mask, place, into=None):
    width = x.shape[1] // 48
    blocks = width // LANES
    whole = lambda cb, place: (0, 0)
    half = lambda cb, place: (0, place[0] * blocks + cb)
    extra = [] if into is None else [into]
    kernel = conv_kernel if into is None else conv_kernel_into
    return pl.pallas_call(
        kernel,
        out_shape=jax.ShapeDtypeStruct((48 * 48, 2 * width), BF),
        grid_spec=pltpu.PrefetchScalarGridSpec(
            num_scalar_prefetch=1,
            grid=(blocks,),
            in_specs=[
                pl.BlockSpec(x.shape, whole),
                pl.BlockSpec(top.shape, whole),
                pl.BlockSpec(bot.shape, whole),
                pl.BlockSpec((49, LANES), lambda cb, place: (0, cb)),
                pl.BlockSpec(mask.shape, lambda cb, place: (0, 0, 0)),
            ]
            + [pl.BlockSpec(memory_space=pl.ANY)] * len(extra),
            out_specs=pl.BlockSpec((48 * 48, LANES), half),
            scratch_shapes=[
                pltpu.VMEM((54, 64, LANES), F32),
                pltpu.VMEM((2, 49, 8, LANES), F32),
            ],
        ),
        input_output_aliases={} if into is None else {6: 0},
        **conv_params(54_000_000 * width, 12_000_000),
    )(place, x, top, bot, taps, mask, *extra)


def conv_kernel_into(place_ref, x_ref, top_ref, bot_ref, taps_ref, mask_ref, into_ref, *rest):
    conv_kernel(place_ref, x_ref, top_ref, bot_ref, taps_ref, mask_ref, *rest)


def back_kernel(place_ref, g_ref, top_ref, bot_ref, x_ref, cot_ref, pool_ref, taps_ref, mask_ref,
                out_ref, tap_out_ref, gs_ref, km_ref, tacc_ref, sp_ref):
    rows, width = 48, x_ref.shape[1] // 48
    cb = pl.program_id(0)

    @pl.when(cb == 0)
    def _():
        for w in (0, 1, 2, 51, 52, 53):
            gs_ref[w] = jnp.zeros_like(gs_ref[w])

    tacc_ref[...] = jnp.zeros_like(tacc_ref)

    def fill(w, carry):
        gs_ref[w + 3, 0:RIM, :] = top_ref[w].astype(F32)
        own = pl.ds(pl.multiple_of(w * rows, rows), rows)
        gs_ref[w + 3, RIM : RIM + rows, :] = g_ref[own, :].astype(F32)
        gs_ref[w + 3, RIM + rows :, :] = bot_ref[w].astype(F32)
        return carry

    lax.fori_loop(0, 48, fill, 0)

    def spread(q, carry):
        quarter = pool_ref[q] * 0.25
        sp_ref[q, pl.ds(0, 24, stride=2), :] = quarter
        sp_ref[q, pl.ds(1, 24, stride=2), :] = quarter
        return carry

    lax.fori_loop(0, 24, spread, 0)

    def band(t, carry):
        for s in range(2):
            masked_taps(taps_ref, mask_ref, km_ref.at[s], t * 2 + s, True)

        def block(i, carry):
            w0 = i * 8
            ats = [
                pl.ds(pl.multiple_of((w0 + j) * width + cb * LANES, LANES), LANES) for j in range(8)
            ]
            band_rows = pl.ds(pl.multiple_of(t * 16, 16), 16)
            vals = [x_ref[band_rows, at].astype(F32) for at in ats]
            accs = []
            for s in range(2):
                acc = [jnp.zeros((8, LANES), F32) for _ in range(8)]
                v = [val[s * 8 : s * 8 + 8] for val in vals]
                for a in range(7):
                    start = t * 16 + (s * 8 + RIM - 3 + a)
                    g = [gs_ref[w0 + j, pl.ds(start, 8), :] for j in range(14)]
                    seen = mask_ref[a, pl.ds(t * 16 + s * 8, 8), :]
                    vm = [item * seen for item in v]
                    for b in range(7):
                        k = km_ref[s, a * 7 + b]
                        tap = None
                        for j in range(8):
                            acc[j] = acc[j] + k * g[j + b]
                            term = vm[j] * g[j + b]
                            tap = term if tap is None else tap + term
                        tacc_ref[48 - (a * 7 + b)] += tap
                accs.append(acc)
            for j in range(8):
                both = jnp.concatenate([accs[0][j], accs[1][j]], axis=0)
                total = both + cot_ref[band_rows, ats[j]].astype(F32)
                total = total + sp_ref[i * 4 + j // 2, band_rows, :]
                out_ref[0, band_rows, ats[j]] = total.astype(out_ref.dtype)
            return carry

        lax.fori_loop(0, 6, block, 0)
        return carry

    lax.fori_loop(0, 3, band, 0)
    tap_out_ref[0:49, :] = jnp.sum(tacc_ref[...], axis=1)


def conv_backward(grad, top, bot, x, cot, pool, taps, mask, place, slots, kind):
    width = x.shape[1] // 48
    blocks = width // LANES
    whole = lambda cb, place: (0, 0)
    half = lambda cb, place: (0, place[0] * blocks + cb)
    return pl.pallas_call(
        back_kernel,
        out_shape=(
            jax.ShapeDtypeStruct((slots, *x.shape), kind),
            jax.ShapeDtypeStruct((56, width), F32),
        ),
        grid_spec=pltpu.PrefetchScalarGridSpec(
            num_scalar_prefetch=1,
            grid=(blocks,),
            in_specs=[
                pl.BlockSpec((48 * 48, LANES), half),
                pl.BlockSpec((48, RIM, LANES), lambda cb, place: (0, 0, place[0] * blocks + cb)),
                pl.BlockSpec((48, RIM, LANES), lambda cb, place: (0, 0, place[0] * blocks + cb)),
                pl.BlockSpec(x.shape, whole),
                pl.BlockSpec(cot.shape, whole),
                pl.BlockSpec((24, 24, LANES), lambda cb, place: (0, 0, place[0] * blocks + cb)),
                pl.BlockSpec((49, LANES), lambda cb, place: (0, cb)),
                pl.BlockSpec(mask.shape, lambda cb, place: (0, 0, 0)),
            ],
            out_specs=(
                pl.BlockSpec((1, *x.shape), lambda cb, place: (place[0] if slots == 2 else 0, 0, 0)),
                pl.BlockSpec((56, LANES), lambda cb, place: (0, cb)),
            ),
            scratch_shapes=[
                pltpu.VMEM((54, 64, LANES), F32),
                pltpu.VMEM((2, 49, 8, LANES), F32),
                pltpu.VMEM((49, 8, LANES), F32),
                pltpu.VMEM((24, 48, LANES), F32),
            ],
        ),
        **conv_params(90_000_000 * width, 25_000_000),
    )(place, grad, top, bot, x, cot, pool, taps, mask)


def join_kernel(place_ref, branch_ref, scale_ref, own_ref, other_ref, own_out, other_out, pool_out, pair_ref):
    rows, width = 48, own_ref.shape[1] // 4
    for g, (src, dst) in enumerate(((own_ref, own_out), (other_ref, other_out))):
        side = place_ref[0] if g == 0 else 1 - place_ref[0]
        at = pl.ds(pl.multiple_of(side * width, LANES), width)
        scale = scale_ref[:, at]
        for q in range(2):
            total = None
            for w in (2 * q, 2 * q + 1):
                field = src[:, w * width : (w + 1) * width].astype(F32)
                field = field + scale * branch_ref[w * rows : (w + 1) * rows, at]
                dst[0, :, w * width : (w + 1) * width] = field.astype(BF)
                total = field if total is None else total + field
            for n in range(width // LANES):
                pair_ref[q, n] = total[:, n * LANES : (n + 1) * LANES]
                even = pair_ref[q, n, pl.ds(0, 24, stride=2), :]
                odd = pair_ref[q, n, pl.ds(1, 24, stride=2), :]
                lane = pl.ds(pl.multiple_of(side * width + n * LANES, LANES), LANES)
                pool_out[q, :, lane] = (even + odd) * 0.25


def join_branch(branch, scale, own, other, place):
    width = own.shape[1] // 48
    raw = pl.BlockSpec((48, 4 * width), lambda i, place: (0, i))
    return pl.pallas_call(
        join_kernel,
        out_shape=(
            jax.ShapeDtypeStruct((2, *own.shape), BF),
            jax.ShapeDtypeStruct((1, *own.shape), BF),
            jax.ShapeDtypeStruct((24, 24, 2 * width), F32),
        ),
        grid_spec=pltpu.PrefetchScalarGridSpec(
            num_scalar_prefetch=1,
            grid=(12,),
            in_specs=[
                pl.BlockSpec((4 * 48, 2 * width), lambda i, place: (i, 0)),
                pl.BlockSpec((1, 2 * width), lambda i, place: (0, 0)),
                raw,
                raw,
            ],
            out_specs=(
                pl.BlockSpec((1, 48, 4 * width), lambda i, place: (place[0], 0, i)),
                pl.BlockSpec((1, 48, 4 * width), lambda i, place: (0, 0, i)),
                pl.BlockSpec((2, 24, 2 * width), lambda i, place: (i, 0, 0)),
            ),
            scratch_shapes=[pltpu.VMEM((2, width // LANES, 48, LANES), F32)],
        ),
        **conv_params(10_000_000, 40_000_000),
    )(place, branch, scale, own, other)


def scaled_kernel(place_ref, pool_ref, branch_ref, scale_ref, own_ref, other_ref, out_ref, sum_ref, pair_ref):
    rows, width = 48, own_ref.shape[1] // 4

    @pl.when(pl.program_id(0) == 0)
    def _():
        sum_ref[...] = jnp.zeros_like(sum_ref)

    for g, src in enumerate((own_ref, other_ref)):
        side = place_ref[0] if g == 0 else 1 - place_ref[0]
        at = pl.ds(pl.multiple_of(side * width, LANES), width)
        scale = scale_ref[:, at]
        for q in range(2):
            quarter = pool_ref[q, :, at] * 0.25
            for n in range(width // LANES):
                part = quarter[:, n * LANES : (n + 1) * LANES]
                pair_ref[q, n, pl.ds(0, 24, stride=2), :] = part
                pair_ref[q, n, pl.ds(1, 24, stride=2), :] = part
            spread = jnp.concatenate([pair_ref[q, n] for n in range(width // LANES)], axis=1)
            for w in (2 * q, 2 * q + 1):
                here = slice(w * rows, (w + 1) * rows)
                grad = src[:, w * width : (w + 1) * width].astype(F32) + spread
                part = grad * branch_ref[here, at]
                sum_ref[:, at] += jnp.sum(part.reshape(6, 8, width), axis=0)
                out_ref[here, at] = (grad * scale).astype(BF)


def scaled_grads(pool, branch, scale, own, other, place):
    width = own.shape[1] // 48
    raw = pl.BlockSpec((48, 4 * width), lambda i, place: (0, i))
    return pl.pallas_call(
        scaled_kernel,
        out_shape=(
            jax.ShapeDtypeStruct(branch.shape, BF),
            jax.ShapeDtypeStruct((8, 2 * width), F32),
        ),
        grid_spec=pltpu.PrefetchScalarGridSpec(
            num_scalar_prefetch=1,
            grid=(12,),
            in_specs=[
                pl.BlockSpec((2, 24, 2 * width), lambda i, place: (i, 0, 0)),
                pl.BlockSpec((4 * 48, 2 * width), lambda i, place: (i, 0)),
                pl.BlockSpec((1, 2 * width), lambda i, place: (0, 0)),
                raw,
                raw,
            ],
            out_specs=(
                pl.BlockSpec((4 * 48, 2 * width), lambda i, place: (i, 0)),
                pl.BlockSpec((8, 2 * width), lambda i, place: (0, 0)),
            ),
            scratch_shapes=[pltpu.VMEM((2, width // LANES, 48, LANES), F32)],
        ),
        **conv_params(10_000_000, 40_000_000),
    )(place, pool, branch, scale, own, other)


CHUNK = 256
PAIRS = 2
WIDE = PAIRS * LANES
NT = (((1,), (1,)), ((), ()))
TN = (((0,), (0,)), ((), ()))


def dot(left, right, dims):
    return lax.dot_general(left, right, dims, preferred_element_type=F32)


NN = (((1,), (0,)), ((), ()))


def lane_half(shape, side):
    lanes = lax.broadcasted_iota(jnp.int32, shape, len(shape) - 1)
    return (lanes < 64) if side == 0 else (lanes >= 64)


def fill_window(win_ref, before, own, after):
    count = own.shape[0]
    win_ref[0:count] = before[...]
    win_ref[count : 2 * count] = own[...]
    win_ref[2 * count : 3 * count] = after[...]
    win_ref[3 * count :] = jnp.zeros_like(win_ref[3 * count :])


def attend_kernel(first_ref, last_ref, q_ref, kb_ref, k_ref, ka_ref, vb_ref, v_ref, va_ref,
                  klab_ref, qlab_ref, out_ref, total_ref, kw_ref, vw_ref):
    fill_window(kw_ref, kb_ref, k_ref, ka_ref)
    fill_window(vw_ref, vb_ref, v_ref, va_ref)
    heads = [(pair, side) for pair in range(PAIRS) for side in range(2)]
    lanes = [slice(pair * LANES, (pair + 1) * LANES) for pair in range(PAIRS)]
    for n in range(3):
        rows = slice(n * 192, (n + 1) * 192)
        q = q_ref[rows, :] * jnp.asarray(0.125, BF)
        q_half = []
        for pair, side in heads:
            own = q[:, lanes[pair]]
            q_half.append(jnp.where(lane_half(own.shape, side), own, jnp.zeros_like(own)))
        q_lab = qlab_ref[n, 0:1, :]

        def chunk(c, carry):
            at = pl.ds(pl.multiple_of(c * CHUNK, CHUNK), CHUNK)
            same = klab_ref[at, 0:1] == q_lab
            new = []
            scores = [
                jnp.where(same, dot(kw_ref[at, lanes[pair]], q_half[i], NT), NEG)
                for i, (pair, side) in enumerate(heads)
            ]
            for i, (pair, side) in enumerate(heads):
                top, total, acc = carry[i]
                best = jnp.maximum(top, jnp.max(scores[i], axis=0, keepdims=True))
                p = jnp.exp(scores[i] - best)
                shrink = jnp.exp(top - best)
                total = total * shrink + jnp.sum(p, axis=0, keepdims=True)
                acc = acc * shrink + dot(vw_ref[at, lanes[pair]], p.astype(BF), TN)
                new.append((best, total, acc))
            return tuple(new)

        start = (jnp.full((1, 192), NEG, F32), jnp.zeros((1, 192), F32), jnp.zeros((LANES, 192), F32))
        done = lax.fori_loop(first_ref[n], last_ref[n], chunk, (start,) * len(heads))
        for pair in range(PAIRS):
            outs = []
            for side in range(2):
                top, total, acc = done[2 * pair + side]
                outs.append(acc * (1.0 / total))
                total_ref[pair, n, side : side + 1, :] = top + jnp.log(total)
            both = jnp.concatenate([outs[0][:64], outs[1][64:]], axis=0)
            out_ref[rows, lanes[pair]] = both.T.astype(BF)


def attend(q, k, v, around, qlab, klab, first, last):
    count, width = q.shape
    window = -(-3 * count // CHUNK) * CHUNK
    block = pl.BlockSpec((count, WIDE), lambda p, *_: (0, p))
    stats = pl.BlockSpec((PAIRS, 3, 2, 192), lambda p, *_: (p, 0, 0, 0))
    return pl.pallas_call(
        attend_kernel,
        out_shape=(
            jax.ShapeDtypeStruct(q.shape, BF),
            jax.ShapeDtypeStruct((width // LANES, 3, 2, 192), F32),
        ),
        grid_spec=pltpu.PrefetchScalarGridSpec(
            num_scalar_prefetch=2,
            grid=(width // WIDE,),
            in_specs=[block] * 7
            + [
                pl.BlockSpec(klab.shape, lambda p, *_: (0, 0)),
                pl.BlockSpec(qlab.shape, lambda p, *_: (0, 0, 0)),
            ],
            out_specs=(block, stats),
            scratch_shapes=[pltpu.VMEM((window, WIDE), BF), pltpu.VMEM((window, WIDE), BF)],
        ),
        **conv_params(40_000_000 * width, 20_000_000),
    )(first, last, q, around[0], k, around[1], around[2], v, around[3], klab, qlab)


def attend_back_kernel(first_ref, last_ref, q_ref, kb_ref, k_ref, ka_ref, vb_ref, v_ref, va_ref,
                       do_ref, o_ref, total_ref, klab_ref, qlab_ref,
                       dq_ref, dk_ref, dv_ref, before_ref, after_ref,
                       kw_ref, vw_ref, dkw_ref, dvw_ref):
    count = q_ref.shape[0]
    fill_window(kw_ref, kb_ref, k_ref, ka_ref)
    fill_window(vw_ref, vb_ref, v_ref, va_ref)
    dkw_ref[...] = jnp.zeros_like(dkw_ref)
    dvw_ref[...] = jnp.zeros_like(dvw_ref)
    heads = [(pair, side) for pair in range(PAIRS) for side in range(2)]
    lanes = [slice(pair * LANES, (pair + 1) * LANES) for pair in range(PAIRS)]
    for n in range(3):
        rows = slice(n * 192, (n + 1) * 192)
        q = q_ref[rows, :] * jnp.asarray(0.125, BF)
        do = do_ref[rows, :]
        halves = [lane_half((192, LANES), side) for side in range(2)]
        q_half = [jnp.where(halves[s], q[:, lanes[p]], jnp.zeros((), BF)) for p, s in heads]
        do_half = [jnp.where(halves[s], do[:, lanes[p]], jnp.zeros((), BF)) for p, s in heads]
        q_lab = qlab_ref[n, 0:1, :]
        flow = do.astype(F32) * o_ref[rows, :].astype(F32)
        delta = []
        for p in range(PAIRS):
            turned = flow[:, lanes[p]].T
            delta += [jnp.sum(turned[s * 64 : s * 64 + 64], axis=0, keepdims=True) for s in range(2)]

        def chunk(c, carry):
            at = pl.ds(pl.multiple_of(c * CHUNK, CHUNK), CHUNK)
            same = klab_ref[at, 0:1] == q_lab
            kcs = [kw_ref[at, lanes[pair]] for pair in range(PAIRS)]
            vcs = [vw_ref[at, lanes[pair]] for pair in range(PAIRS)]
            scores = [dot(kcs[p], q_half[i], NT) for i, (p, s) in enumerate(heads)]
            dps = [dot(vcs[p], do_half[i], NT) for i, (p, s) in enumerate(heads)]
            ps, dss = [], []
            for i, (p, s) in enumerate(heads):
                raised = jnp.where(same, scores[i] - total_ref[p, n, s : s + 1, :], NEG)
                ps.append(jnp.exp(raised))
            for i, (p, s) in enumerate(heads):
                dss.append((ps[i] * (dps[i] - delta[i])).astype(BF))
            low = [item.astype(BF) for item in ps]
            dqs = []
            for p in range(PAIRS):
                e, o = 2 * p, 2 * p + 1
                dvw_ref[at, lanes[p]] += dot(low[e], do_half[e], NN) + dot(low[o], do_half[o], NN)
                dkw_ref[at, lanes[p]] += dot(dss[e], q_half[e], NN) + dot(dss[o], q_half[o], NN)
                two = [dot(dss[e], kcs[p], TN), dot(dss[o], kcs[p], TN)]
                dqs.append(carry[p] + jnp.where(lane_half((192, LANES), 0), two[0], two[1]))
            return tuple(dqs)

        dqs = lax.fori_loop(
            first_ref[n], last_ref[n], chunk, tuple(jnp.zeros((192, LANES), F32) for _ in range(PAIRS))
        )
        for pair in range(PAIRS):
            dq_ref[rows, lanes[pair]] = (dqs[pair] * 0.125).astype(BF)
    dk_ref[...] = dkw_ref[count : 2 * count, :]
    dv_ref[...] = dvw_ref[count : 2 * count, :]
    before_ref[0] = dkw_ref[0:count, :].astype(BF)
    before_ref[1] = dvw_ref[0:count, :].astype(BF)
    after_ref[0] = dkw_ref[2 * count : 3 * count, :].astype(BF)
    after_ref[1] = dvw_ref[2 * count : 3 * count, :].astype(BF)


def attend_back(q, k, v, around, grad, out, total, qlab, klab, first, last):
    count, width = q.shape
    window = -(-3 * count // CHUNK) * CHUNK
    block = pl.BlockSpec((count, WIDE), lambda p, *_: (0, p))
    stats = pl.BlockSpec((PAIRS, 3, 2, 192), lambda p, *_: (p, 0, 0, 0))
    pair = pl.BlockSpec((2, count, WIDE), lambda p, *_: (0, 0, p))
    return pl.pallas_call(
        attend_back_kernel,
        out_shape=(
            jax.ShapeDtypeStruct(q.shape, BF),
            jax.ShapeDtypeStruct(q.shape, F32),
            jax.ShapeDtypeStruct(q.shape, F32),
            jax.ShapeDtypeStruct((2, count, width), BF),
            jax.ShapeDtypeStruct((2, count, width), BF),
        ),
        grid_spec=pltpu.PrefetchScalarGridSpec(
            num_scalar_prefetch=2,
            grid=(width // WIDE,),
            in_specs=[block] * 9
            + [
                stats,
                pl.BlockSpec(klab.shape, lambda p, *_: (0, 0)),
                pl.BlockSpec(qlab.shape, lambda p, *_: (0, 0, 0)),
            ],
            out_specs=(block, block, block, pair, pair),
            scratch_shapes=[
                pltpu.VMEM((window, WIDE), BF),
                pltpu.VMEM((window, WIDE), BF),
                pltpu.VMEM((window, WIDE), F32),
                pltpu.VMEM((window, WIDE), F32),
            ],
        ),
        **conv_params(55_000_000 * width, 20_000_000),
    )(first, last, q, around[0], k, around[1], around[2], v, around[3], grad, out, total, klab, qlab)


def on_device(
    lo_in,
    hi_in,
    image_ids,
    cn_kernel,
    cn_gain,
    cn_w1,
    cn_w2,
    cn_scale,
    ad_proj,
    ad_kernel,
    gate_w1,
    gate_w2,
    ln1_gain,
    qkv,
    out_proj,
    ln2_gain,
    fc1,
    fc2,
    d_lo_out,
    d_hi_out,
):
    micro_count, row_count, col_count, d_shard = lo_in.shape
    hi_rows = hi_in.shape[1]
    hi_cols = HCOLS
    c_shard = hi_in.shape[3] // hi_cols
    d_own, c_own = 2 * d_shard, 2 * c_shard
    tok_count = row_count * col_count
    pix_count = hi_rows * hi_cols
    mine = lax.axis_index("mb")
    row_start = lax.axis_index(TILE) * row_count
    head_count = d_own // HDIM

    fast = c_shard % LANES == 0 and lax.axis_size("tp") == 1
    hi_raw = hi_in.reshape(2, hi_rows, hi_cols * c_shard)
    hi_own, hi_other = swap_micro(hi_raw)
    up, down = rim_pair(hi_raw, RIM, 1)
    own_rims, other_rims = swap_micro(jnp.stack([up, down], axis=1))
    hid_shard, gh_shard, ff_shard = cn_w1.shape[1], gate_w1.shape[1], fc1.shape[1]
    mlp = gather_all(jnp.concatenate([cn_w1, cn_w2.T, ad_proj, gate_w1], axis=1))
    def apply(left, pair):
        return jnp.concatenate([matmul(left, pair[0]), matmul(left, pair[1])], axis=1)

    def apply_t(left, pair):
        width = pair[0].shape[1]
        return matmul_nt(left[:, :width], pair[0]) + matmul_nt(left[:, width:], pair[1])

    def cols(values):
        width = values.shape[1] // 2
        return [values[:, :width], values[:, width:]]

    canvas_ids = lax.dynamic_index_in_dim(image_ids, mine, 0, keepdims=False)
    small_ids = row_labels(canvas_ids, row_start, row_count, 1)
    lo_mid = small_ids[1 : 1 + row_count]
    hi_ids = row_labels(jnp.repeat(canvas_ids, 2), 2 * row_start, hi_rows, 3)
    hi_mid = hi_ids[3 : 3 + hi_rows]

    def both_shards(shard, axis):
        return in_order(shard, lax.ppermute(shard, "mb", SWAP), axis)

    other_kernel = lax.ppermute(cn_kernel, "mb", SWAP)
    conv_taps = in_order(cn_kernel, other_kernel, 1)

    own_place = mine.reshape(1).astype(jnp.int32)
    other_place = 1 - own_place
    seen = jnp.stack([(hi_ids[a : a + hi_rows] == hi_mid).astype(F32) for a in range(7)])
    mask = jnp.broadcast_to(seen[:, :, None], (7, hi_rows, LANES))
    own_taps, other_taps = cn_kernel.astype(F32), other_kernel.astype(F32)

    def natural(own, other):
        shape = (-1, hi_cols, c_shard)
        return in_order(own.reshape(shape), other.reshape(shape), 2)

    if fast:
        conv_flat = conv_forward(hi_own, *own_rims, own_taps, mask, own_place)
        conv_flat = conv_forward(hi_other, *other_rims, other_taps, mask, other_place, conv_flat)
    else:
        hi_field = natural(hi_own, hi_other)
        hi_pad = jnp.concatenate(
            [
                natural(own_rims[0], other_rims[0])[-3:],
                hi_field,
                natural(own_rims[1], other_rims[1])[:3],
            ]
        )
        conv_low = depthwise(hi_pad, conv_taps, hi_ids, hi_mid, 7, False).astype(BF)
        conv_flat = conv_low.transpose(1, 0, 2).reshape(pix_count, c_own)
    conv_full = features(conv_flat)
    normed, norm_pull = jax.vjp(layer_norm, conv_full.astype(F32), cn_gain.astype(F32))
    normed_low, mlp, gate_w2 = together(normed.astype(BF), mlp, gate_w2)
    mlp_in = [mlp[g, :, :hid_shard] for g in range(2)]
    mlp_out = [mlp[g, :, hid_shard : 2 * hid_shard] for g in range(2)]
    ad_matrix = [mlp[g, :, 2 * hid_shard : 2 * hid_shard + d_shard] for g in range(2)]
    gate_in = [mlp[g, :, 2 * hid_shard + d_shard :] for g in range(2)]
    vit = gather_all(
        jnp.concatenate(
            [
                gate_w2.T,
                qkv[0],
                qkv[1],
                qkv[2],
                out_proj.T,
                fc1,
                fc2.T,
            ],
            axis=1,
        )
    )
    cuts = np.cumsum([0, gh_shard, d_shard, d_shard, d_shard, d_shard, ff_shard, ff_shard])
    gate_out, q_w, k_w, v_w, out_w, ff_in, ff_out = [
        [vit[g, :, int(cuts[i]) : int(cuts[i + 1])] for g in range(2)] for i in range(7)
    ]

    inner_act, inner_slope = zip(*[gelu_pair(matmul(normed_low, mlp_in[g])) for g in range(2)])
    lo_in, d_lo_out, cn_scale, ad_kernel, first_act = together(
        lo_in, d_lo_out, cn_scale, ad_kernel, inner_act[0]
    )
    inner_act = (first_act, inner_act[1])
    lo_low = in_order(*swap_micro(lo_in.reshape(2, tok_count, d_shard)), 1)
    lo_field = lo_low.astype(F32)
    ad_taps = both_shards(ad_kernel, 1)
    hi_scale = both_shards(cn_scale, 0).astype(F32)
    branch = partial_sums(
        matmul_nt(inner_act[0], mlp_out[0]) + matmul_nt(inner_act[1], mlp_out[1])
    )
    if fast:
        hi_mine, hi_sent, pooled = join_branch(branch, hi_scale[None], hi_own, hi_other, own_place)
        pooled = pooled.transpose(1, 0, 2)
    else:
        branch_rows = branch.reshape(hi_cols, hi_rows, c_own).transpose(1, 0, 2)
        hi_sum = hi_field.astype(F32) + hi_scale * branch_rows
        pooled = jnp.mean(hi_sum.reshape(row_count, 2, col_count, 2, c_own), axis=(1, 3))
    pooled_full = features(pooled.reshape(tok_count, c_own).astype(BF))
    pooled_full, d_hi_out = together(pooled_full, d_hi_out)
    cot_own, cot_other = swap_micro(d_hi_out.reshape(2, hi_rows, hi_cols * c_shard))
    proj_low = apply(pooled_full, ad_matrix).astype(BF)
    proj_pad = rim_rows(proj_low.reshape(row_count, col_count, d_own), 1)
    local_conv = depthwise(proj_pad, ad_taps, small_ids, lo_mid, 3, False).reshape(
        tok_count, d_own
    )
    gate_hidden, gate_slope = gelu_pair(apply(pooled_full, gate_in))
    gate_val = jnp.tanh(partial_sums(apply_t(gate_hidden, gate_out)))
    mixed_one = lo_field + gate_val * local_conv
    mixed_full = features(mixed_one.astype(BF))
    norm_one, first_pull = jax.vjp(layer_norm, mixed_full.astype(F32), ln1_gain.astype(F32))
    norm_low = norm_one.astype(BF)
    queries = apply(norm_low, q_w).astype(BF)
    key_rows = apply(norm_low, k_w).astype(BF)
    value_rows = apply(norm_low, v_w).astype(BF)
    around = rim_pair(key_rows, tok_count, 0) + rim_pair(value_rows, tok_count, 0)
    near = row_labels(canvas_ids, row_start, row_count, row_count)
    key_tok = jnp.repeat(near, col_count)
    window = -(-3 * tok_count // CHUNK) * CHUNK
    key_tok = jnp.pad(key_tok, (0, window - 3 * tok_count), constant_values=-2)
    key_lab = jnp.broadcast_to(key_tok[:, None], (window, LANES))
    query_lab = jnp.broadcast_to(jnp.repeat(lo_mid, col_count).reshape(3, 1, 192), (3, 8, 192))
    edge = jnp.arange(3 * row_count)
    first_row = jnp.min(jnp.where(near[None] == lo_mid[::8][:, None], edge, 3 * row_count), axis=1)
    last_row = jnp.max(jnp.where(near[None] == lo_mid[7::8][:, None], edge, -1), axis=1) + 1
    first = (first_row * col_count // CHUNK).astype(jnp.int32)
    last = ((last_row * col_count + CHUNK - 1) // CHUNK).astype(jnp.int32)
    attended, log_total = attend(
        queries, key_rows, value_rows, around, query_lab, key_lab, first, last
    )
    mixed_two = mixed_one + partial_sums(apply_t(attended, out_w))
    if fast:
        hi_got = lax.ppermute(hi_sent, "mb", SWAP)
        mixed_two, hi_got = together(mixed_two, hi_got)
    mixed2_full = features(mixed_two.astype(BF))
    norm_two, second_pull = jax.vjp(layer_norm, mixed2_full.astype(F32), ln2_gain.astype(F32))
    norm2_low = norm_two.astype(BF)
    ff_hidden, ff_slope = gelu_pair(apply(norm2_low, ff_in))
    lo_result = (mixed_two + partial_sums(apply_t(ff_hidden, ff_out))).astype(BF)

    grad_low = in_order(*swap_micro(d_lo_out.reshape(2, tok_count, d_shard)), 1)
    grad_out = grad_low.astype(F32)
    ff_grad_full = features(grad_low)
    ff_pre_grad = (apply(ff_grad_full, ff_out) * ff_slope.astype(F32)).astype(BF)
    second_grad = partial_sums(apply_t(ff_pre_grad, ff_in)).astype(BF)
    back_two, grad_ln2 = second_pull(features(second_grad).astype(F32))
    p_ff = stacked_grads([norm2_low, ff_grad_full], [ff_pre_grad, ff_hidden])
    grad_two, p_ff, cot_other = together(grad_out + own_slice(back_two), p_ff, cot_other)
    s_ff = reduce_tiles(p_ff)
    att_grad_full = features(grad_two.astype(BF))
    att_grad = apply(att_grad_full, out_w).astype(BF)
    query_grad, key_own, value_own, to_before, to_after = attend_back(
        queries, key_rows, value_rows, around, att_grad, attended, log_total, query_lab, key_lab, first, last
    )
    devices = tile_count()
    steps = [(i, i + 1) for i in range(devices - 1)]
    from_before = lax.ppermute(to_after, TILE, steps)
    from_after = lax.ppermute(to_before, TILE, [(j, i) for i, j in steps])
    key_grad, value_grad = [
        (own + from_before[i].astype(F32) + from_after[i].astype(F32)).astype(BF)
        for i, own in enumerate((key_own, value_own))
    ]
    first_grad = partial_sums(
        apply_t(query_grad, q_w) + apply_t(key_grad, k_w) + apply_t(value_grad, v_w)
    ).astype(BF)
    back_one, grad_ln1 = first_pull(features(first_grad).astype(F32))
    grad_one = grad_two + own_slice(back_one)
    gate_pre_grad = (grad_one * local_conv * (1.0 - gate_val * gate_val)).astype(BF)
    gate_grad_full = features(gate_pre_grad)
    p_att = stacked_grads(
        [gate_grad_full, norm_low, att_grad_full],
        [gate_hidden, jnp.concatenate([query_grad, key_grad, value_grad], axis=1), attended],
    )
    hidden_grad = (apply(gate_grad_full, gate_out) * gate_slope.astype(F32)).astype(BF)
    local_grad = (grad_one * gate_val).astype(BF).reshape(row_count, col_count, d_own)
    local_pad = rim_rows(local_grad, 1)
    proj_grad = (
        depthwise(local_pad, ad_taps, small_ids, lo_mid, 3, True)
        .reshape(tok_count, d_own)
        .astype(BF)
    )
    grad_ad_kernel = tap_grads(proj_pad, local_grad, small_ids, lo_mid, 3)
    p_ad = matmul_tn(pooled_full, jnp.concatenate([proj_grad, hidden_grad], axis=1)).astype(BF)
    pooled_grad = partial_sums(apply_t(hidden_grad, gate_in) + apply_t(proj_grad, ad_matrix))
    pooled_grad, p_att, p_ad = together(pooled_grad, p_att, p_ad)
    s_att, s_ad = reduce_tiles(p_att), reduce_tiles(p_ad)
    pool_cols = pooled_grad.reshape(row_count, col_count, c_own).transpose(1, 0, 2)
    if fast:
        scaled_grad, scale_parts = scaled_grads(
            pool_cols, branch, hi_scale[None], cot_own, cot_other, own_place
        )
        grad_scale = jnp.sum(scale_parts, axis=0)
    else:
        spread_grad = jnp.repeat(jnp.repeat(pool_cols.transpose(1, 0, 2) * 0.25, 2, 0), 2, 1)
        hi_grad = natural(cot_own, cot_other).astype(F32) + spread_grad
        grad_cols = hi_grad.transpose(1, 0, 2).reshape(pix_count, c_own)
        grad_scale = jnp.sum(grad_cols * branch, axis=0)
        scaled_grad = (grad_cols * hi_scale).astype(BF)
    branch_full = lax.optimization_barrier(features(scaled_grad))
    first = mine == 0
    p_w2 = [matmul_tn(branch_full, act).astype(BF) for act in inner_act]
    branch_full, *p_w2, s_ff = together(branch_full, *p_w2, s_ff)
    s_w2 = [reduce_tiles(item) for item in p_w2]
    grad_first = (matmul(branch_full, mlp_out[0]) * inner_slope[0].astype(F32)).astype(BF)
    w1_first = matmul_tn(normed_low, grad_first).astype(BF)
    branch_full, w1_first = together(branch_full, w1_first)
    core_first = core_sum(w1_first)
    grad_second = (matmul(branch_full, mlp_out[1]) * inner_slope[1].astype(F32)).astype(BF)
    w1_second = matmul_tn(normed_low, grad_second).astype(BF)
    grad_second, w1_second = together(grad_second, w1_second)
    core_second = core_sum(w1_second)
    normed_grad = partial_sums(
        matmul_nt(grad_first, mlp_in[0]) + matmul_nt(grad_second, mlp_in[1])
    ).astype(BF)
    back_conv, grad_cn_gain = norm_pull(features(normed_grad).astype(F32))
    conv_grad, core_first, core_second = together(
        own_slice(back_conv).astype(BF), core_first, core_second
    )
    w1_sent, w1_own = jnp.where(first, core_second, core_first), jnp.where(first, core_first, core_second)
    w1_got = lax.ppermute(w1_sent, "mb", SWAP)
    conv_cols = conv_grad.reshape(hi_cols, hi_rows, c_own)
    grad_up, grad_down = rim_pair(conv_cols, RIM, 1)
    if fast:
        ghi_sent, taps_other = conv_backward(
            conv_grad, grad_up, grad_down, hi_other, cot_other, pool_cols, other_taps, mask, other_place, 1, BF
        )
        conv_grad, ghi_sent, w1_got = together(conv_grad, ghi_sent, w1_got)
        ghi_mine, taps_own = conv_backward(
            conv_grad, grad_up, grad_down, hi_own, cot_own, pool_cols, own_taps, mask, own_place, 2, F32
        )
        w1_sum = (w1_own.astype(F32) + w1_got.astype(F32)).astype(BF)
        grad_cn_kernel = in_order(taps_own[:49], taps_other[:49], 1)
    else:
        conv_grad = conv_cols.transpose(1, 0, 2)
        conv_pad = jnp.concatenate(
            [grad_up.transpose(1, 0, 2)[-3:], conv_grad, grad_down.transpose(1, 0, 2)[:3]]
        )
        hi_back = hi_grad + depthwise(conv_pad, conv_taps, hi_ids, hi_mid, 7, True)
        grad_cn_kernel = tap_grads(hi_pad, conv_grad, hi_ids, hi_mid, 7)
        w1_sum = (w1_own.astype(F32) + w1_got.astype(F32)).astype(BF)
    w1_sum, s_att, s_ad, *s_w2 = together(w1_sum, s_att, s_ad, *s_w2)

    own_terms, sent_terms = zip(*[halves(item) for item in (grad_cn_kernel, grad_scale, grad_ad_kernel)])
    gains = [grad_cn_gain, grad_ln1, grad_ln2]
    flat, sent = [
        jnp.concatenate([item.reshape(-1) for item in (*terms, *gains)])
        for terms in (own_terms, sent_terms)
    ]
    flat, sent, w1_sum = together(flat, sent, w1_sum)
    g_w1 = reduce_chips(w1_sum).astype(F32)
    flat = flat + lax.ppermute(sent, "mb", SWAP)
    if fast:
        ghi_got = lax.ppermute(ghi_sent, "mb", SWAP)
    flat = sum_everywhere(flat)
    sizes = np.cumsum([0] + [item.size for item in (*own_terms, *gains)])
    g_kernel, g_scale, g_taps, *gain_sums = [
        flat[int(sizes[i]) : int(sizes[i + 1])].reshape(item.shape)
        for i, item in enumerate((*own_terms, *gains))
    ]

    def leave(values, kind):
        own, sent = halves(values)
        other = lax.ppermute(sent.astype(BF), "mb", SWAP)
        return both_micro(own.astype(kind), other.astype(kind))

    lo_stack = leave(lo_result.reshape(row_count, col_count, d_own), BF)
    if fast:
        hi_stack, ghi_stack = [
            lax.dynamic_update_slice_in_dim(stack, got.astype(stack.dtype), 1 - mine, 0)
            for stack, got in ((hi_mine, hi_got), (ghi_mine, ghi_got))
        ]
    else:
        hi_stack = leave(hi_sum, BF)
        ghi_stack = leave(hi_back, F32)
    glo_stack = leave(grad_one.reshape(row_count, col_count, d_own), F32)

    (g_w2,) = settle(jnp.concatenate(s_w2, axis=1), (hid_shard,))
    g_fc1, g_fc2 = settle(s_ff, (ff_shard, ff_shard))
    g_gate_w2, g_q, g_k, g_v, g_out = settle(s_att, (gh_shard, d_shard, d_shard, d_shard, d_shard))
    g_ad, g_gate_w1 = settle(s_ad, (d_shard, gh_shard))

    return (
        lo_stack,
        hi_stack.reshape(2, hi_rows, 1, hi_cols * c_shard),
        glo_stack,
        ghi_stack.reshape(2, hi_rows, 1, hi_cols * c_shard),
        g_kernel,
        gain_sums[0],
        g_w1,
        g_w2.T,
        g_scale,
        g_ad,
        g_taps,
        g_gate_w1,
        g_gate_w2.T,
        gain_sums[1],
        jnp.stack([g_q, g_k, g_v]),
        g_out.T,
        gain_sums[2],
        g_fc1,
        g_fc2.T,
    )


def solution(mesh):
    tiles, mps = mesh.shape["tile"], mesh.shape["mp"]
    fine = Mesh(mesh.devices.reshape(tiles // 2, 2, 2, mps // 2), (*TILE, "mb", "tp"))
    mp = ("mb", "tp")
    in_specs = (
        P(None, TILE, None, mp),
        P(None, TILE, mp, None),
        P(),
        P(None, mp),
        P(),
        P(TILE, mp),
        P(mp, TILE),
        P(mp),
        P(TILE, mp),
        P(None, mp),
        P(TILE, mp),
        P(mp, TILE),
        P(),
        P(None, TILE, mp),
        P(mp, TILE),
        P(),
        P(TILE, mp),
        P(mp, TILE),
        P(None, TILE, None, mp),
        P(None, TILE, mp, None),
    )
    out_specs = (
        P(None, TILE, None, mp),
        P(None, TILE, mp, None),
        P(None, TILE, None, mp),
        P(None, TILE, mp, None),
        P(None, mp),
        P(),
        P(TILE, mp),
        P(mp, TILE),
        P(mp),
        P(TILE, mp),
        P(None, mp),
        P(TILE, mp),
        P(mp, TILE),
        P(),
        P(None, TILE, mp),
        P(mp, TILE),
        P(),
        P(TILE, mp),
        P(mp, TILE),
    )
    return jax.shard_map(
        on_device, mesh=fine, in_specs=in_specs, out_specs=out_specs, check_vma=False
    )
```

```python
import functools

import jax
import jax.numpy as jnp
import numpy as np
from jax import lax
from jax.experimental import pallas as pl
from jax.experimental.pallas import tpu as pltpu
from jax.sharding import Mesh
from jax.sharding import PartitionSpec as P

HDIM = 64
IMG_ROWS = 24
HCOLS = 48

EPS = 1e-06
NEG = -1e30
BF = jnp.bfloat16
F32 = jnp.float32
TILE = ("chip", "core")
ALL = ("mb", *TILE)


def tile_count():
    return lax.axis_size("chip") * lax.axis_size("core")


def rim_pair(value, width, axis):
    devices, length = tile_count(), value.shape[axis]
    up = [(i, (i + 1) % devices) for i in range(devices - 1)]
    down = [(j, i) for i, j in up]
    before = lax.ppermute(lax.slice_in_dim(value, length - width, length, axis=axis), TILE, up)
    after = lax.ppermute(lax.slice_in_dim(value, 0, width, axis=axis), TILE, down)
    return before, after


def rim_rows(value, width):
    devices, length = tile_count(), value.shape[0]
    up = [(i, (i + 1) % devices) for i in range(devices - 1)]
    down = [(j, i) for i, j in up]
    before = lax.ppermute(value[length - width :], TILE, up)
    after = lax.ppermute(value[:width], TILE, down)
    return jnp.concatenate([before, value, after], axis=0)


def matmul(left, right):
    return jnp.dot(left, right, preferred_element_type=F32)


def matmul_tn(left, right):
    return lax.dot_general(left, right, (((0,), (0,)), ((), ())), preferred_element_type=F32)


def matmul_nt(left, right):
    return lax.dot_general(left, right, (((1,), (1,)), ((), ())), preferred_element_type=F32)


def layer_norm(values, gain_vec):
    average = jnp.mean(values, axis=-1, keepdims=True)
    centered = values - average
    variance = jnp.mean(centered * centered, axis=-1, keepdims=True)
    return centered * lax.rsqrt(variance + EPS) * gain_vec


def gelu_pair(values):
    cdf = 0.5 + 0.5 * lax.erf(values * 0.7071067811865476)
    slope = cdf + values * (0.3989422804014327 * jnp.exp(-0.5 * values * values))
    return (values * cdf).astype(BF), slope.astype(BF)


def features(values):
    parts = lax.axis_size("tp")
    if parts == 1:
        return values
    rows, width = values.shape
    full = lax.all_gather(values.reshape(rows, 2, width // 2), "tp", axis=2)
    return full.reshape(rows, parts * width)


def partial_sums(values):
    parts = lax.axis_size("tp")
    if parts == 1:
        return values
    rows, width = values.shape
    split = values.reshape(rows, 2, parts, width // (2 * parts))
    return lax.psum_scatter(split, "tp", scatter_dimension=2).reshape(rows, width // parts)


def own_slice(values):
    parts = lax.axis_size("tp")
    if parts == 1:
        return values
    rows, width = values.shape
    split = values.reshape(rows, 2, parts, width // (2 * parts))
    own = lax.dynamic_index_in_dim(split, lax.axis_index("tp"), 2, keepdims=False)
    return own.reshape(rows, width // parts)


SWAP = [(0, 1), (1, 0)]


def swap_micro(values):
    mine = lax.axis_index("mb")
    own = lax.dynamic_index_in_dim(values, mine, 0, keepdims=False)
    sent = lax.dynamic_index_in_dim(values, 1 - mine, 0, keepdims=False)
    return own, lax.ppermute(sent, "mb", SWAP)


def in_order(own, other, axis):
    first = lax.axis_index("mb") == 0
    return jnp.concatenate(
        [jnp.where(first, own, other), jnp.where(first, other, own)], axis=axis
    )


def both_micro(own, other):
    first = lax.axis_index("mb") == 0
    return jnp.stack([jnp.where(first, own, other), jnp.where(first, other, own)])


def halves(values):
    width = values.shape[-1] // 2
    mine = lax.axis_index("mb")
    own = lax.dynamic_slice_in_dim(values, mine * width, width, values.ndim - 1)
    sent = lax.dynamic_slice_in_dim(values, (1 - mine) * width, width, values.ndim - 1)
    return own, sent


def row_labels(labels, first_row, count_rows, margin):
    padded = jnp.pad(labels, (margin, margin), constant_values=-1)
    return lax.dynamic_slice_in_dim(padded, first_row, count_rows + 2 * margin, 0)


def depthwise(padded, kernel, ids_pad, ids_mid, tap_size, flipped):
    margin = tap_size // 2
    row_count = ids_mid.shape[0]
    col_count = padded.shape[1]
    widened = jnp.pad(padded, ((0, 0), (margin, margin), (0, 0)))
    summed = jnp.zeros((row_count, col_count, padded.shape[2]), F32)
    for a in range(tap_size):
        same_img = (ids_pad[a : a + row_count] == ids_mid)[:, None, None]
        shifted = jnp.where(same_img, widened[a : a + row_count].astype(F32), 0.0)
        for b in range(tap_size):
            tap_index = (
                (tap_size - 1 - a) * tap_size + (tap_size - 1 - b) if flipped else a * tap_size + b
            )
            summed = summed + kernel[tap_index].astype(F32) * shifted[:, b : b + col_count]
    return summed


def tap_grads(padded, grad_low, ids_pad, ids_mid, tap_size):
    margin = tap_size // 2
    row_count = ids_mid.shape[0]
    col_count = padded.shape[1]
    widened = jnp.pad(padded, ((0, 0), (margin, margin), (0, 0)))
    grad_vals = grad_low.astype(F32)
    results = []
    for a in range(tap_size):
        same_img = (ids_pad[a : a + row_count] == ids_mid)[:, None, None]
        shifted = jnp.where(same_img, widened[a : a + row_count].astype(F32), 0.0)
        for b in range(tap_size):
            results.append(jnp.sum(shifted[:, b : b + col_count] * grad_vals, axis=(0, 1)))
    return jnp.stack(results)


def stacked_kernel(cuts, *refs):
    count = len(cuts) - 1
    step = pl.program_id(0)
    for i in range(count):

        @pl.when((step >= cuts[i]) & (step < cuts[i + 1]))
        def _(i=i):
            refs[-1][...] = dot(refs[i][...], refs[count + i][...], NN).astype(BF)


def stacked_grads(lefts, rights):
    widths = [item.shape[1] for item in rights]
    step_width = next((size for size in (512, 256) if not any(width % size for width in widths)), 0)
    if not step_width:
        return jnp.concatenate(
            [matmul_tn(left, right).astype(BF) for left, right in zip(lefts, rights)], axis=1
        )
    tokens, rows = lefts[0].shape
    cuts = [int(item) for item in np.cumsum([0] + [width // step_width for width in widths])]

    def column(i):
        return lambda step: (0, jnp.clip(step - cuts[i], 0, cuts[i + 1] - cuts[i] - 1))

    return pl.pallas_call(
        functools.partial(stacked_kernel, cuts),
        out_shape=jax.ShapeDtypeStruct((rows, sum(widths)), BF),
        grid=(cuts[-1],),
        in_specs=[pl.BlockSpec((rows, tokens), lambda step: (0, 0)) for _ in lefts]
        + [pl.BlockSpec((tokens, step_width), column(i)) for i in range(len(rights))],
        out_specs=pl.BlockSpec((rows, step_width), lambda step: (0, step)),
        **conv_params(5 * tokens * rows * sum(widths), 2 * rows * sum(widths)),
    )(*[left.T for left in lefts], *rights)


def gather_all(shard):
    full = lax.all_gather(shard, ALL, axis=0)
    return full.reshape(2, -1, shard.shape[1])


def reduce_tiles(terms):
    return lax.psum_scatter(terms, TILE, scatter_dimension=0, tiled=True)


def core_sum(terms):
    width = terms.shape[1] // 2
    core = lax.axis_index("core")
    own = lax.dynamic_slice_in_dim(terms, core * width, width, 1)
    sent = lax.dynamic_slice_in_dim(terms, (1 - core) * width, width, 1)
    got = lax.ppermute(sent, "core", SWAP)
    return (own.astype(F32) + got.astype(F32)).astype(BF)


def pass_half(first, second):
    mine = lax.axis_index("mb") == 0
    own = jnp.where(mine, first, second)
    return own, lax.ppermute(jnp.where(mine, second, first), "mb", SWAP)


def add_low(own, got):
    return (own.astype(F32) + got.astype(F32)).astype(BF)


def reduce_chips(terms):
    return lax.psum_scatter(terms, "chip", scatter_dimension=0, tiled=True)


def all_columns(both):
    rows = both.shape[0] // 2
    core = lax.axis_index("core")
    own = lax.dynamic_slice_in_dim(both, core * rows, rows, 0)
    sent = lax.dynamic_slice_in_dim(both, (1 - core) * rows, rows, 0)
    got = lax.ppermute(sent, "core", SWAP)
    first = core == 0
    return jnp.concatenate([jnp.where(first, own, got), jnp.where(first, got, own)], axis=1)


def settle(summed, widths):
    own, sent, start = [], [], 0
    for width in widths:
        mine, other = halves(summed[:, start : start + 2 * width])
        own.append(mine)
        sent.append(other)
        start += 2 * width
    got = lax.ppermute(jnp.concatenate(sent, axis=1), "mb", SWAP)
    cuts = [int(item) for item in np.cumsum([0] + list(widths))]
    return [
        item.astype(F32) + got[:, cuts[i] : cuts[i + 1]].astype(F32) for i, item in enumerate(own)
    ]


def sum_everywhere(flat):
    devices = tile_count()
    if devices & (devices - 1):
        return lax.psum(flat, TILE)
    bit = 1
    while bit < devices:
        flat = flat + lax.ppermute(flat, TILE, [(i, i ^ bit) for i in range(devices)])
        bit *= 2
    return flat


def together(*values):
    return lax.optimization_barrier(values)


LANES = 128
RIM = 8
VMEM_LIMIT = 60 * 1024 * 1024


def conv_params(flops=0, moved=0):
    return dict(
        compiler_params=pltpu.CompilerParams(vmem_limit_bytes=VMEM_LIMIT),
        cost_estimate=pl.CostEstimate(flops=flops, bytes_accessed=moved, transcendentals=0),
    )


def masked_taps(taps_ref, mask_ref, km_ref, sub, flip):
    for a in range(7):
        seen = mask_ref[a, pl.ds(sub * 8, 8), :]
        for b in range(7):
            tap = 48 - (a * 7 + b) if flip else a * 7 + b
            km_ref[a * 7 + b] = taps_ref[tap : tap + 1, :] * seen


def conv_kernel(place_ref, x_ref, top_ref, bot_ref, taps_ref, mask_ref, out_ref, xs_ref, km_ref):
    rows, width = 48, x_ref.shape[1] // 48
    cb = pl.program_id(0)

    @pl.when(cb == 0)
    def _():
        for w in (0, 1, 2, 51, 52, 53):
            xs_ref[w] = jnp.zeros_like(xs_ref[w])

    def fill(w, carry):
        at = pl.ds(pl.multiple_of(w * width + cb * LANES, LANES), LANES)
        xs_ref[w + 3, 0:RIM, :] = top_ref[:, at].astype(F32)
        xs_ref[w + 3, RIM : RIM + rows, :] = x_ref[:, at].astype(F32)
        xs_ref[w + 3, RIM + rows :, :] = bot_ref[:, at].astype(F32)
        return carry

    lax.fori_loop(0, 48, fill, 0)

    def band(t, carry):
        for s in range(2):
            masked_taps(taps_ref, mask_ref, km_ref.at[s], t * 2 + s, False)

        def block(i, carry):
            w0 = i * 8
            accs = []
            for s in range(2):
                acc = [jnp.zeros((8, LANES), F32) for _ in range(8)]
                for a in range(7):
                    start = t * 16 + (s * 8 + RIM - 3 + a)
                    x = [xs_ref[w0 + j, pl.ds(start, 8), :] for j in range(14)]
                    for b in range(7):
                        k = km_ref[s, a * 7 + b]
                        for j in range(8):
                            acc[j] = acc[j] + k * x[j + b]
                accs.append(acc)
            for j in range(8):
                both = jnp.concatenate([accs[0][j], accs[1][j]], axis=0).astype(BF)
                out_ref[pl.ds(pl.multiple_of((w0 + j) * rows + t * 16, 16), 16), :] = both
            return carry

        lax.fori_loop(0, 6, block, 0)
        return carry

    lax.fori_loop(0, 3, band, 0)


def conv_forward(x, top, bot, taps, mask, place, into=None):
    width = x.shape[1] // 48
    blocks = width // LANES
    whole = lambda cb, place: (0, 0)
    half = lambda cb, place: (0, place[0] * blocks + cb)
    extra = [] if into is None else [into]
    kernel = conv_kernel if into is None else conv_kernel_into
    return pl.pallas_call(
        kernel,
        out_shape=jax.ShapeDtypeStruct((48 * 48, 2 * width), BF),
        grid_spec=pltpu.PrefetchScalarGridSpec(
            num_scalar_prefetch=1,
            grid=(blocks,),
            in_specs=[
                pl.BlockSpec(x.shape, whole),
                pl.BlockSpec(top.shape, whole),
                pl.BlockSpec(bot.shape, whole),
                pl.BlockSpec((49, LANES), lambda cb, place: (0, cb)),
                pl.BlockSpec(mask.shape, lambda cb, place: (0, 0, 0)),
            ]
            + [pl.BlockSpec(memory_space=pl.ANY)] * len(extra),
            out_specs=pl.BlockSpec((48 * 48, LANES), half),
            scratch_shapes=[
                pltpu.VMEM((54, 64, LANES), F32),
                pltpu.VMEM((2, 49, 8, LANES), F32),
            ],
        ),
        input_output_aliases={} if into is None else {6: 0},
        **conv_params(54_000_000 * width, 12_000_000),
    )(place, x, top, bot, taps, mask, *extra)


def conv_kernel_into(place_ref, x_ref, top_ref, bot_ref, taps_ref, mask_ref, into_ref, *rest):
    conv_kernel(place_ref, x_ref, top_ref, bot_ref, taps_ref, mask_ref, *rest)


def back_kernel(place_ref, g_ref, top_ref, bot_ref, x_ref, cot_ref, pool_ref, taps_ref, mask_ref,
                out_ref, tap_out_ref, gs_ref, km_ref, tacc_ref, sp_ref):
    rows, width = 48, x_ref.shape[1] // 48
    cb = pl.program_id(0)

    @pl.when(cb == 0)
    def _():
        for w in (0, 1, 2, 51, 52, 53):
            gs_ref[w] = jnp.zeros_like(gs_ref[w])

    tacc_ref[...] = jnp.zeros_like(tacc_ref)

    def fill(w, carry):
        gs_ref[w + 3, 0:RIM, :] = top_ref[w].astype(F32)
        own = pl.ds(pl.multiple_of(w * rows, rows), rows)
        gs_ref[w + 3, RIM : RIM + rows, :] = g_ref[own, :].astype(F32)
        gs_ref[w + 3, RIM + rows :, :] = bot_ref[w].astype(F32)
        return carry

    lax.fori_loop(0, 48, fill, 0)

    def spread(q, carry):
        quarter = pool_ref[q] * 0.25
        sp_ref[q, pl.ds(0, 24, stride=2), :] = quarter
        sp_ref[q, pl.ds(1, 24, stride=2), :] = quarter
        return carry

    lax.fori_loop(0, 24, spread, 0)

    def band(t, carry):
        for s in range(2):
            masked_taps(taps_ref, mask_ref, km_ref.at[s], t * 2 + s, True)

        def block(i, carry):
            w0 = i * 8
            ats = [
                pl.ds(pl.multiple_of((w0 + j) * width + cb * LANES, LANES), LANES) for j in range(8)
            ]
            band_rows = pl.ds(pl.multiple_of(t * 16, 16), 16)
            vals = [x_ref[band_rows, at].astype(F32) for at in ats]
            accs = []
            for s in range(2):
                acc = [jnp.zeros((8, LANES), F32) for _ in range(8)]
                v = [val[s * 8 : s * 8 + 8] for val in vals]
                for a in range(7):
                    start = t * 16 + (s * 8 + RIM - 3 + a)
                    g = [gs_ref[w0 + j, pl.ds(start, 8), :] for j in range(14)]
                    seen = mask_ref[a, pl.ds(t * 16 + s * 8, 8), :]
                    vm = [item * seen for item in v]
                    for b in range(7):
                        k = km_ref[s, a * 7 + b]
                        tap = None
                        for j in range(8):
                            acc[j] = acc[j] + k * g[j + b]
                            term = vm[j] * g[j + b]
                            tap = term if tap is None else tap + term
                        tacc_ref[48 - (a * 7 + b)] += tap
                accs.append(acc)
            for j in range(8):
                both = jnp.concatenate([accs[0][j], accs[1][j]], axis=0)
                total = both + cot_ref[band_rows, ats[j]].astype(F32)
                total = total + sp_ref[i * 4 + j // 2, band_rows, :]
                out_ref[0, band_rows, ats[j]] = total.astype(out_ref.dtype)
            return carry

        lax.fori_loop(0, 6, block, 0)
        return carry

    lax.fori_loop(0, 3, band, 0)
    tap_out_ref[0:49, :] = jnp.sum(tacc_ref[...], axis=1)


def conv_backward(grad, top, bot, x, cot, pool, taps, mask, place, slots, kind):
    width = x.shape[1] // 48
    blocks = width // LANES
    whole = lambda cb, place: (0, 0)
    half = lambda cb, place: (0, place[0] * blocks + cb)
    return pl.pallas_call(
        back_kernel,
        out_shape=(
            jax.ShapeDtypeStruct((slots, *x.shape), kind),
            jax.ShapeDtypeStruct((56, width), F32),
        ),
        grid_spec=pltpu.PrefetchScalarGridSpec(
            num_scalar_prefetch=1,
            grid=(blocks,),
            in_specs=[
                pl.BlockSpec((48 * 48, LANES), half),
                pl.BlockSpec((48, RIM, LANES), lambda cb, place: (0, 0, place[0] * blocks + cb)),
                pl.BlockSpec((48, RIM, LANES), lambda cb, place: (0, 0, place[0] * blocks + cb)),
                pl.BlockSpec(x.shape, whole),
                pl.BlockSpec(cot.shape, whole),
                pl.BlockSpec((24, 24, LANES), lambda cb, place: (0, 0, place[0] * blocks + cb)),
                pl.BlockSpec((49, LANES), lambda cb, place: (0, cb)),
                pl.BlockSpec(mask.shape, lambda cb, place: (0, 0, 0)),
            ],
            out_specs=(
                pl.BlockSpec((1, *x.shape), lambda cb, place: (place[0] if slots == 2 else 0, 0, 0)),
                pl.BlockSpec((56, LANES), lambda cb, place: (0, cb)),
            ),
            scratch_shapes=[
                pltpu.VMEM((54, 64, LANES), F32),
                pltpu.VMEM((2, 49, 8, LANES), F32),
                pltpu.VMEM((49, 8, LANES), F32),
                pltpu.VMEM((24, 48, LANES), F32),
            ],
        ),
        **conv_params(90_000_000 * width, 25_000_000),
    )(place, grad, top, bot, x, cot, pool, taps, mask)


def join_kernel(place_ref, branch_ref, scale_ref, own_ref, other_ref, own_out, other_out, pool_out, pair_ref):
    rows, width = 48, own_ref.shape[1] // 4
    for g, (src, dst) in enumerate(((own_ref, own_out), (other_ref, other_out))):
        side = place_ref[0] if g == 0 else 1 - place_ref[0]
        at = pl.ds(pl.multiple_of(side * width, LANES), width)
        scale = scale_ref[:, at]
        for q in range(2):
            total = None
            for w in (2 * q, 2 * q + 1):
                field = src[:, w * width : (w + 1) * width].astype(F32)
                field = field + scale * branch_ref[w * rows : (w + 1) * rows, at]
                dst[0, :, w * width : (w + 1) * width] = field.astype(BF)
                total = field if total is None else total + field
            for n in range(width // LANES):
                pair_ref[q, n] = total[:, n * LANES : (n + 1) * LANES]
                even = pair_ref[q, n, pl.ds(0, 24, stride=2), :]
                odd = pair_ref[q, n, pl.ds(1, 24, stride=2), :]
                lane = pl.ds(pl.multiple_of(side * width + n * LANES, LANES), LANES)
                pool_out[q, :, lane] = (even + odd) * 0.25


def join_branch(branch, scale, own, other, place):
    width = own.shape[1] // 48
    raw = pl.BlockSpec((48, 4 * width), lambda i, place: (0, i))
    return pl.pallas_call(
        join_kernel,
        out_shape=(
            jax.ShapeDtypeStruct((2, *own.shape), BF),
            jax.ShapeDtypeStruct((1, *own.shape), BF),
            jax.ShapeDtypeStruct((24, 24, 2 * width), F32),
        ),
        grid_spec=pltpu.PrefetchScalarGridSpec(
            num_scalar_prefetch=1,
            grid=(12,),
            in_specs=[
                pl.BlockSpec((4 * 48, 2 * width), lambda i, place: (i, 0)),
                pl.BlockSpec((1, 2 * width), lambda i, place: (0, 0)),
                raw,
                raw,
            ],
            out_specs=(
                pl.BlockSpec((1, 48, 4 * width), lambda i, place: (place[0], 0, i)),
                pl.BlockSpec((1, 48, 4 * width), lambda i, place: (0, 0, i)),
                pl.BlockSpec((2, 24, 2 * width), lambda i, place: (i, 0, 0)),
            ),
            scratch_shapes=[pltpu.VMEM((2, width // LANES, 48, LANES), F32)],
        ),
        **conv_params(10_000_000, 40_000_000),
    )(place, branch, scale, own, other)


def scaled_kernel(place_ref, pool_ref, branch_ref, scale_ref, own_ref, other_ref, out_ref, sum_ref, pair_ref):
    rows, width = 48, own_ref.shape[1] // 4

    @pl.when(pl.program_id(0) == 0)
    def _():
        sum_ref[...] = jnp.zeros_like(sum_ref)

    for g, src in enumerate((own_ref, other_ref)):
        side = place_ref[0] if g == 0 else 1 - place_ref[0]
        at = pl.ds(pl.multiple_of(side * width, LANES), width)
        scale = scale_ref[:, at]
        for q in range(2):
            quarter = pool_ref[q, :, at] * 0.25
            for n in range(width // LANES):
                part = quarter[:, n * LANES : (n + 1) * LANES]
                pair_ref[q, n, pl.ds(0, 24, stride=2), :] = part
                pair_ref[q, n, pl.ds(1, 24, stride=2), :] = part
            spread = jnp.concatenate([pair_ref[q, n] for n in range(width // LANES)], axis=1)
            for w in (2 * q, 2 * q + 1):
                here = slice(w * rows, (w + 1) * rows)
                grad = src[:, w * width : (w + 1) * width].astype(F32) + spread
                part = grad * branch_ref[here, at]
                sum_ref[:, at] += jnp.sum(part.reshape(6, 8, width), axis=0)
                out_ref[here, at] = (grad * scale).astype(BF)


def scaled_grads(pool, branch, scale, own, other, place):
    width = own.shape[1] // 48
    raw = pl.BlockSpec((48, 4 * width), lambda i, place: (0, i))
    return pl.pallas_call(
        scaled_kernel,
        out_shape=(
            jax.ShapeDtypeStruct(branch.shape, BF),
            jax.ShapeDtypeStruct((8, 2 * width), F32),
        ),
        grid_spec=pltpu.PrefetchScalarGridSpec(
            num_scalar_prefetch=1,
            grid=(12,),
            in_specs=[
                pl.BlockSpec((2, 24, 2 * width), lambda i, place: (i, 0, 0)),
                pl.BlockSpec((4 * 48, 2 * width), lambda i, place: (i, 0)),
                pl.BlockSpec((1, 2 * width), lambda i, place: (0, 0)),
                raw,
                raw,
            ],
            out_specs=(
                pl.BlockSpec((4 * 48, 2 * width), lambda i, place: (i, 0)),
                pl.BlockSpec((8, 2 * width), lambda i, place: (0, 0)),
            ),
            scratch_shapes=[pltpu.VMEM((2, width // LANES, 48, LANES), F32)],
        ),
        **conv_params(10_000_000, 40_000_000),
    )(place, pool, branch, scale, own, other)


CHUNK = 256
PAIRS = 2
WIDE = PAIRS * LANES
NT = (((1,), (1,)), ((), ()))
TN = (((0,), (0,)), ((), ()))


def dot(left, right, dims):
    return lax.dot_general(left, right, dims, preferred_element_type=F32)


NN = (((1,), (0,)), ((), ()))


def lane_half(shape, side):
    lanes = lax.broadcasted_iota(jnp.int32, shape, len(shape) - 1)
    return (lanes < 64) if side == 0 else (lanes >= 64)


def fill_window(win_ref, before, own, after):
    count = own.shape[0]
    win_ref[0:count] = before[...]
    win_ref[count : 2 * count] = own[...]
    win_ref[2 * count : 3 * count] = after[...]
    win_ref[3 * count :] = jnp.zeros_like(win_ref[3 * count :])


def attend_kernel(first_ref, last_ref, q_ref, kb_ref, k_ref, ka_ref, vb_ref, v_ref, va_ref,
                  klab_ref, qlab_ref, out_ref, total_ref, kw_ref, vw_ref):
    fill_window(kw_ref, kb_ref, k_ref, ka_ref)
    fill_window(vw_ref, vb_ref, v_ref, va_ref)
    heads = [(pair, side) for pair in range(PAIRS) for side in range(2)]
    lanes = [slice(pair * LANES, (pair + 1) * LANES) for pair in range(PAIRS)]
    for n in range(3):
        rows = slice(n * 192, (n + 1) * 192)
        q = q_ref[rows, :] * jnp.asarray(0.125, BF)
        q_half = []
        for pair, side in heads:
            own = q[:, lanes[pair]]
            q_half.append(jnp.where(lane_half(own.shape, side), own, jnp.zeros_like(own)))
        q_lab = qlab_ref[n, 0:1, :]

        def chunk(c, carry):
            at = pl.ds(pl.multiple_of(c * CHUNK, CHUNK), CHUNK)
            same = klab_ref[at, 0:1] == q_lab
            new = []
            scores = [
                jnp.where(same, dot(kw_ref[at, lanes[pair]], q_half[i], NT), NEG)
                for i, (pair, side) in enumerate(heads)
            ]
            for i, (pair, side) in enumerate(heads):
                top, total, acc = carry[i]
                best = jnp.maximum(top, jnp.max(scores[i], axis=0, keepdims=True))
                p = jnp.exp(scores[i] - best)
                shrink = jnp.exp(top - best)
                total = total * shrink + jnp.sum(p, axis=0, keepdims=True)
                acc = acc * shrink + dot(vw_ref[at, lanes[pair]], p.astype(BF), TN)
                new.append((best, total, acc))
            return tuple(new)

        start = (jnp.full((1, 192), NEG, F32), jnp.zeros((1, 192), F32), jnp.zeros((LANES, 192), F32))
        done = lax.fori_loop(first_ref[n], last_ref[n], chunk, (start,) * len(heads))
        for pair in range(PAIRS):
            outs = []
            for side in range(2):
                top, total, acc = done[2 * pair + side]
                outs.append(acc * (1.0 / total))
                total_ref[pair, n, side : side + 1, :] = top + jnp.log(total)
            both = jnp.concatenate([outs[0][:64], outs[1][64:]], axis=0)
            out_ref[rows, lanes[pair]] = both.T.astype(BF)


def attend(q, k, v, around, qlab, klab, first, last):
    count, width = q.shape
    window = -(-3 * count // CHUNK) * CHUNK
    block = pl.BlockSpec((count, WIDE), lambda p, *_: (0, p))
    stats = pl.BlockSpec((PAIRS, 3, 2, 192), lambda p, *_: (p, 0, 0, 0))
    return pl.pallas_call(
        attend_kernel,
        out_shape=(
            jax.ShapeDtypeStruct(q.shape, BF),
            jax.ShapeDtypeStruct((width // LANES, 3, 2, 192), F32),
        ),
        grid_spec=pltpu.PrefetchScalarGridSpec(
            num_scalar_prefetch=2,
            grid=(width // WIDE,),
            in_specs=[block] * 7
            + [
                pl.BlockSpec(klab.shape, lambda p, *_: (0, 0)),
                pl.BlockSpec(qlab.shape, lambda p, *_: (0, 0, 0)),
            ],
            out_specs=(block, stats),
            scratch_shapes=[pltpu.VMEM((window, WIDE), BF), pltpu.VMEM((window, WIDE), BF)],
        ),
        **conv_params(40_000_000 * width, 20_000_000),
    )(first, last, q, around[0], k, around[1], around[2], v, around[3], klab, qlab)


def attend_back_kernel(first_ref, last_ref, q_ref, kb_ref, k_ref, ka_ref, vb_ref, v_ref, va_ref,
                       do_ref, o_ref, total_ref, klab_ref, qlab_ref,
                       dq_ref, dk_ref, dv_ref, before_ref, after_ref,
                       kw_ref, vw_ref, dkw_ref, dvw_ref):
    count = q_ref.shape[0]
    fill_window(kw_ref, kb_ref, k_ref, ka_ref)
    fill_window(vw_ref, vb_ref, v_ref, va_ref)
    dkw_ref[...] = jnp.zeros_like(dkw_ref)
    dvw_ref[...] = jnp.zeros_like(dvw_ref)
    heads = [(pair, side) for pair in range(PAIRS) for side in range(2)]
    lanes = [slice(pair * LANES, (pair + 1) * LANES) for pair in range(PAIRS)]
    for n in range(3):
        rows = slice(n * 192, (n + 1) * 192)
        q = q_ref[rows, :] * jnp.asarray(0.125, BF)
        do = do_ref[rows, :]
        halves = [lane_half((192, LANES), side) for side in range(2)]
        q_half = [jnp.where(halves[s], q[:, lanes[p]], jnp.zeros((), BF)) for p, s in heads]
        do_half = [jnp.where(halves[s], do[:, lanes[p]], jnp.zeros((), BF)) for p, s in heads]
        q_lab = qlab_ref[n, 0:1, :]
        flow = do.astype(F32) * o_ref[rows, :].astype(F32)
        delta = []
        for p in range(PAIRS):
            turned = flow[:, lanes[p]].T
            delta += [jnp.sum(turned[s * 64 : s * 64 + 64], axis=0, keepdims=True) for s in range(2)]

        def chunk(c, carry):
            at = pl.ds(pl.multiple_of(c * CHUNK, CHUNK), CHUNK)
            same = klab_ref[at, 0:1] == q_lab
            kcs = [kw_ref[at, lanes[pair]] for pair in range(PAIRS)]
            vcs = [vw_ref[at, lanes[pair]] for pair in range(PAIRS)]
            scores = [dot(kcs[p], q_half[i], NT) for i, (p, s) in enumerate(heads)]
            dps = [dot(vcs[p], do_half[i], NT) for i, (p, s) in enumerate(heads)]
            ps, dss = [], []
            for i, (p, s) in enumerate(heads):
                raised = jnp.where(same, scores[i] - total_ref[p, n, s : s + 1, :], NEG)
                ps.append(jnp.exp(raised))
            for i, (p, s) in enumerate(heads):
                dss.append((ps[i] * (dps[i] - delta[i])).astype(BF))
            low = [item.astype(BF) for item in ps]
            dqs = []
            for p in range(PAIRS):
                e, o = 2 * p, 2 * p + 1
                dvw_ref[at, lanes[p]] += dot(low[e], do_half[e], NN) + dot(low[o], do_half[o], NN)
                dkw_ref[at, lanes[p]] += dot(dss[e], q_half[e], NN) + dot(dss[o], q_half[o], NN)
                two = [dot(dss[e], kcs[p], TN), dot(dss[o], kcs[p], TN)]
                dqs.append(carry[p] + jnp.where(lane_half((192, LANES), 0), two[0], two[1]))
            return tuple(dqs)

        dqs = lax.fori_loop(
            first_ref[n], last_ref[n], chunk, tuple(jnp.zeros((192, LANES), F32) for _ in range(PAIRS))
        )
        for pair in range(PAIRS):
            dq_ref[rows, lanes[pair]] = (dqs[pair] * 0.125).astype(BF)
    dk_ref[...] = dkw_ref[count : 2 * count, :]
    dv_ref[...] = dvw_ref[count : 2 * count, :]
    before_ref[0] = dkw_ref[0:count, :].astype(BF)
    before_ref[1] = dvw_ref[0:count, :].astype(BF)
    after_ref[0] = dkw_ref[2 * count : 3 * count, :].astype(BF)
    after_ref[1] = dvw_ref[2 * count : 3 * count, :].astype(BF)


def attend_back(q, k, v, around, grad, out, total, qlab, klab, first, last):
    count, width = q.shape
    window = -(-3 * count // CHUNK) * CHUNK
    block = pl.BlockSpec((count, WIDE), lambda p, *_: (0, p))
    stats = pl.BlockSpec((PAIRS, 3, 2, 192), lambda p, *_: (p, 0, 0, 0))
    pair = pl.BlockSpec((2, count, WIDE), lambda p, *_: (0, 0, p))
    return pl.pallas_call(
        attend_back_kernel,
        out_shape=(
            jax.ShapeDtypeStruct(q.shape, BF),
            jax.ShapeDtypeStruct(q.shape, F32),
            jax.ShapeDtypeStruct(q.shape, F32),
            jax.ShapeDtypeStruct((2, count, width), BF),
            jax.ShapeDtypeStruct((2, count, width), BF),
        ),
        grid_spec=pltpu.PrefetchScalarGridSpec(
            num_scalar_prefetch=2,
            grid=(width // WIDE,),
            in_specs=[block] * 9
            + [
                stats,
                pl.BlockSpec(klab.shape, lambda p, *_: (0, 0)),
                pl.BlockSpec(qlab.shape, lambda p, *_: (0, 0, 0)),
            ],
            out_specs=(block, block, block, pair, pair),
            scratch_shapes=[
                pltpu.VMEM((window, WIDE), BF),
                pltpu.VMEM((window, WIDE), BF),
                pltpu.VMEM((window, WIDE), F32),
                pltpu.VMEM((window, WIDE), F32),
            ],
        ),
        **conv_params(55_000_000 * width, 20_000_000),
    )(first, last, q, around[0], k, around[1], around[2], v, around[3], grad, out, total, klab, qlab)


def on_device(
    lo_in,
    hi_in,
    image_ids,
    cn_kernel,
    cn_gain,
    cn_w1,
    cn_w2,
    cn_scale,
    ad_proj,
    ad_kernel,
    gate_w1,
    gate_w2,
    ln1_gain,
    qkv,
    out_proj,
    ln2_gain,
    fc1,
    fc2,
    d_lo_out,
    d_hi_out,
):
    micro_count, row_count, col_count, d_shard = lo_in.shape
    hi_rows = hi_in.shape[1]
    hi_cols = HCOLS
    c_shard = hi_in.shape[3] // hi_cols
    d_own, c_own = 2 * d_shard, 2 * c_shard
    tok_count = row_count * col_count
    pix_count = hi_rows * hi_cols
    mine = lax.axis_index("mb")
    row_start = lax.axis_index(TILE) * row_count
    head_count = d_own // HDIM

    fast = c_shard % LANES == 0 and lax.axis_size("tp") == 1
    hi_raw = hi_in.reshape(2, hi_rows, hi_cols * c_shard)
    hi_own, hi_other = swap_micro(hi_raw)
    up, down = rim_pair(hi_raw, RIM, 1)
    own_rims, other_rims = swap_micro(jnp.stack([up, down], axis=1))
    hid_shard, gh_shard, ff_shard = cn_w1.shape[1], gate_w1.shape[1], fc1.shape[1]
    mlp = gather_all(jnp.concatenate([cn_w1, cn_w2.T, ad_proj, gate_w1], axis=1))
    def apply(left, pair):
        return jnp.concatenate([matmul(left, pair[0]), matmul(left, pair[1])], axis=1)

    def apply_t(left, pair):
        width = pair[0].shape[1]
        return matmul_nt(left[:, :width], pair[0]) + matmul_nt(left[:, width:], pair[1])

    def cols(values):
        width = values.shape[1] // 2
        return [values[:, :width], values[:, width:]]

    canvas_ids = lax.dynamic_index_in_dim(image_ids, mine, 0, keepdims=False)
    small_ids = row_labels(canvas_ids, row_start, row_count, 1)
    lo_mid = small_ids[1 : 1 + row_count]
    hi_ids = row_labels(jnp.repeat(canvas_ids, 2), 2 * row_start, hi_rows, 3)
    hi_mid = hi_ids[3 : 3 + hi_rows]

    def both_shards(shard, axis):
        return in_order(shard, lax.ppermute(shard, "mb", SWAP), axis)

    other_kernel = lax.ppermute(cn_kernel, "mb", SWAP)
    conv_taps = in_order(cn_kernel, other_kernel, 1)

    own_place = mine.reshape(1).astype(jnp.int32)
    other_place = 1 - own_place
    seen = jnp.stack([(hi_ids[a : a + hi_rows] == hi_mid).astype(F32) for a in range(7)])
    mask = jnp.broadcast_to(seen[:, :, None], (7, hi_rows, LANES))
    own_taps, other_taps = cn_kernel.astype(F32), other_kernel.astype(F32)

    def natural(own, other):
        shape = (-1, hi_cols, c_shard)
        return in_order(own.reshape(shape), other.reshape(shape), 2)

    if fast:
        conv_flat = conv_forward(hi_own, *own_rims, own_taps, mask, own_place)
        conv_flat = conv_forward(hi_other, *other_rims, other_taps, mask, other_place, conv_flat)
    else:
        hi_field = natural(hi_own, hi_other)
        hi_pad = jnp.concatenate(
            [
                natural(own_rims[0], other_rims[0])[-3:],
                hi_field,
                natural(own_rims[1], other_rims[1])[:3],
            ]
        )
        conv_low = depthwise(hi_pad, conv_taps, hi_ids, hi_mid, 7, False).astype(BF)
        conv_flat = conv_low.transpose(1, 0, 2).reshape(pix_count, c_own)
    conv_full = features(conv_flat)
    normed, norm_pull = jax.vjp(layer_norm, conv_full.astype(F32), cn_gain.astype(F32))
    normed_low, mlp, gate_w2 = together(normed.astype(BF), mlp, gate_w2)
    mlp_in = [mlp[g, :, :hid_shard] for g in range(2)]
    mlp_out = [mlp[g, :, hid_shard : 2 * hid_shard] for g in range(2)]
    ad_matrix = [mlp[g, :, 2 * hid_shard : 2 * hid_shard + d_shard] for g in range(2)]
    gate_in = [mlp[g, :, 2 * hid_shard + d_shard :] for g in range(2)]
    vit = gather_all(
        jnp.concatenate(
            [
                gate_w2.T,
                qkv[0],
                qkv[1],
                qkv[2],
                out_proj.T,
                fc1,
                fc2.T,
            ],
            axis=1,
        )
    )
    cuts = np.cumsum([0, gh_shard, d_shard, d_shard, d_shard, d_shard, ff_shard, ff_shard])
    gate_out, q_w, k_w, v_w, out_w, ff_in, ff_out = [
        [vit[g, :, int(cuts[i]) : int(cuts[i + 1])] for g in range(2)] for i in range(7)
    ]

    inner_act, inner_slope = zip(*[gelu_pair(matmul(normed_low, mlp_in[g])) for g in range(2)])
    lo_in, d_lo_out, cn_scale, ad_kernel, first_act = together(
        lo_in, d_lo_out, cn_scale, ad_kernel, inner_act[0]
    )
    inner_act = (first_act, inner_act[1])
    lo_low = in_order(*swap_micro(lo_in.reshape(2, tok_count, d_shard)), 1)
    lo_field = lo_low.astype(F32)
    ad_taps = both_shards(ad_kernel, 1)
    hi_scale = both_shards(cn_scale, 0).astype(F32)
    branch = partial_sums(
        matmul_nt(inner_act[0], mlp_out[0]) + matmul_nt(inner_act[1], mlp_out[1])
    )
    if fast:
        hi_mine, hi_sent, pooled = join_branch(branch, hi_scale[None], hi_own, hi_other, own_place)
        pooled = pooled.transpose(1, 0, 2)
    else:
        branch_rows = branch.reshape(hi_cols, hi_rows, c_own).transpose(1, 0, 2)
        hi_sum = hi_field.astype(F32) + hi_scale * branch_rows
        pooled = jnp.mean(hi_sum.reshape(row_count, 2, col_count, 2, c_own), axis=(1, 3))
    pooled_full = features(pooled.reshape(tok_count, c_own).astype(BF))
    pooled_full, d_hi_out = together(pooled_full, d_hi_out)
    cot_own, cot_other = swap_micro(d_hi_out.reshape(2, hi_rows, hi_cols * c_shard))
    proj_low = apply(pooled_full, ad_matrix).astype(BF)
    proj_pad = rim_rows(proj_low.reshape(row_count, col_count, d_own), 1)
    local_conv = depthwise(proj_pad, ad_taps, small_ids, lo_mid, 3, False).reshape(
        tok_count, d_own
    )
    gate_hidden, gate_slope = gelu_pair(apply(pooled_full, gate_in))
    gate_val = jnp.tanh(partial_sums(apply_t(gate_hidden, gate_out)))
    mixed_one = lo_field + gate_val * local_conv
    mixed_full = features(mixed_one.astype(BF))
    norm_one, first_pull = jax.vjp(layer_norm, mixed_full.astype(F32), ln1_gain.astype(F32))
    norm_low = norm_one.astype(BF)
    queries = apply(norm_low, q_w).astype(BF)
    key_rows = apply(norm_low, k_w).astype(BF)
    value_rows = apply(norm_low, v_w).astype(BF)
    around = rim_pair(key_rows, tok_count, 0) + rim_pair(value_rows, tok_count, 0)
    near = row_labels(canvas_ids, row_start, row_count, row_count)
    key_tok = jnp.repeat(near, col_count)
    window = -(-3 * tok_count // CHUNK) * CHUNK
    key_tok = jnp.pad(key_tok, (0, window - 3 * tok_count), constant_values=-2)
    key_lab = jnp.broadcast_to(key_tok[:, None], (window, LANES))
    query_lab = jnp.broadcast_to(jnp.repeat(lo_mid, col_count).reshape(3, 1, 192), (3, 8, 192))
    edge = jnp.arange(3 * row_count)
    first_row = jnp.min(jnp.where(near[None] == lo_mid[::8][:, None], edge, 3 * row_count), axis=1)
    last_row = jnp.max(jnp.where(near[None] == lo_mid[7::8][:, None], edge, -1), axis=1) + 1
    first = (first_row * col_count // CHUNK).astype(jnp.int32)
    last = ((last_row * col_count + CHUNK - 1) // CHUNK).astype(jnp.int32)
    attended, log_total = attend(
        queries, key_rows, value_rows, around, query_lab, key_lab, first, last
    )
    mixed_two = mixed_one + partial_sums(apply_t(attended, out_w))
    if fast:
        hi_got = lax.ppermute(hi_sent, "mb", SWAP)
        mixed_two, hi_got = together(mixed_two, hi_got)
    mixed2_full = features(mixed_two.astype(BF))
    norm_two, second_pull = jax.vjp(layer_norm, mixed2_full.astype(F32), ln2_gain.astype(F32))
    norm2_low = norm_two.astype(BF)
    ff_hidden, ff_slope = gelu_pair(apply(norm2_low, ff_in))
    lo_result = (mixed_two + partial_sums(apply_t(ff_hidden, ff_out))).astype(BF)

    grad_low = in_order(*swap_micro(d_lo_out.reshape(2, tok_count, d_shard)), 1)
    grad_out = grad_low.astype(F32)
    ff_grad_full = features(grad_low)
    ff_pre_grad = (apply(ff_grad_full, ff_out) * ff_slope.astype(F32)).astype(BF)
    second_grad = partial_sums(apply_t(ff_pre_grad, ff_in)).astype(BF)
    back_two, grad_ln2 = second_pull(features(second_grad).astype(F32))
    p_ff = stacked_grads([norm2_low, ff_grad_full], [ff_pre_grad, ff_hidden])
    grad_two, p_ff, cot_other = together(grad_out + own_slice(back_two), p_ff, cot_other)
    s_ff = reduce_tiles(p_ff)
    att_grad_full = features(grad_two.astype(BF))
    att_grad = apply(att_grad_full, out_w).astype(BF)
    query_grad, key_own, value_own, to_before, to_after = attend_back(
        queries, key_rows, value_rows, around, att_grad, attended, log_total, query_lab, key_lab, first, last
    )
    devices = tile_count()
    steps = [(i, i + 1) for i in range(devices - 1)]
    from_before = lax.ppermute(to_after, TILE, steps)
    from_after = lax.ppermute(to_before, TILE, [(j, i) for i, j in steps])
    key_grad, value_grad = [
        (own + from_before[i].astype(F32) + from_after[i].astype(F32)).astype(BF)
        for i, own in enumerate((key_own, value_own))
    ]
    first_grad = partial_sums(
        apply_t(query_grad, q_w) + apply_t(key_grad, k_w) + apply_t(value_grad, v_w)
    ).astype(BF)
    back_one, grad_ln1 = first_pull(features(first_grad).astype(F32))
    grad_one = grad_two + own_slice(back_one)
    gate_pre_grad = (grad_one * local_conv * (1.0 - gate_val * gate_val)).astype(BF)
    gate_grad_full = features(gate_pre_grad)
    p_att = stacked_grads(
        [gate_grad_full, norm_low, att_grad_full],
        [gate_hidden, jnp.concatenate([query_grad, key_grad, value_grad], axis=1), attended],
    )
    hidden_grad = (apply(gate_grad_full, gate_out) * gate_slope.astype(F32)).astype(BF)
    local_grad = (grad_one * gate_val).astype(BF).reshape(row_count, col_count, d_own)
    local_pad = rim_rows(local_grad, 1)
    proj_grad = (
        depthwise(local_pad, ad_taps, small_ids, lo_mid, 3, True)
        .reshape(tok_count, d_own)
        .astype(BF)
    )
    grad_ad_kernel = tap_grads(proj_pad, local_grad, small_ids, lo_mid, 3)
    p_ad = matmul_tn(pooled_full, jnp.concatenate([proj_grad, hidden_grad], axis=1)).astype(BF)
    pooled_grad = partial_sums(apply_t(hidden_grad, gate_in) + apply_t(proj_grad, ad_matrix))
    pooled_grad, p_att, p_ad = together(pooled_grad, p_att, p_ad)
    s_att, s_ad = reduce_tiles(p_att), reduce_tiles(p_ad)
    pool_cols = pooled_grad.reshape(row_count, col_count, c_own).transpose(1, 0, 2)
    if fast:
        scaled_grad, scale_parts = scaled_grads(
            pool_cols, branch, hi_scale[None], cot_own, cot_other, own_place
        )
        grad_scale = jnp.sum(scale_parts, axis=0)
    else:
        spread_grad = jnp.repeat(jnp.repeat(pool_cols.transpose(1, 0, 2) * 0.25, 2, 0), 2, 1)
        hi_grad = natural(cot_own, cot_other).astype(F32) + spread_grad
        grad_cols = hi_grad.transpose(1, 0, 2).reshape(pix_count, c_own)
        grad_scale = jnp.sum(grad_cols * branch, axis=0)
        scaled_grad = (grad_cols * hi_scale).astype(BF)
    branch_full = lax.optimization_barrier(features(scaled_grad))
    p_w2 = [matmul_tn(branch_full, act).astype(BF) for act in inner_act]
    branch_full, *p_w2, s_ff = together(branch_full, *p_w2, s_ff)
    core_w2 = [core_sum(item) for item in p_w2]
    grad_first = (matmul(branch_full, mlp_out[0]) * inner_slope[0].astype(F32)).astype(BF)
    w1_first = matmul_tn(normed_low, grad_first).astype(BF)
    branch_full, w1_first, *core_w2 = together(branch_full, w1_first, *core_w2)
    w2_own, w2_got = pass_half(*core_w2)
    core_first = core_sum(w1_first)
    grad_second = (matmul(branch_full, mlp_out[1]) * inner_slope[1].astype(F32)).astype(BF)
    w1_second = matmul_tn(normed_low, grad_second).astype(BF)
    grad_second, w1_second, w2_got = together(grad_second, w1_second, w2_got)
    s_w2 = reduce_chips(add_low(w2_own, w2_got))
    core_second = core_sum(w1_second)
    normed_grad = partial_sums(
        matmul_nt(grad_first, mlp_in[0]) + matmul_nt(grad_second, mlp_in[1])
    ).astype(BF)
    back_conv, grad_cn_gain = norm_pull(features(normed_grad).astype(F32))
    conv_grad, core_first, core_second = together(
        own_slice(back_conv).astype(BF), core_first, core_second
    )
    w1_own, w1_got = pass_half(core_first, core_second)
    conv_cols = conv_grad.reshape(hi_cols, hi_rows, c_own)
    grad_up, grad_down = rim_pair(conv_cols, RIM, 1)
    if fast:
        ghi_sent, taps_other = conv_backward(
            conv_grad, grad_up, grad_down, hi_other, cot_other, pool_cols, other_taps, mask, other_place, 1, BF
        )
        w1_got, s_att, s_ad, s_w2 = together(w1_got, s_att, s_ad, s_w2)
        w1_sum = add_low(w1_own, w1_got)
        conv_grad, ghi_sent, w1_sum = together(conv_grad, ghi_sent, w1_sum)
        ghi_mine, taps_own = conv_backward(
            conv_grad, grad_up, grad_down, hi_own, cot_own, pool_cols, own_taps, mask, own_place, 2, F32
        )
        tap_sums = jnp.concatenate([taps_own, taps_other])
    else:
        conv_grad = conv_cols.transpose(1, 0, 2)
        conv_pad = jnp.concatenate(
            [grad_up.transpose(1, 0, 2)[-3:], conv_grad, grad_down.transpose(1, 0, 2)[:3]]
        )
        hi_back = hi_grad + depthwise(conv_pad, conv_taps, hi_ids, hi_mid, 7, True)
        grad_cn_kernel = tap_grads(hi_pad, conv_grad, hi_ids, hi_mid, 7)
        tap_sums = jnp.concatenate(halves(grad_cn_kernel))
        w1_sum = add_low(w1_own, w1_got)

    g_w1 = reduce_chips(w1_sum)
    own_terms, sent_terms = zip(*[halves(item) for item in (grad_scale, grad_ad_kernel)])
    gains = [grad_cn_gain, grad_ln1, grad_ln2]
    flat, sent = [
        jnp.concatenate([item.reshape(-1) for item in (*terms, *gains)])
        for terms in (own_terms, sent_terms)
    ]
    flat = sum_everywhere(flat + lax.ppermute(sent, "mb", SWAP))
    sizes = np.cumsum([0] + [item.size for item in (*own_terms, *gains)])
    g_scale, g_taps, *gain_sums = [
        flat[int(sizes[i]) : int(sizes[i + 1])].reshape(item.shape)
        for i, item in enumerate((*own_terms, *gains))
    ]
    if fast:
        ghi_got = lax.ppermute(ghi_sent, "mb", SWAP)
        tap_sums, ghi_got = together(tap_sums, ghi_got)
    tap_sums = sum_everywhere(tap_sums)
    tap_rows = tap_sums.shape[0] // 2
    g_kernel = (tap_sums[:tap_rows] + lax.ppermute(tap_sums[tap_rows:], "mb", SWAP))[: cn_kernel.shape[0]]

    def leave(values, kind):
        own, sent = halves(values)
        other = lax.ppermute(sent.astype(BF), "mb", SWAP)
        return both_micro(own.astype(kind), other.astype(kind))

    lo_stack = leave(lo_result.reshape(row_count, col_count, d_own), BF)
    if fast:
        hi_stack, ghi_stack = [
            lax.dynamic_update_slice_in_dim(stack, got.astype(stack.dtype), 1 - mine, 0)
            for stack, got in ((hi_mine, hi_got), (ghi_mine, ghi_got))
        ]
    else:
        hi_stack = leave(hi_sum, BF)
        ghi_stack = leave(hi_back, F32)
    glo_stack = leave(grad_one.reshape(row_count, col_count, d_own), F32)

    hi_stack = hi_stack.reshape(2, hi_rows, 1, hi_cols * c_shard)
    ghi_stack, g_w1 = together(ghi_stack.reshape(2, hi_rows, -1, 128), g_w1)
    ghi_stack = ghi_stack.reshape(2, hi_rows, 1, hi_cols * c_shard)
    g_w1, g_w2 = all_columns(g_w1).astype(F32), all_columns(s_w2).astype(F32)
    g_fc1, g_fc2 = settle(s_ff, (ff_shard, ff_shard))
    g_gate_w2, g_q, g_k, g_v, g_out = settle(s_att, (gh_shard, d_shard, d_shard, d_shard, d_shard))
    g_ad, g_gate_w1 = settle(s_ad, (d_shard, gh_shard))

    return (
        lo_stack,
        hi_stack,
        glo_stack,
        ghi_stack,
        g_kernel,
        gain_sums[0],
        g_w1,
        g_w2.T,
        g_scale,
        g_ad,
        g_taps,
        g_gate_w1,
        g_gate_w2.T,
        gain_sums[1],
        jnp.stack([g_q, g_k, g_v]),
        g_out.T,
        gain_sums[2],
        g_fc1,
        g_fc2.T,
    )


def solution(mesh):
    tiles, mps = mesh.shape["tile"], mesh.shape["mp"]
    fine = Mesh(mesh.devices.reshape(tiles // 2, 2, 2, mps // 2), (*TILE, "mb", "tp"))
    mp = ("mb", "tp")
    in_specs = (
        P(None, TILE, None, mp),
        P(None, TILE, mp, None),
        P(),
        P(None, mp),
        P(),
        P(TILE, mp),
        P(mp, TILE),
        P(mp),
        P(TILE, mp),
        P(None, mp),
        P(TILE, mp),
        P(mp, TILE),
        P(),
        P(None, TILE, mp),
        P(mp, TILE),
        P(),
        P(TILE, mp),
        P(mp, TILE),
        P(None, TILE, None, mp),
        P(None, TILE, mp, None),
    )
    out_specs = (
        P(None, TILE, None, mp),
        P(None, TILE, mp, None),
        P(None, TILE, None, mp),
        P(None, TILE, mp, None),
        P(None, mp),
        P(),
        P(TILE, mp),
        P(mp, TILE),
        P(mp),
        P(TILE, mp),
        P(None, mp),
        P(TILE, mp),
        P(mp, TILE),
        P(),
        P(None, TILE, mp),
        P(mp, TILE),
        P(),
        P(TILE, mp),
        P(mp, TILE),
    )
    return jax.shard_map(
        on_device, mesh=fine, in_specs=in_specs, out_specs=out_specs, check_vma=False
    )
```

```python
import functools

import jax
import jax.numpy as jnp
import numpy as np
from jax import lax
from jax.experimental import pallas as pl
from jax.experimental.pallas import tpu as pltpu
from jax.sharding import Mesh
from jax.sharding import PartitionSpec as P

HDIM = 64
IMG_ROWS = 24
HCOLS = 48

EPS = 1e-06
NEG = -1e30
BF = jnp.bfloat16
F32 = jnp.float32
TILE = ("chip", "core")
ALL = ("mb", *TILE)


def tile_count():
    return lax.axis_size("chip") * lax.axis_size("core")


def rim_pair(value, width, axis):
    devices, length = tile_count(), value.shape[axis]
    up = [(i, (i + 1) % devices) for i in range(devices - 1)]
    down = [(j, i) for i, j in up]
    before = lax.ppermute(lax.slice_in_dim(value, length - width, length, axis=axis), TILE, up)
    after = lax.ppermute(lax.slice_in_dim(value, 0, width, axis=axis), TILE, down)
    return before, after


def rim_rows(value, width):
    devices, length = tile_count(), value.shape[0]
    up = [(i, (i + 1) % devices) for i in range(devices - 1)]
    down = [(j, i) for i, j in up]
    before = lax.ppermute(value[length - width :], TILE, up)
    after = lax.ppermute(value[:width], TILE, down)
    return jnp.concatenate([before, value, after], axis=0)


def matmul(left, right):
    return jnp.dot(left, right, preferred_element_type=F32)


def matmul_tn(left, right):
    return lax.dot_general(left, right, (((0,), (0,)), ((), ())), preferred_element_type=F32)


def matmul_nt(left, right):
    return lax.dot_general(left, right, (((1,), (1,)), ((), ())), preferred_element_type=F32)


def layer_norm(values, gain_vec):
    average = jnp.mean(values, axis=-1, keepdims=True)
    centered = values - average
    variance = jnp.mean(centered * centered, axis=-1, keepdims=True)
    return centered * lax.rsqrt(variance + EPS) * gain_vec


def gelu_pair(values):
    cdf = 0.5 + 0.5 * lax.erf(values * 0.7071067811865476)
    slope = cdf + values * (0.3989422804014327 * jnp.exp(-0.5 * values * values))
    return (values * cdf).astype(BF), slope.astype(BF)


def features(values):
    parts = lax.axis_size("tp")
    if parts == 1:
        return values
    rows, width = values.shape
    full = lax.all_gather(values.reshape(rows, 2, width // 2), "tp", axis=2)
    return full.reshape(rows, parts * width)


def partial_sums(values):
    parts = lax.axis_size("tp")
    if parts == 1:
        return values
    rows, width = values.shape
    split = values.reshape(rows, 2, parts, width // (2 * parts))
    return lax.psum_scatter(split, "tp", scatter_dimension=2).reshape(rows, width // parts)


def own_slice(values):
    parts = lax.axis_size("tp")
    if parts == 1:
        return values
    rows, width = values.shape
    split = values.reshape(rows, 2, parts, width // (2 * parts))
    own = lax.dynamic_index_in_dim(split, lax.axis_index("tp"), 2, keepdims=False)
    return own.reshape(rows, width // parts)


SWAP = [(0, 1), (1, 0)]


def swap_micro(values):
    mine = lax.axis_index("mb")
    own = lax.dynamic_index_in_dim(values, mine, 0, keepdims=False)
    sent = lax.dynamic_index_in_dim(values, 1 - mine, 0, keepdims=False)
    return own, lax.ppermute(sent, "mb", SWAP)


def in_order(own, other, axis):
    first = lax.axis_index("mb") == 0
    return jnp.concatenate(
        [jnp.where(first, own, other), jnp.where(first, other, own)], axis=axis
    )


def both_micro(own, other):
    first = lax.axis_index("mb") == 0
    return jnp.stack([jnp.where(first, own, other), jnp.where(first, other, own)])


def halves(values):
    width = values.shape[-1] // 2
    mine = lax.axis_index("mb")
    own = lax.dynamic_slice_in_dim(values, mine * width, width, values.ndim - 1)
    sent = lax.dynamic_slice_in_dim(values, (1 - mine) * width, width, values.ndim - 1)
    return own, sent


def row_labels(labels, first_row, count_rows, margin):
    padded = jnp.pad(labels, (margin, margin), constant_values=-1)
    return lax.dynamic_slice_in_dim(padded, first_row, count_rows + 2 * margin, 0)


def depthwise(padded, kernel, ids_pad, ids_mid, tap_size, flipped):
    margin = tap_size // 2
    row_count = ids_mid.shape[0]
    col_count = padded.shape[1]
    widened = jnp.pad(padded, ((0, 0), (margin, margin), (0, 0)))
    summed = jnp.zeros((row_count, col_count, padded.shape[2]), F32)
    for a in range(tap_size):
        same_img = (ids_pad[a : a + row_count] == ids_mid)[:, None, None]
        shifted = jnp.where(same_img, widened[a : a + row_count].astype(F32), 0.0)
        for b in range(tap_size):
            tap_index = (
                (tap_size - 1 - a) * tap_size + (tap_size - 1 - b) if flipped else a * tap_size + b
            )
            summed = summed + kernel[tap_index].astype(F32) * shifted[:, b : b + col_count]
    return summed


def tap_grads(padded, grad_low, ids_pad, ids_mid, tap_size):
    margin = tap_size // 2
    row_count = ids_mid.shape[0]
    col_count = padded.shape[1]
    widened = jnp.pad(padded, ((0, 0), (margin, margin), (0, 0)))
    grad_vals = grad_low.astype(F32)
    results = []
    for a in range(tap_size):
        same_img = (ids_pad[a : a + row_count] == ids_mid)[:, None, None]
        shifted = jnp.where(same_img, widened[a : a + row_count].astype(F32), 0.0)
        for b in range(tap_size):
            results.append(jnp.sum(shifted[:, b : b + col_count] * grad_vals, axis=(0, 1)))
    return jnp.stack(results)


def stacked_kernel(cuts, *refs):
    count = len(cuts) - 1
    step = pl.program_id(0)
    for i in range(count):

        @pl.when((step >= cuts[i]) & (step < cuts[i + 1]))
        def _(i=i):
            refs[-1][...] = dot(refs[i][...], refs[count + i][...], NN).astype(BF)


def stacked_grads(lefts, rights):
    widths = [item.shape[1] for item in rights]
    step_width = next((size for size in (512, 256) if not any(width % size for width in widths)), 0)
    if not step_width:
        return jnp.concatenate(
            [matmul_tn(left, right).astype(BF) for left, right in zip(lefts, rights)], axis=1
        )
    tokens, rows = lefts[0].shape
    cuts = [int(item) for item in np.cumsum([0] + [width // step_width for width in widths])]

    def column(i):
        return lambda step: (0, jnp.clip(step - cuts[i], 0, cuts[i + 1] - cuts[i] - 1))

    return pl.pallas_call(
        functools.partial(stacked_kernel, cuts),
        out_shape=jax.ShapeDtypeStruct((rows, sum(widths)), BF),
        grid=(cuts[-1],),
        in_specs=[pl.BlockSpec((rows, tokens), lambda step: (0, 0)) for _ in lefts]
        + [pl.BlockSpec((tokens, step_width), column(i)) for i in range(len(rights))],
        out_specs=pl.BlockSpec((rows, step_width), lambda step: (0, step)),
        **conv_params(5 * tokens * rows * sum(widths), 2 * rows * sum(widths)),
    )(*[left.T for left in lefts], *rights)


def gather_all(shard):
    full = lax.all_gather(shard, ALL, axis=0)
    return full.reshape(2, -1, shard.shape[1])


def reduce_tiles(terms):
    return lax.psum_scatter(terms, TILE, scatter_dimension=0, tiled=True)


def core_sum(terms):
    width = terms.shape[1] // 2
    core = lax.axis_index("core")
    own = lax.dynamic_slice_in_dim(terms, core * width, width, 1)
    sent = lax.dynamic_slice_in_dim(terms, (1 - core) * width, width, 1)
    got = lax.ppermute(sent, "core", SWAP)
    return (own.astype(F32) + got.astype(F32)).astype(BF)


def add_low(own, got):
    return (own.astype(F32) + got.astype(F32)).astype(BF)


def chip_step(terms, bit):
    pairs = terms.reshape(terms.shape[0] // 2, 2, *terms.shape[1:])
    side = (lax.axis_index("chip") // bit) % 2
    own = lax.dynamic_index_in_dim(pairs, side, 1, keepdims=False)
    sent = lax.dynamic_index_in_dim(pairs, 1 - side, 1, keepdims=False)
    got = lax.ppermute(sent, "chip", [(i, i ^ bit) for i in range(lax.axis_size("chip"))])
    return own, got


def all_columns(both):
    rows = both.shape[0] // 2
    core = lax.axis_index("core")
    own = lax.dynamic_slice_in_dim(both, core * rows, rows, 0)
    sent = lax.dynamic_slice_in_dim(both, (1 - core) * rows, rows, 0)
    got = lax.ppermute(sent, "core", SWAP)
    first = core == 0
    return jnp.concatenate([jnp.where(first, own, got), jnp.where(first, got, own)], axis=1)


def settle(summed, widths):
    own, sent, start = [], [], 0
    for width in widths:
        mine, other = halves(summed[:, start : start + 2 * width])
        own.append(mine)
        sent.append(other)
        start += 2 * width
    got = lax.ppermute(jnp.concatenate(sent, axis=1), "mb", SWAP)
    cuts = [int(item) for item in np.cumsum([0] + list(widths))]
    return [
        item.astype(F32) + got[:, cuts[i] : cuts[i + 1]].astype(F32) for i, item in enumerate(own)
    ]


def sum_everywhere(flat):
    devices = tile_count()
    if devices & (devices - 1):
        return lax.psum(flat, TILE)
    bit = 1
    while bit < devices:
        flat = flat + lax.ppermute(flat, TILE, [(i, i ^ bit) for i in range(devices)])
        bit *= 2
    return flat


def together(*values):
    return lax.optimization_barrier(values)


LANES = 128
RIM = 8
VMEM_LIMIT = 60 * 1024 * 1024


def conv_params(flops=0, moved=0):
    return dict(
        compiler_params=pltpu.CompilerParams(vmem_limit_bytes=VMEM_LIMIT),
        cost_estimate=pl.CostEstimate(flops=flops, bytes_accessed=moved, transcendentals=0),
    )


def masked_taps(taps_ref, mask_ref, km_ref, sub, flip):
    for a in range(7):
        seen = mask_ref[a, pl.ds(sub * 8, 8), :]
        for b in range(7):
            tap = 48 - (a * 7 + b) if flip else a * 7 + b
            km_ref[a * 7 + b] = taps_ref[tap : tap + 1, :] * seen


def conv_kernel(place_ref, x_ref, top_ref, bot_ref, taps_ref, mask_ref, out_ref, xs_ref, km_ref):
    rows, width = 48, x_ref.shape[1] // 48
    cb = pl.program_id(0)

    @pl.when(cb == 0)
    def _():
        for w in (0, 1, 2, 51, 52, 53):
            xs_ref[w] = jnp.zeros_like(xs_ref[w])

    def fill(w, carry):
        at = pl.ds(pl.multiple_of(w * width + cb * LANES, LANES), LANES)
        xs_ref[w + 3, 0:RIM, :] = top_ref[:, at].astype(F32)
        xs_ref[w + 3, RIM : RIM + rows, :] = x_ref[:, at].astype(F32)
        xs_ref[w + 3, RIM + rows :, :] = bot_ref[:, at].astype(F32)
        return carry

    lax.fori_loop(0, 48, fill, 0)

    def band(t, carry):
        for s in range(2):
            masked_taps(taps_ref, mask_ref, km_ref.at[s], t * 2 + s, False)

        def block(i, carry):
            w0 = i * 8
            accs = []
            for s in range(2):
                acc = [jnp.zeros((8, LANES), F32) for _ in range(8)]
                for a in range(7):
                    start = t * 16 + (s * 8 + RIM - 3 + a)
                    x = [xs_ref[w0 + j, pl.ds(start, 8), :] for j in range(14)]
                    for b in range(7):
                        k = km_ref[s, a * 7 + b]
                        for j in range(8):
                            acc[j] = acc[j] + k * x[j + b]
                accs.append(acc)
            for j in range(8):
                both = jnp.concatenate([accs[0][j], accs[1][j]], axis=0).astype(BF)
                out_ref[pl.ds(pl.multiple_of((w0 + j) * rows + t * 16, 16), 16), :] = both
            return carry

        lax.fori_loop(0, 6, block, 0)
        return carry

    lax.fori_loop(0, 3, band, 0)


def conv_forward(x, top, bot, taps, mask, place, into=None):
    width = x.shape[1] // 48
    blocks = width // LANES
    whole = lambda cb, place: (0, 0)
    half = lambda cb, place: (0, place[0] * blocks + cb)
    extra = [] if into is None else [into]
    kernel = conv_kernel if into is None else conv_kernel_into
    return pl.pallas_call(
        kernel,
        out_shape=jax.ShapeDtypeStruct((48 * 48, 2 * width), BF),
        grid_spec=pltpu.PrefetchScalarGridSpec(
            num_scalar_prefetch=1,
            grid=(blocks,),
            in_specs=[
                pl.BlockSpec(x.shape, whole),
                pl.BlockSpec(top.shape, whole),
                pl.BlockSpec(bot.shape, whole),
                pl.BlockSpec((49, LANES), lambda cb, place: (0, cb)),
                pl.BlockSpec(mask.shape, lambda cb, place: (0, 0, 0)),
            ]
            + [pl.BlockSpec(memory_space=pl.ANY)] * len(extra),
            out_specs=pl.BlockSpec((48 * 48, LANES), half),
            scratch_shapes=[
                pltpu.VMEM((54, 64, LANES), F32),
                pltpu.VMEM((2, 49, 8, LANES), F32),
            ],
        ),
        input_output_aliases={} if into is None else {6: 0},
        **conv_params(54_000_000 * width, 12_000_000),
    )(place, x, top, bot, taps, mask, *extra)


def conv_kernel_into(place_ref, x_ref, top_ref, bot_ref, taps_ref, mask_ref, into_ref, *rest):
    conv_kernel(place_ref, x_ref, top_ref, bot_ref, taps_ref, mask_ref, *rest)


def back_kernel(place_ref, g_ref, top_ref, bot_ref, x_ref, cot_ref, pool_ref, taps_ref, mask_ref,
                out_ref, tap_out_ref, gs_ref, km_ref, tacc_ref, sp_ref):
    rows, width = 48, x_ref.shape[1] // 48
    cb = pl.program_id(0)

    @pl.when(cb == 0)
    def _():
        for w in (0, 1, 2, 51, 52, 53):
            gs_ref[w] = jnp.zeros_like(gs_ref[w])

    tacc_ref[...] = jnp.zeros_like(tacc_ref)

    def fill(w, carry):
        gs_ref[w + 3, 0:RIM, :] = top_ref[w].astype(F32)
        own = pl.ds(pl.multiple_of(w * rows, rows), rows)
        gs_ref[w + 3, RIM : RIM + rows, :] = g_ref[own, :].astype(F32)
        gs_ref[w + 3, RIM + rows :, :] = bot_ref[w].astype(F32)
        return carry

    lax.fori_loop(0, 48, fill, 0)

    def spread(q, carry):
        quarter = pool_ref[q] * 0.25
        sp_ref[q, pl.ds(0, 24, stride=2), :] = quarter
        sp_ref[q, pl.ds(1, 24, stride=2), :] = quarter
        return carry

    lax.fori_loop(0, 24, spread, 0)

    def band(t, carry):
        for s in range(2):
            masked_taps(taps_ref, mask_ref, km_ref.at[s], t * 2 + s, True)

        def block(i, carry):
            w0 = i * 8
            ats = [
                pl.ds(pl.multiple_of((w0 + j) * width + cb * LANES, LANES), LANES) for j in range(8)
            ]
            band_rows = pl.ds(pl.multiple_of(t * 16, 16), 16)
            vals = [x_ref[band_rows, at].astype(F32) for at in ats]
            accs = []
            for s in range(2):
                acc = [jnp.zeros((8, LANES), F32) for _ in range(8)]
                v = [val[s * 8 : s * 8 + 8] for val in vals]
                for a in range(7):
                    start = t * 16 + (s * 8 + RIM - 3 + a)
                    g = [gs_ref[w0 + j, pl.ds(start, 8), :] for j in range(14)]
                    seen = mask_ref[a, pl.ds(t * 16 + s * 8, 8), :]
                    vm = [item * seen for item in v]
                    for b in range(7):
                        k = km_ref[s, a * 7 + b]
                        tap = None
                        for j in range(8):
                            acc[j] = acc[j] + k * g[j + b]
                            term = vm[j] * g[j + b]
                            tap = term if tap is None else tap + term
                        tacc_ref[48 - (a * 7 + b)] += tap
                accs.append(acc)
            for j in range(8):
                both = jnp.concatenate([accs[0][j], accs[1][j]], axis=0)
                total = both + cot_ref[band_rows, ats[j]].astype(F32)
                total = total + sp_ref[i * 4 + j // 2, band_rows, :]
                out_ref[0, band_rows, ats[j]] = total.astype(out_ref.dtype)
            return carry

        lax.fori_loop(0, 6, block, 0)
        return carry

    lax.fori_loop(0, 3, band, 0)
    tap_out_ref[0:49, :] = jnp.sum(tacc_ref[...], axis=1)


def conv_backward(grad, top, bot, x, cot, pool, taps, mask, place, slots, kind):
    width = x.shape[1] // 48
    blocks = width // LANES
    whole = lambda cb, place: (0, 0)
    half = lambda cb, place: (0, place[0] * blocks + cb)
    return pl.pallas_call(
        back_kernel,
        out_shape=(
            jax.ShapeDtypeStruct((slots, *x.shape), kind),
            jax.ShapeDtypeStruct((56, width), F32),
        ),
        grid_spec=pltpu.PrefetchScalarGridSpec(
            num_scalar_prefetch=1,
            grid=(blocks,),
            in_specs=[
                pl.BlockSpec((48 * 48, LANES), half),
                pl.BlockSpec((48, RIM, LANES), lambda cb, place: (0, 0, place[0] * blocks + cb)),
                pl.BlockSpec((48, RIM, LANES), lambda cb, place: (0, 0, place[0] * blocks + cb)),
                pl.BlockSpec(x.shape, whole),
                pl.BlockSpec(cot.shape, whole),
                pl.BlockSpec((24, 24, LANES), lambda cb, place: (0, 0, place[0] * blocks + cb)),
                pl.BlockSpec((49, LANES), lambda cb, place: (0, cb)),
                pl.BlockSpec(mask.shape, lambda cb, place: (0, 0, 0)),
            ],
            out_specs=(
                pl.BlockSpec((1, *x.shape), lambda cb, place: (place[0] if slots == 2 else 0, 0, 0)),
                pl.BlockSpec((56, LANES), lambda cb, place: (0, cb)),
            ),
            scratch_shapes=[
                pltpu.VMEM((54, 64, LANES), F32),
                pltpu.VMEM((2, 49, 8, LANES), F32),
                pltpu.VMEM((49, 8, LANES), F32),
                pltpu.VMEM((24, 48, LANES), F32),
            ],
        ),
        **conv_params(90_000_000 * width, 25_000_000),
    )(place, grad, top, bot, x, cot, pool, taps, mask)


def join_kernel(place_ref, branch_ref, scale_ref, own_ref, other_ref, own_out, other_out, pool_out, pair_ref):
    rows, width = 48, own_ref.shape[1] // 4
    for g, (src, dst) in enumerate(((own_ref, own_out), (other_ref, other_out))):
        side = place_ref[0] if g == 0 else 1 - place_ref[0]
        at = pl.ds(pl.multiple_of(side * width, LANES), width)
        scale = scale_ref[:, at]
        for q in range(2):
            total = None
            for w in (2 * q, 2 * q + 1):
                field = src[:, w * width : (w + 1) * width].astype(F32)
                field = field + scale * branch_ref[w * rows : (w + 1) * rows, at]
                dst[0, :, w * width : (w + 1) * width] = field.astype(BF)
                total = field if total is None else total + field
            for n in range(width // LANES):
                pair_ref[q, n] = total[:, n * LANES : (n + 1) * LANES]
                even = pair_ref[q, n, pl.ds(0, 24, stride=2), :]
                odd = pair_ref[q, n, pl.ds(1, 24, stride=2), :]
                lane = pl.ds(pl.multiple_of(side * width + n * LANES, LANES), LANES)
                pool_out[q, :, lane] = (even + odd) * 0.25


def join_branch(branch, scale, own, other, place):
    width = own.shape[1] // 48
    raw = pl.BlockSpec((48, 4 * width), lambda i, place: (0, i))
    return pl.pallas_call(
        join_kernel,
        out_shape=(
            jax.ShapeDtypeStruct((2, *own.shape), BF),
            jax.ShapeDtypeStruct((1, *own.shape), BF),
            jax.ShapeDtypeStruct((24, 24, 2 * width), F32),
        ),
        grid_spec=pltpu.PrefetchScalarGridSpec(
            num_scalar_prefetch=1,
            grid=(12,),
            in_specs=[
                pl.BlockSpec((4 * 48, 2 * width), lambda i, place: (i, 0)),
                pl.BlockSpec((1, 2 * width), lambda i, place: (0, 0)),
                raw,
                raw,
            ],
            out_specs=(
                pl.BlockSpec((1, 48, 4 * width), lambda i, place: (place[0], 0, i)),
                pl.BlockSpec((1, 48, 4 * width), lambda i, place: (0, 0, i)),
                pl.BlockSpec((2, 24, 2 * width), lambda i, place: (i, 0, 0)),
            ),
            scratch_shapes=[pltpu.VMEM((2, width // LANES, 48, LANES), F32)],
        ),
        **conv_params(10_000_000, 40_000_000),
    )(place, branch, scale, own, other)


def scaled_kernel(place_ref, pool_ref, branch_ref, scale_ref, own_ref, other_ref, out_ref, sum_ref, pair_ref):
    rows, width = 48, own_ref.shape[1] // 4

    @pl.when(pl.program_id(0) == 0)
    def _():
        sum_ref[...] = jnp.zeros_like(sum_ref)

    for g, src in enumerate((own_ref, other_ref)):
        side = place_ref[0] if g == 0 else 1 - place_ref[0]
        at = pl.ds(pl.multiple_of(side * width, LANES), width)
        scale = scale_ref[:, at]
        for q in range(2):
            quarter = pool_ref[q, :, at] * 0.25
            for n in range(width // LANES):
                part = quarter[:, n * LANES : (n + 1) * LANES]
                pair_ref[q, n, pl.ds(0, 24, stride=2), :] = part
                pair_ref[q, n, pl.ds(1, 24, stride=2), :] = part
            spread = jnp.concatenate([pair_ref[q, n] for n in range(width // LANES)], axis=1)
            for w in (2 * q, 2 * q + 1):
                here = slice(w * rows, (w + 1) * rows)
                grad = src[:, w * width : (w + 1) * width].astype(F32) + spread
                part = grad * branch_ref[here, at]
                sum_ref[:, at] += jnp.sum(part.reshape(6, 8, width), axis=0)
                out_ref[here, at] = (grad * scale).astype(BF)


def scaled_grads(pool, branch, scale, own, other, place):
    width = own.shape[1] // 48
    raw = pl.BlockSpec((48, 4 * width), lambda i, place: (0, i))
    return pl.pallas_call(
        scaled_kernel,
        out_shape=(
            jax.ShapeDtypeStruct(branch.shape, BF),
            jax.ShapeDtypeStruct((8, 2 * width), F32),
        ),
        grid_spec=pltpu.PrefetchScalarGridSpec(
            num_scalar_prefetch=1,
            grid=(12,),
            in_specs=[
                pl.BlockSpec((2, 24, 2 * width), lambda i, place: (i, 0, 0)),
                pl.BlockSpec((4 * 48, 2 * width), lambda i, place: (i, 0)),
                pl.BlockSpec((1, 2 * width), lambda i, place: (0, 0)),
                raw,
                raw,
            ],
            out_specs=(
                pl.BlockSpec((4 * 48, 2 * width), lambda i, place: (i, 0)),
                pl.BlockSpec((8, 2 * width), lambda i, place: (0, 0)),
            ),
            scratch_shapes=[pltpu.VMEM((2, width // LANES, 48, LANES), F32)],
        ),
        **conv_params(10_000_000, 40_000_000),
    )(place, pool, branch, scale, own, other)


CHUNK = 256
PAIRS = 2
WIDE = PAIRS * LANES
NT = (((1,), (1,)), ((), ()))
TN = (((0,), (0,)), ((), ()))


def dot(left, right, dims):
    return lax.dot_general(left, right, dims, preferred_element_type=F32)


NN = (((1,), (0,)), ((), ()))


def lane_half(shape, side):
    lanes = lax.broadcasted_iota(jnp.int32, shape, len(shape) - 1)
    return (lanes < 64) if side == 0 else (lanes >= 64)


def fill_window(win_ref, before, own, after):
    count = own.shape[0]
    win_ref[0:count] = before[...]
    win_ref[count : 2 * count] = own[...]
    win_ref[2 * count : 3 * count] = after[...]
    win_ref[3 * count :] = jnp.zeros_like(win_ref[3 * count :])


def attend_kernel(first_ref, last_ref, q_ref, kb_ref, k_ref, ka_ref, vb_ref, v_ref, va_ref,
                  klab_ref, qlab_ref, out_ref, total_ref, kw_ref, vw_ref):
    fill_window(kw_ref, kb_ref, k_ref, ka_ref)
    fill_window(vw_ref, vb_ref, v_ref, va_ref)
    heads = [(pair, side) for pair in range(PAIRS) for side in range(2)]
    lanes = [slice(pair * LANES, (pair + 1) * LANES) for pair in range(PAIRS)]
    for n in range(3):
        rows = slice(n * 192, (n + 1) * 192)
        q = q_ref[rows, :] * jnp.asarray(0.125, BF)
        q_half = []
        for pair, side in heads:
            own = q[:, lanes[pair]]
            q_half.append(jnp.where(lane_half(own.shape, side), own, jnp.zeros_like(own)))
        q_lab = qlab_ref[n, 0:1, :]

        def chunk(c, carry):
            at = pl.ds(pl.multiple_of(c * CHUNK, CHUNK), CHUNK)
            same = klab_ref[at, 0:1] == q_lab
            new = []
            scores = [
                jnp.where(same, dot(kw_ref[at, lanes[pair]], q_half[i], NT), NEG)
                for i, (pair, side) in enumerate(heads)
            ]
            for i, (pair, side) in enumerate(heads):
                top, total, acc = carry[i]
                best = jnp.maximum(top, jnp.max(scores[i], axis=0, keepdims=True))
                p = jnp.exp(scores[i] - best)
                shrink = jnp.exp(top - best)
                total = total * shrink + jnp.sum(p, axis=0, keepdims=True)
                acc = acc * shrink + dot(vw_ref[at, lanes[pair]], p.astype(BF), TN)
                new.append((best, total, acc))
            return tuple(new)

        start = (jnp.full((1, 192), NEG, F32), jnp.zeros((1, 192), F32), jnp.zeros((LANES, 192), F32))
        done = lax.fori_loop(first_ref[n], last_ref[n], chunk, (start,) * len(heads))
        for pair in range(PAIRS):
            outs = []
            for side in range(2):
                top, total, acc = done[2 * pair + side]
                outs.append(acc * (1.0 / total))
                total_ref[pair, n, side : side + 1, :] = top + jnp.log(total)
            both = jnp.concatenate([outs[0][:64], outs[1][64:]], axis=0)
            out_ref[rows, lanes[pair]] = both.T.astype(BF)


def attend(q, k, v, around, qlab, klab, first, last):
    count, width = q.shape
    window = -(-3 * count // CHUNK) * CHUNK
    block = pl.BlockSpec((count, WIDE), lambda p, *_: (0, p))
    stats = pl.BlockSpec((PAIRS, 3, 2, 192), lambda p, *_: (p, 0, 0, 0))
    return pl.pallas_call(
        attend_kernel,
        out_shape=(
            jax.ShapeDtypeStruct(q.shape, BF),
            jax.ShapeDtypeStruct((width // LANES, 3, 2, 192), F32),
        ),
        grid_spec=pltpu.PrefetchScalarGridSpec(
            num_scalar_prefetch=2,
            grid=(width // WIDE,),
            in_specs=[block] * 7
            + [
                pl.BlockSpec(klab.shape, lambda p, *_: (0, 0)),
                pl.BlockSpec(qlab.shape, lambda p, *_: (0, 0, 0)),
            ],
            out_specs=(block, stats),
            scratch_shapes=[pltpu.VMEM((window, WIDE), BF), pltpu.VMEM((window, WIDE), BF)],
        ),
        **conv_params(40_000_000 * width, 20_000_000),
    )(first, last, q, around[0], k, around[1], around[2], v, around[3], klab, qlab)


def attend_back_kernel(first_ref, last_ref, q_ref, kb_ref, k_ref, ka_ref, vb_ref, v_ref, va_ref,
                       do_ref, o_ref, total_ref, klab_ref, qlab_ref,
                       dq_ref, dk_ref, dv_ref, before_ref, after_ref,
                       kw_ref, vw_ref, dkw_ref, dvw_ref):
    count = q_ref.shape[0]
    fill_window(kw_ref, kb_ref, k_ref, ka_ref)
    fill_window(vw_ref, vb_ref, v_ref, va_ref)
    dkw_ref[...] = jnp.zeros_like(dkw_ref)
    dvw_ref[...] = jnp.zeros_like(dvw_ref)
    heads = [(pair, side) for pair in range(PAIRS) for side in range(2)]
    lanes = [slice(pair * LANES, (pair + 1) * LANES) for pair in range(PAIRS)]
    for n in range(3):
        rows = slice(n * 192, (n + 1) * 192)
        q = q_ref[rows, :] * jnp.asarray(0.125, BF)
        do = do_ref[rows, :]
        halves = [lane_half((192, LANES), side) for side in range(2)]
        q_half = [jnp.where(halves[s], q[:, lanes[p]], jnp.zeros((), BF)) for p, s in heads]
        do_half = [jnp.where(halves[s], do[:, lanes[p]], jnp.zeros((), BF)) for p, s in heads]
        q_lab = qlab_ref[n, 0:1, :]
        flow = do.astype(F32) * o_ref[rows, :].astype(F32)
        delta = []
        for p in range(PAIRS):
            turned = flow[:, lanes[p]].T
            delta += [jnp.sum(turned[s * 64 : s * 64 + 64], axis=0, keepdims=True) for s in range(2)]

        def chunk(c, carry):
            at = pl.ds(pl.multiple_of(c * CHUNK, CHUNK), CHUNK)
            same = klab_ref[at, 0:1] == q_lab
            kcs = [kw_ref[at, lanes[pair]] for pair in range(PAIRS)]
            vcs = [vw_ref[at, lanes[pair]] for pair in range(PAIRS)]
            scores = [dot(kcs[p], q_half[i], NT) for i, (p, s) in enumerate(heads)]
            dps = [dot(vcs[p], do_half[i], NT) for i, (p, s) in enumerate(heads)]
            ps, dss = [], []
            for i, (p, s) in enumerate(heads):
                raised = jnp.where(same, scores[i] - total_ref[p, n, s : s + 1, :], NEG)
                ps.append(jnp.exp(raised))
            for i, (p, s) in enumerate(heads):
                dss.append((ps[i] * (dps[i] - delta[i])).astype(BF))
            low = [item.astype(BF) for item in ps]
            dqs = []
            for p in range(PAIRS):
                e, o = 2 * p, 2 * p + 1
                dvw_ref[at, lanes[p]] += dot(low[e], do_half[e], NN) + dot(low[o], do_half[o], NN)
                dkw_ref[at, lanes[p]] += dot(dss[e], q_half[e], NN) + dot(dss[o], q_half[o], NN)
                two = [dot(dss[e], kcs[p], TN), dot(dss[o], kcs[p], TN)]
                dqs.append(carry[p] + jnp.where(lane_half((192, LANES), 0), two[0], two[1]))
            return tuple(dqs)

        dqs = lax.fori_loop(
            first_ref[n], last_ref[n], chunk, tuple(jnp.zeros((192, LANES), F32) for _ in range(PAIRS))
        )
        for pair in range(PAIRS):
            dq_ref[rows, lanes[pair]] = (dqs[pair] * 0.125).astype(BF)
    dk_ref[...] = dkw_ref[count : 2 * count, :]
    dv_ref[...] = dvw_ref[count : 2 * count, :]
    before_ref[0] = dkw_ref[0:count, :].astype(BF)
    before_ref[1] = dvw_ref[0:count, :].astype(BF)
    after_ref[0] = dkw_ref[2 * count : 3 * count, :].astype(BF)
    after_ref[1] = dvw_ref[2 * count : 3 * count, :].astype(BF)


def attend_back(q, k, v, around, grad, out, total, qlab, klab, first, last):
    count, width = q.shape
    window = -(-3 * count // CHUNK) * CHUNK
    block = pl.BlockSpec((count, WIDE), lambda p, *_: (0, p))
    stats = pl.BlockSpec((PAIRS, 3, 2, 192), lambda p, *_: (p, 0, 0, 0))
    pair = pl.BlockSpec((2, count, WIDE), lambda p, *_: (0, 0, p))
    return pl.pallas_call(
        attend_back_kernel,
        out_shape=(
            jax.ShapeDtypeStruct(q.shape, BF),
            jax.ShapeDtypeStruct(q.shape, F32),
            jax.ShapeDtypeStruct(q.shape, F32),
            jax.ShapeDtypeStruct((2, count, width), BF),
            jax.ShapeDtypeStruct((2, count, width), BF),
        ),
        grid_spec=pltpu.PrefetchScalarGridSpec(
            num_scalar_prefetch=2,
            grid=(width // WIDE,),
            in_specs=[block] * 9
            + [
                stats,
                pl.BlockSpec(klab.shape, lambda p, *_: (0, 0)),
                pl.BlockSpec(qlab.shape, lambda p, *_: (0, 0, 0)),
            ],
            out_specs=(block, block, block, pair, pair),
            scratch_shapes=[
                pltpu.VMEM((window, WIDE), BF),
                pltpu.VMEM((window, WIDE), BF),
                pltpu.VMEM((window, WIDE), F32),
                pltpu.VMEM((window, WIDE), F32),
            ],
        ),
        **conv_params(55_000_000 * width, 20_000_000),
    )(first, last, q, around[0], k, around[1], around[2], v, around[3], grad, out, total, klab, qlab)


def on_device(
    lo_in,
    hi_in,
    image_ids,
    cn_kernel,
    cn_gain,
    cn_w1,
    cn_w2,
    cn_scale,
    ad_proj,
    ad_kernel,
    gate_w1,
    gate_w2,
    ln1_gain,
    qkv,
    out_proj,
    ln2_gain,
    fc1,
    fc2,
    d_lo_out,
    d_hi_out,
):
    micro_count, row_count, col_count, d_shard = lo_in.shape
    hi_rows = hi_in.shape[1]
    hi_cols = HCOLS
    c_shard = hi_in.shape[3] // hi_cols
    d_own, c_own = 2 * d_shard, 2 * c_shard
    tok_count = row_count * col_count
    pix_count = hi_rows * hi_cols
    mine = lax.axis_index("mb")
    row_start = lax.axis_index(TILE) * row_count
    head_count = d_own // HDIM

    fast = c_shard % LANES == 0 and lax.axis_size("tp") == 1
    hi_raw = hi_in.reshape(2, hi_rows, hi_cols * c_shard)
    hi_own, hi_other = swap_micro(hi_raw)
    up, down = rim_pair(hi_raw, RIM, 1)
    own_rims, other_rims = swap_micro(jnp.stack([up, down], axis=1))
    hid_shard, gh_shard, ff_shard = cn_w1.shape[1], gate_w1.shape[1], fc1.shape[1]
    mlp = gather_all(jnp.concatenate([cn_w1, cn_w2.T, ad_proj, gate_w1], axis=1))
    def apply(left, pair):
        return jnp.concatenate([matmul(left, pair[0]), matmul(left, pair[1])], axis=1)

    def apply_t(left, pair):
        width = pair[0].shape[1]
        return matmul_nt(left[:, :width], pair[0]) + matmul_nt(left[:, width:], pair[1])

    def cols(values):
        width = values.shape[1] // 2
        return [values[:, :width], values[:, width:]]

    canvas_ids = lax.dynamic_index_in_dim(image_ids, mine, 0, keepdims=False)
    small_ids = row_labels(canvas_ids, row_start, row_count, 1)
    lo_mid = small_ids[1 : 1 + row_count]
    hi_ids = row_labels(jnp.repeat(canvas_ids, 2), 2 * row_start, hi_rows, 3)
    hi_mid = hi_ids[3 : 3 + hi_rows]

    def both_shards(shard, axis):
        return in_order(shard, lax.ppermute(shard, "mb", SWAP), axis)

    other_kernel = lax.ppermute(cn_kernel, "mb", SWAP)
    conv_taps = in_order(cn_kernel, other_kernel, 1)

    own_place = mine.reshape(1).astype(jnp.int32)
    other_place = 1 - own_place
    seen = jnp.stack([(hi_ids[a : a + hi_rows] == hi_mid).astype(F32) for a in range(7)])
    mask = jnp.broadcast_to(seen[:, :, None], (7, hi_rows, LANES))
    own_taps, other_taps = cn_kernel.astype(F32), other_kernel.astype(F32)

    def natural(own, other):
        shape = (-1, hi_cols, c_shard)
        return in_order(own.reshape(shape), other.reshape(shape), 2)

    if fast:
        conv_flat = conv_forward(hi_own, *own_rims, own_taps, mask, own_place)
        conv_flat = conv_forward(hi_other, *other_rims, other_taps, mask, other_place, conv_flat)
    else:
        hi_field = natural(hi_own, hi_other)
        hi_pad = jnp.concatenate(
            [
                natural(own_rims[0], other_rims[0])[-3:],
                hi_field,
                natural(own_rims[1], other_rims[1])[:3],
            ]
        )
        conv_low = depthwise(hi_pad, conv_taps, hi_ids, hi_mid, 7, False).astype(BF)
        conv_flat = conv_low.transpose(1, 0, 2).reshape(pix_count, c_own)
    conv_full = features(conv_flat)
    normed, norm_pull = jax.vjp(layer_norm, conv_full.astype(F32), cn_gain.astype(F32))
    normed_low, mlp, gate_w2 = together(normed.astype(BF), mlp, gate_w2)
    mlp_in = [mlp[g, :, :hid_shard] for g in range(2)]
    mlp_out = [mlp[g, :, hid_shard : 2 * hid_shard] for g in range(2)]
    ad_matrix = [mlp[g, :, 2 * hid_shard : 2 * hid_shard + d_shard] for g in range(2)]
    gate_in = [mlp[g, :, 2 * hid_shard + d_shard :] for g in range(2)]
    vit = gather_all(
        jnp.concatenate(
            [
                gate_w2.T,
                qkv[0],
                qkv[1],
                qkv[2],
                out_proj.T,
                fc1,
                fc2.T,
            ],
            axis=1,
        )
    )
    cuts = np.cumsum([0, gh_shard, d_shard, d_shard, d_shard, d_shard, ff_shard, ff_shard])
    gate_out, q_w, k_w, v_w, out_w, ff_in, ff_out = [
        [vit[g, :, int(cuts[i]) : int(cuts[i + 1])] for g in range(2)] for i in range(7)
    ]

    inner_act, inner_slope = zip(*[gelu_pair(matmul(normed_low, mlp_in[g])) for g in range(2)])
    lo_in, d_lo_out, cn_scale, ad_kernel, first_act = together(
        lo_in, d_lo_out, cn_scale, ad_kernel, inner_act[0]
    )
    inner_act = (first_act, inner_act[1])
    lo_low = in_order(*swap_micro(lo_in.reshape(2, tok_count, d_shard)), 1)
    lo_field = lo_low.astype(F32)
    ad_taps = both_shards(ad_kernel, 1)
    hi_scale = both_shards(cn_scale, 0).astype(F32)
    branch = partial_sums(
        matmul_nt(inner_act[0], mlp_out[0]) + matmul_nt(inner_act[1], mlp_out[1])
    )
    if fast:
        hi_mine, hi_sent, pooled = join_branch(branch, hi_scale[None], hi_own, hi_other, own_place)
        pooled = pooled.transpose(1, 0, 2)
    else:
        branch_rows = branch.reshape(hi_cols, hi_rows, c_own).transpose(1, 0, 2)
        hi_sum = hi_field.astype(F32) + hi_scale * branch_rows
        pooled = jnp.mean(hi_sum.reshape(row_count, 2, col_count, 2, c_own), axis=(1, 3))
    pooled_full = features(pooled.reshape(tok_count, c_own).astype(BF))
    pooled_full, d_hi_out = together(pooled_full, d_hi_out)
    cot_own, cot_other = swap_micro(d_hi_out.reshape(2, hi_rows, hi_cols * c_shard))
    proj_low = apply(pooled_full, ad_matrix).astype(BF)
    proj_pad = rim_rows(proj_low.reshape(row_count, col_count, d_own), 1)
    local_conv = depthwise(proj_pad, ad_taps, small_ids, lo_mid, 3, False).reshape(
        tok_count, d_own
    )
    gate_hidden, gate_slope = gelu_pair(apply(pooled_full, gate_in))
    gate_val = jnp.tanh(partial_sums(apply_t(gate_hidden, gate_out)))
    mixed_one = lo_field + gate_val * local_conv
    mixed_full = features(mixed_one.astype(BF))
    norm_one, first_pull = jax.vjp(layer_norm, mixed_full.astype(F32), ln1_gain.astype(F32))
    norm_low = norm_one.astype(BF)
    queries = apply(norm_low, q_w).astype(BF)
    key_rows = apply(norm_low, k_w).astype(BF)
    value_rows = apply(norm_low, v_w).astype(BF)
    around = rim_pair(key_rows, tok_count, 0) + rim_pair(value_rows, tok_count, 0)
    near = row_labels(canvas_ids, row_start, row_count, row_count)
    key_tok = jnp.repeat(near, col_count)
    window = -(-3 * tok_count // CHUNK) * CHUNK
    key_tok = jnp.pad(key_tok, (0, window - 3 * tok_count), constant_values=-2)
    key_lab = jnp.broadcast_to(key_tok[:, None], (window, LANES))
    query_lab = jnp.broadcast_to(jnp.repeat(lo_mid, col_count).reshape(3, 1, 192), (3, 8, 192))
    edge = jnp.arange(3 * row_count)
    first_row = jnp.min(jnp.where(near[None] == lo_mid[::8][:, None], edge, 3 * row_count), axis=1)
    last_row = jnp.max(jnp.where(near[None] == lo_mid[7::8][:, None], edge, -1), axis=1) + 1
    first = (first_row * col_count // CHUNK).astype(jnp.int32)
    last = ((last_row * col_count + CHUNK - 1) // CHUNK).astype(jnp.int32)
    attended, log_total = attend(
        queries, key_rows, value_rows, around, query_lab, key_lab, first, last
    )
    mixed_two = mixed_one + partial_sums(apply_t(attended, out_w))
    if fast:
        hi_got = lax.ppermute(hi_sent, "mb", SWAP)
        mixed_two, hi_got = together(mixed_two, hi_got)
    mixed2_full = features(mixed_two.astype(BF))
    norm_two, second_pull = jax.vjp(layer_norm, mixed2_full.astype(F32), ln2_gain.astype(F32))
    norm2_low = norm_two.astype(BF)
    ff_hidden, ff_slope = gelu_pair(apply(norm2_low, ff_in))
    lo_result = (mixed_two + partial_sums(apply_t(ff_hidden, ff_out))).astype(BF)

    grad_low = in_order(*swap_micro(d_lo_out.reshape(2, tok_count, d_shard)), 1)
    grad_out = grad_low.astype(F32)
    ff_grad_full = features(grad_low)
    ff_pre_grad = (apply(ff_grad_full, ff_out) * ff_slope.astype(F32)).astype(BF)
    second_grad = partial_sums(apply_t(ff_pre_grad, ff_in)).astype(BF)
    back_two, grad_ln2 = second_pull(features(second_grad).astype(F32))
    p_ff = stacked_grads([norm2_low, ff_grad_full], [ff_pre_grad, ff_hidden])
    grad_two, p_ff, cot_other = together(grad_out + own_slice(back_two), p_ff, cot_other)
    s_ff = reduce_tiles(p_ff)
    att_grad_full = features(grad_two.astype(BF))
    att_grad = apply(att_grad_full, out_w).astype(BF)
    query_grad, key_own, value_own, to_before, to_after = attend_back(
        queries, key_rows, value_rows, around, att_grad, attended, log_total, query_lab, key_lab, first, last
    )
    devices = tile_count()
    steps = [(i, i + 1) for i in range(devices - 1)]
    from_before = lax.ppermute(to_after, TILE, steps)
    from_after = lax.ppermute(to_before, TILE, [(j, i) for i, j in steps])
    key_grad, value_grad = [
        (own + from_before[i].astype(F32) + from_after[i].astype(F32)).astype(BF)
        for i, own in enumerate((key_own, value_own))
    ]
    first_grad = partial_sums(
        apply_t(query_grad, q_w) + apply_t(key_grad, k_w) + apply_t(value_grad, v_w)
    ).astype(BF)
    back_one, grad_ln1 = first_pull(features(first_grad).astype(F32))
    grad_one = grad_two + own_slice(back_one)
    gate_pre_grad = (grad_one * local_conv * (1.0 - gate_val * gate_val)).astype(BF)
    gate_grad_full = features(gate_pre_grad)
    p_att = stacked_grads(
        [gate_grad_full, norm_low, att_grad_full],
        [gate_hidden, jnp.concatenate([query_grad, key_grad, value_grad], axis=1), attended],
    )
    hidden_grad = (apply(gate_grad_full, gate_out) * gate_slope.astype(F32)).astype(BF)
    local_grad = (grad_one * gate_val).astype(BF).reshape(row_count, col_count, d_own)
    local_pad = rim_rows(local_grad, 1)
    proj_grad = (
        depthwise(local_pad, ad_taps, small_ids, lo_mid, 3, True)
        .reshape(tok_count, d_own)
        .astype(BF)
    )
    grad_ad_kernel = tap_grads(proj_pad, local_grad, small_ids, lo_mid, 3)
    p_ad = matmul_tn(pooled_full, jnp.concatenate([proj_grad, hidden_grad], axis=1)).astype(BF)
    pooled_grad = partial_sums(apply_t(hidden_grad, gate_in) + apply_t(proj_grad, ad_matrix))
    pooled_grad, p_att, p_ad = together(pooled_grad, p_att, p_ad)
    s_att, s_ad = reduce_tiles(p_att), reduce_tiles(p_ad)
    pool_cols = pooled_grad.reshape(row_count, col_count, c_own).transpose(1, 0, 2)
    if fast:
        scaled_grad, scale_parts = scaled_grads(
            pool_cols, branch, hi_scale[None], cot_own, cot_other, own_place
        )
        grad_scale = jnp.sum(scale_parts, axis=0)
    else:
        spread_grad = jnp.repeat(jnp.repeat(pool_cols.transpose(1, 0, 2) * 0.25, 2, 0), 2, 1)
        hi_grad = natural(cot_own, cot_other).astype(F32) + spread_grad
        grad_cols = hi_grad.transpose(1, 0, 2).reshape(pix_count, c_own)
        grad_scale = jnp.sum(grad_cols * branch, axis=0)
        scaled_grad = (grad_cols * hi_scale).astype(BF)
    branch_full = lax.optimization_barrier(features(scaled_grad))
    first = mine == 0
    p_w2 = [matmul_tn(branch_full, act).astype(BF) for act in inner_act]
    branch_full, *p_w2, s_ff = together(branch_full, *p_w2, s_ff)
    s_w2 = [reduce_tiles(item) for item in p_w2]
    grad_first = (matmul(branch_full, mlp_out[0]) * inner_slope[0].astype(F32)).astype(BF)
    w1_first = matmul_tn(normed_low, grad_first).astype(BF)
    branch_full, w1_first = together(branch_full, w1_first)
    core_first = core_sum(w1_first)
    grad_second = (matmul(branch_full, mlp_out[1]) * inner_slope[1].astype(F32)).astype(BF)
    w1_second = matmul_tn(normed_low, grad_second).astype(BF)
    grad_second, w1_second = together(grad_second, w1_second)
    core_second = core_sum(w1_second)
    normed_part = matmul_nt(grad_first, mlp_in[0])
    normed_part, core_first, core_second = together(normed_part, core_first, core_second)
    w1_own = jnp.where(first, core_first, core_second)
    w1_sent = jnp.where(first, core_second, core_first)
    piece = w1_sent.shape[1] // 2
    w1_got = [
        lax.ppermute(item, "mb", SWAP) for item in (w1_sent[:, :piece], w1_sent[:, piece:])
    ]
    normed_grad = partial_sums(normed_part + matmul_nt(grad_second, mlp_in[1])).astype(BF)
    back_conv, grad_cn_gain = norm_pull(features(normed_grad).astype(F32))
    conv_grad, w1_got[0] = together(own_slice(back_conv).astype(BF), w1_got[0])
    conv_cols = conv_grad.reshape(hi_cols, hi_rows, c_own)
    grad_up, grad_down = rim_pair(conv_cols, RIM, 1)
    if fast:
        ghi_sent, taps_other = conv_backward(
            conv_grad, grad_up, grad_down, hi_other, cot_other, pool_cols, other_taps, mask, other_place, 1, BF
        )
        conv_grad, ghi_sent, w1_got[1] = together(conv_grad, ghi_sent, w1_got[1])
        w1_sum = add_low(w1_own, jnp.concatenate(w1_got, axis=1))
        ghi_mine, taps_own = conv_backward(
            conv_grad, grad_up, grad_down, hi_own, cot_own, pool_cols, own_taps, mask, own_place, 2, F32
        )
        tap_sums = jnp.concatenate([taps_own, taps_other])
    else:
        conv_grad = conv_cols.transpose(1, 0, 2)
        conv_pad = jnp.concatenate(
            [grad_up.transpose(1, 0, 2)[-3:], conv_grad, grad_down.transpose(1, 0, 2)[:3]]
        )
        hi_back = hi_grad + depthwise(conv_pad, conv_taps, hi_ids, hi_mid, 7, True)
        grad_cn_kernel = tap_grads(hi_pad, conv_grad, hi_ids, hi_mid, 7)
        tap_sums = jnp.concatenate(halves(grad_cn_kernel))
        w1_sum = add_low(w1_own, jnp.concatenate(w1_got, axis=1))

    chips = lax.axis_size("chip")
    w1_sum = w1_sum.reshape(chips, w1_sum.shape[0] // chips, w1_sum.shape[1])
    if chips & (chips - 1):
        w1_sum = lax.psum_scatter(w1_sum, "chip", scatter_dimension=0, tiled=True)
    else:
        own, got = chip_step(w1_sum, 1)
        tap_sums, got, s_att, s_ad = together(tap_sums, got, s_att, s_ad)
        w1_sum, bit = add_low(own, got), 2
        while bit < chips:
            w1_sum, bit = add_low(*chip_step(w1_sum, bit)), 2 * bit

    own_terms, sent_terms = zip(*[halves(item) for item in (grad_scale, grad_ad_kernel)])
    others = (*own_terms, *sent_terms, grad_cn_gain, grad_ln1, grad_ln2)
    sizes = [int(item) for item in np.cumsum([0] + [item.size for item in others])]
    flat = jnp.concatenate([item.reshape(-1) for item in others])
    flat = jnp.pad(flat, (0, -sizes[-1] % (8 * c_shard))).reshape(-1, c_shard)
    tap_rows = tap_sums.shape[0] // 2
    small = jnp.concatenate([tap_sums, flat])
    if fast:
        ghi_got = lax.ppermute(ghi_sent, "mb", SWAP)
        small, ghi_got = together(small, ghi_got)
    small = sum_everywhere(small)
    got = lax.ppermute(small[tap_rows:], "mb", SWAP)
    g_kernel = (small[:tap_rows] + got[:tap_rows])[: cn_kernel.shape[0]]
    flat, got = small[2 * tap_rows :].reshape(-1), got[tap_rows:].reshape(-1)
    pieces = [
        (flat[sizes[i] : sizes[i + 1]] + got[sizes[j] : sizes[j + 1]]).reshape(others[i].shape)
        for i, j in ((0, 2), (1, 3), (4, 4), (5, 5), (6, 6))
    ]
    g_scale, g_taps, *gain_sums = pieces

    def leave(values, kind):
        own, sent = halves(values)
        other = lax.ppermute(sent.astype(BF), "mb", SWAP)
        return both_micro(own.astype(kind), other.astype(kind))

    lo_stack = leave(lo_result.reshape(row_count, col_count, d_own), BF)
    if fast:
        hi_stack, ghi_stack = [
            lax.dynamic_update_slice_in_dim(stack, got.astype(stack.dtype), 1 - mine, 0)
            for stack, got in ((hi_mine, hi_got), (ghi_mine, ghi_got))
        ]
    else:
        hi_stack = leave(hi_sum, BF)
        ghi_stack = leave(hi_back, F32)
    glo_stack = leave(grad_one.reshape(row_count, col_count, d_own), F32)

    (g_w2,) = settle(jnp.concatenate(s_w2, axis=1), (hid_shard,))
    hi_stack = hi_stack.reshape(2, hi_rows, 1, hi_cols * c_shard)
    ghi_stack, w1_sum = together(ghi_stack.reshape(2, hi_rows, -1, 128), w1_sum)
    ghi_stack = ghi_stack.reshape(2, hi_rows, 1, hi_cols * c_shard)
    g_w1 = all_columns(w1_sum.reshape(-1, w1_sum.shape[-1])).astype(F32)
    g_fc1, g_fc2 = settle(s_ff, (ff_shard, ff_shard))
    g_gate_w2, g_q, g_k, g_v, g_out = settle(s_att, (gh_shard, d_shard, d_shard, d_shard, d_shard))
    g_ad, g_gate_w1 = settle(s_ad, (d_shard, gh_shard))

    return (
        lo_stack,
        hi_stack,
        glo_stack,
        ghi_stack,
        g_kernel,
        gain_sums[0],
        g_w1,
        g_w2.T,
        g_scale,
        g_ad,
        g_taps,
        g_gate_w1,
        g_gate_w2.T,
        gain_sums[1],
        jnp.stack([g_q, g_k, g_v]),
        g_out.T,
        gain_sums[2],
        g_fc1,
        g_fc2.T,
    )


def solution(mesh):
    tiles, mps = mesh.shape["tile"], mesh.shape["mp"]
    fine = Mesh(mesh.devices.reshape(tiles // 2, 2, 2, mps // 2), (*TILE, "mb", "tp"))
    mp = ("mb", "tp")
    in_specs = (
        P(None, TILE, None, mp),
        P(None, TILE, mp, None),
        P(),
        P(None, mp),
        P(),
        P(TILE, mp),
        P(mp, TILE),
        P(mp),
        P(TILE, mp),
        P(None, mp),
        P(TILE, mp),
        P(mp, TILE),
        P(),
        P(None, TILE, mp),
        P(mp, TILE),
        P(),
        P(TILE, mp),
        P(mp, TILE),
        P(None, TILE, None, mp),
        P(None, TILE, mp, None),
    )
    out_specs = (
        P(None, TILE, None, mp),
        P(None, TILE, mp, None),
        P(None, TILE, None, mp),
        P(None, TILE, mp, None),
        P(None, mp),
        P(),
        P(TILE, mp),
        P(mp, TILE),
        P(mp),
        P(TILE, mp),
        P(None, mp),
        P(TILE, mp),
        P(mp, TILE),
        P(),
        P(None, TILE, mp),
        P(mp, TILE),
        P(),
        P(TILE, mp),
        P(mp, TILE),
    )
    return jax.shard_map(
        on_device, mesh=fine, in_specs=in_specs, out_specs=out_specs, check_vma=False
    )
```

```python
import functools

import jax
import jax.numpy as jnp
import numpy as np
from jax import lax
from jax.experimental import pallas as pl
from jax.experimental.pallas import tpu as pltpu
from jax.sharding import Mesh
from jax.sharding import PartitionSpec as P

HDIM = 64
IMG_ROWS = 24
HCOLS = 48

EPS = 1e-06
NEG = -1e30
BF = jnp.bfloat16
F32 = jnp.float32
TILE = ("chip", "core")
ALL = ("mb", *TILE)


def tile_count():
    return lax.axis_size("chip") * lax.axis_size("core")


def rim_pair(value, width, axis):
    devices, length = tile_count(), value.shape[axis]
    up = [(i, (i + 1) % devices) for i in range(devices - 1)]
    down = [(j, i) for i, j in up]
    before = lax.ppermute(lax.slice_in_dim(value, length - width, length, axis=axis), TILE, up)
    after = lax.ppermute(lax.slice_in_dim(value, 0, width, axis=axis), TILE, down)
    return before, after


def rim_rows(value, width):
    devices, length = tile_count(), value.shape[0]
    up = [(i, (i + 1) % devices) for i in range(devices - 1)]
    down = [(j, i) for i, j in up]
    before = lax.ppermute(value[length - width :], TILE, up)
    after = lax.ppermute(value[:width], TILE, down)
    return jnp.concatenate([before, value, after], axis=0)


def matmul(left, right):
    return jnp.dot(left, right, preferred_element_type=F32)


def matmul_tn(left, right):
    return lax.dot_general(left, right, (((0,), (0,)), ((), ())), preferred_element_type=F32)


def matmul_nt(left, right):
    return lax.dot_general(left, right, (((1,), (1,)), ((), ())), preferred_element_type=F32)


def layer_norm(values, gain_vec):
    average = jnp.mean(values, axis=-1, keepdims=True)
    centered = values - average
    variance = jnp.mean(centered * centered, axis=-1, keepdims=True)
    return centered * lax.rsqrt(variance + EPS) * gain_vec


def gelu_pair(values):
    cdf = 0.5 + 0.5 * lax.erf(values * 0.7071067811865476)
    slope = cdf + values * (0.3989422804014327 * jnp.exp(-0.5 * values * values))
    return (values * cdf).astype(BF), slope.astype(BF)


def features(values):
    parts = lax.axis_size("tp")
    if parts == 1:
        return values
    rows, width = values.shape
    full = lax.all_gather(values.reshape(rows, 2, width // 2), "tp", axis=2)
    return full.reshape(rows, parts * width)


def partial_sums(values):
    parts = lax.axis_size("tp")
    if parts == 1:
        return values
    rows, width = values.shape
    split = values.reshape(rows, 2, parts, width // (2 * parts))
    return lax.psum_scatter(split, "tp", scatter_dimension=2).reshape(rows, width // parts)


def own_slice(values):
    parts = lax.axis_size("tp")
    if parts == 1:
        return values
    rows, width = values.shape
    split = values.reshape(rows, 2, parts, width // (2 * parts))
    own = lax.dynamic_index_in_dim(split, lax.axis_index("tp"), 2, keepdims=False)
    return own.reshape(rows, width // parts)


SWAP = [(0, 1), (1, 0)]


def swap_micro(values):
    mine = lax.axis_index("mb")
    own = lax.dynamic_index_in_dim(values, mine, 0, keepdims=False)
    sent = lax.dynamic_index_in_dim(values, 1 - mine, 0, keepdims=False)
    return own, lax.ppermute(sent, "mb", SWAP)


def in_order(own, other, axis):
    first = lax.axis_index("mb") == 0
    return jnp.concatenate(
        [jnp.where(first, own, other), jnp.where(first, other, own)], axis=axis
    )


def both_micro(own, other):
    first = lax.axis_index("mb") == 0
    return jnp.stack([jnp.where(first, own, other), jnp.where(first, other, own)])


def halves(values):
    width = values.shape[-1] // 2
    mine = lax.axis_index("mb")
    own = lax.dynamic_slice_in_dim(values, mine * width, width, values.ndim - 1)
    sent = lax.dynamic_slice_in_dim(values, (1 - mine) * width, width, values.ndim - 1)
    return own, sent


def row_labels(labels, first_row, count_rows, margin):
    padded = jnp.pad(labels, (margin, margin), constant_values=-1)
    return lax.dynamic_slice_in_dim(padded, first_row, count_rows + 2 * margin, 0)


def depthwise(padded, kernel, ids_pad, ids_mid, tap_size, flipped):
    margin = tap_size // 2
    row_count = ids_mid.shape[0]
    col_count = padded.shape[1]
    widened = jnp.pad(padded, ((0, 0), (margin, margin), (0, 0)))
    summed = jnp.zeros((row_count, col_count, padded.shape[2]), F32)
    for a in range(tap_size):
        same_img = (ids_pad[a : a + row_count] == ids_mid)[:, None, None]
        shifted = jnp.where(same_img, widened[a : a + row_count].astype(F32), 0.0)
        for b in range(tap_size):
            tap_index = (
                (tap_size - 1 - a) * tap_size + (tap_size - 1 - b) if flipped else a * tap_size + b
            )
            summed = summed + kernel[tap_index].astype(F32) * shifted[:, b : b + col_count]
    return summed


def tap_grads(padded, grad_low, ids_pad, ids_mid, tap_size):
    margin = tap_size // 2
    row_count = ids_mid.shape[0]
    col_count = padded.shape[1]
    widened = jnp.pad(padded, ((0, 0), (margin, margin), (0, 0)))
    grad_vals = grad_low.astype(F32)
    results = []
    for a in range(tap_size):
        same_img = (ids_pad[a : a + row_count] == ids_mid)[:, None, None]
        shifted = jnp.where(same_img, widened[a : a + row_count].astype(F32), 0.0)
        for b in range(tap_size):
            results.append(jnp.sum(shifted[:, b : b + col_count] * grad_vals, axis=(0, 1)))
    return jnp.stack(results)


def stacked_kernel(cuts, *refs):
    count = len(cuts) - 1
    step = pl.program_id(0)
    for i in range(count):

        @pl.when((step >= cuts[i]) & (step < cuts[i + 1]))
        def _(i=i):
            refs[-1][...] = dot(refs[i][...], refs[count + i][...], NN).astype(BF)


def stacked_grads(lefts, rights):
    widths = [item.shape[1] for item in rights]
    step_width = next((size for size in (512, 256) if not any(width % size for width in widths)), 0)
    if not step_width:
        return jnp.concatenate(
            [matmul_tn(left, right).astype(BF) for left, right in zip(lefts, rights)], axis=1
        )
    tokens, rows = lefts[0].shape
    cuts = [int(item) for item in np.cumsum([0] + [width // step_width for width in widths])]

    def column(i):
        return lambda step: (0, jnp.clip(step - cuts[i], 0, cuts[i + 1] - cuts[i] - 1))

    return pl.pallas_call(
        functools.partial(stacked_kernel, cuts),
        out_shape=jax.ShapeDtypeStruct((rows, sum(widths)), BF),
        grid=(cuts[-1],),
        in_specs=[pl.BlockSpec((rows, tokens), lambda step: (0, 0)) for _ in lefts]
        + [pl.BlockSpec((tokens, step_width), column(i)) for i in range(len(rights))],
        out_specs=pl.BlockSpec((rows, step_width), lambda step: (0, step)),
        **conv_params(5 * tokens * rows * sum(widths), 2 * rows * sum(widths)),
    )(*[left.T for left in lefts], *rights)


def gather_all(shard):
    full = lax.all_gather(shard, ALL, axis=0)
    return full.reshape(2, -1, shard.shape[1])


def reduce_tiles(terms):
    return lax.psum_scatter(terms, TILE, scatter_dimension=0, tiled=True)


def core_sum(terms):
    width = terms.shape[1] // 2
    core = lax.axis_index("core")
    own = lax.dynamic_slice_in_dim(terms, core * width, width, 1)
    sent = lax.dynamic_slice_in_dim(terms, (1 - core) * width, width, 1)
    got = lax.ppermute(sent, "core", SWAP)
    return (own.astype(F32) + got.astype(F32)).astype(BF)


def add_low(own, got):
    return (own.astype(F32) + got.astype(F32)).astype(BF)


def chip_step(terms, bit):
    pairs = terms.reshape(terms.shape[0] // 2, 2, *terms.shape[1:])
    side = (lax.axis_index("chip") // bit) % 2
    own = lax.dynamic_index_in_dim(pairs, side, 1, keepdims=False)
    sent = lax.dynamic_index_in_dim(pairs, 1 - side, 1, keepdims=False)
    got = lax.ppermute(sent, "chip", [(i, i ^ bit) for i in range(lax.axis_size("chip"))])
    return own, got


def all_columns(both):
    rows = both.shape[0] // 2
    core = lax.axis_index("core")
    own = lax.dynamic_slice_in_dim(both, core * rows, rows, 0)
    sent = lax.dynamic_slice_in_dim(both, (1 - core) * rows, rows, 0)
    got = lax.ppermute(sent, "core", SWAP)
    first = core == 0
    return jnp.concatenate([jnp.where(first, own, got), jnp.where(first, got, own)], axis=1)


def settle(summed, widths):
    own, sent, start = [], [], 0
    for width in widths:
        mine, other = halves(summed[:, start : start + 2 * width])
        own.append(mine)
        sent.append(other)
        start += 2 * width
    got = lax.ppermute(jnp.concatenate(sent, axis=1), "mb", SWAP)
    cuts = [int(item) for item in np.cumsum([0] + list(widths))]
    return [
        item.astype(F32) + got[:, cuts[i] : cuts[i + 1]].astype(F32) for i, item in enumerate(own)
    ]


def pair_sum(values, axis, pairs):
    low = values.astype(BF)
    return low.astype(F32) + lax.ppermute(low, axis, pairs).astype(F32)


def sum_tiles(values, bits):
    devices = tile_count()
    for bit in bits:
        values = pair_sum(values, TILE, [(i, i ^ bit) for i in range(devices)])
    return values


def together(*values):
    return lax.optimization_barrier(values)


LANES = 128
RIM = 8
VMEM_LIMIT = 60 * 1024 * 1024


def conv_params(flops=0, moved=0):
    return dict(
        compiler_params=pltpu.CompilerParams(vmem_limit_bytes=VMEM_LIMIT),
        cost_estimate=pl.CostEstimate(flops=flops, bytes_accessed=moved, transcendentals=0),
    )


def masked_taps(taps_ref, mask_ref, km_ref, sub, flip):
    for a in range(7):
        seen = mask_ref[a, pl.ds(sub * 8, 8), :]
        for b in range(7):
            tap = 48 - (a * 7 + b) if flip else a * 7 + b
            km_ref[a * 7 + b] = taps_ref[tap : tap + 1, :] * seen


def conv_kernel(place_ref, x_ref, top_ref, bot_ref, taps_ref, mask_ref, out_ref, xs_ref, km_ref):
    rows, width = 48, x_ref.shape[1] // 48
    cb = pl.program_id(0)

    @pl.when(cb == 0)
    def _():
        for w in (0, 1, 2, 51, 52, 53):
            xs_ref[w] = jnp.zeros_like(xs_ref[w])

    def fill(w, carry):
        at = pl.ds(pl.multiple_of(w * width + cb * LANES, LANES), LANES)
        xs_ref[w + 3, 0:RIM, :] = top_ref[:, at].astype(F32)
        xs_ref[w + 3, RIM : RIM + rows, :] = x_ref[:, at].astype(F32)
        xs_ref[w + 3, RIM + rows :, :] = bot_ref[:, at].astype(F32)
        return carry

    lax.fori_loop(0, 48, fill, 0)

    def band(t, carry):
        for s in range(2):
            masked_taps(taps_ref, mask_ref, km_ref.at[s], t * 2 + s, False)

        def block(i, carry):
            w0 = i * 8
            accs = []
            for s in range(2):
                acc = [jnp.zeros((8, LANES), F32) for _ in range(8)]
                for a in range(7):
                    start = t * 16 + (s * 8 + RIM - 3 + a)
                    x = [xs_ref[w0 + j, pl.ds(start, 8), :] for j in range(14)]
                    for b in range(7):
                        k = km_ref[s, a * 7 + b]
                        for j in range(8):
                            acc[j] = acc[j] + k * x[j + b]
                accs.append(acc)
            for j in range(8):
                both = jnp.concatenate([accs[0][j], accs[1][j]], axis=0).astype(BF)
                out_ref[pl.ds(pl.multiple_of((w0 + j) * rows + t * 16, 16), 16), :] = both
            return carry

        lax.fori_loop(0, 6, block, 0)
        return carry

    lax.fori_loop(0, 3, band, 0)


def conv_forward(x, top, bot, taps, mask, place, into=None):
    width = x.shape[1] // 48
    blocks = width // LANES
    whole = lambda cb, place: (0, 0)
    half = lambda cb, place: (0, place[0] * blocks + cb)
    extra = [] if into is None else [into]
    kernel = conv_kernel if into is None else conv_kernel_into
    return pl.pallas_call(
        kernel,
        out_shape=jax.ShapeDtypeStruct((48 * 48, 2 * width), BF),
        grid_spec=pltpu.PrefetchScalarGridSpec(
            num_scalar_prefetch=1,
            grid=(blocks,),
            in_specs=[
                pl.BlockSpec(x.shape, whole),
                pl.BlockSpec(top.shape, whole),
                pl.BlockSpec(bot.shape, whole),
                pl.BlockSpec((49, LANES), lambda cb, place: (0, cb)),
                pl.BlockSpec(mask.shape, lambda cb, place: (0, 0, 0)),
            ]
            + [pl.BlockSpec(memory_space=pl.ANY)] * len(extra),
            out_specs=pl.BlockSpec((48 * 48, LANES), half),
            scratch_shapes=[
                pltpu.VMEM((54, 64, LANES), F32),
                pltpu.VMEM((2, 49, 8, LANES), F32),
            ],
        ),
        input_output_aliases={} if into is None else {6: 0},
        **conv_params(54_000_000 * width, 12_000_000),
    )(place, x, top, bot, taps, mask, *extra)


def conv_kernel_into(place_ref, x_ref, top_ref, bot_ref, taps_ref, mask_ref, into_ref, *rest):
    conv_kernel(place_ref, x_ref, top_ref, bot_ref, taps_ref, mask_ref, *rest)


def back_kernel(place_ref, g_ref, top_ref, bot_ref, x_ref, cot_ref, pool_ref, taps_ref, mask_ref,
                out_ref, tap_out_ref, gs_ref, km_ref, tacc_ref, sp_ref):
    rows, width = 48, x_ref.shape[1] // 48
    cb = pl.program_id(0)

    @pl.when(cb == 0)
    def _():
        for w in (0, 1, 2, 51, 52, 53):
            gs_ref[w] = jnp.zeros_like(gs_ref[w])

    tacc_ref[...] = jnp.zeros_like(tacc_ref)

    def fill(w, carry):
        gs_ref[w + 3, 0:RIM, :] = top_ref[w].astype(F32)
        own = pl.ds(pl.multiple_of(w * rows, rows), rows)
        gs_ref[w + 3, RIM : RIM + rows, :] = g_ref[own, :].astype(F32)
        gs_ref[w + 3, RIM + rows :, :] = bot_ref[w].astype(F32)
        return carry

    lax.fori_loop(0, 48, fill, 0)

    def spread(q, carry):
        quarter = pool_ref[q] * 0.25
        sp_ref[q, pl.ds(0, 24, stride=2), :] = quarter
        sp_ref[q, pl.ds(1, 24, stride=2), :] = quarter
        return carry

    lax.fori_loop(0, 24, spread, 0)

    def band(t, carry):
        for s in range(2):
            masked_taps(taps_ref, mask_ref, km_ref.at[s], t * 2 + s, True)

        def block(i, carry):
            w0 = i * 8
            ats = [
                pl.ds(pl.multiple_of((w0 + j) * width + cb * LANES, LANES), LANES) for j in range(8)
            ]
            band_rows = pl.ds(pl.multiple_of(t * 16, 16), 16)
            vals = [x_ref[band_rows, at].astype(F32) for at in ats]
            accs = []
            for s in range(2):
                acc = [jnp.zeros((8, LANES), F32) for _ in range(8)]
                v = [val[s * 8 : s * 8 + 8] for val in vals]
                for a in range(7):
                    start = t * 16 + (s * 8 + RIM - 3 + a)
                    g = [gs_ref[w0 + j, pl.ds(start, 8), :] for j in range(14)]
                    seen = mask_ref[a, pl.ds(t * 16 + s * 8, 8), :]
                    vm = [item * seen for item in v]
                    for b in range(7):
                        k = km_ref[s, a * 7 + b]
                        tap = None
                        for j in range(8):
                            acc[j] = acc[j] + k * g[j + b]
                            term = vm[j] * g[j + b]
                            tap = term if tap is None else tap + term
                        tacc_ref[48 - (a * 7 + b)] += tap
                accs.append(acc)
            for j in range(8):
                both = jnp.concatenate([accs[0][j], accs[1][j]], axis=0)
                total = both + cot_ref[band_rows, ats[j]].astype(F32)
                total = total + sp_ref[i * 4 + j // 2, band_rows, :]
                out_ref[0, band_rows, ats[j]] = total.astype(out_ref.dtype)
            return carry

        lax.fori_loop(0, 6, block, 0)
        return carry

    lax.fori_loop(0, 3, band, 0)
    tap_out_ref[0:49, :] = jnp.sum(tacc_ref[...], axis=1)


def conv_backward(grad, top, bot, x, cot, pool, taps, mask, place, slots, kind):
    width = x.shape[1] // 48
    blocks = width // LANES
    whole = lambda cb, place: (0, 0)
    half = lambda cb, place: (0, place[0] * blocks + cb)
    return pl.pallas_call(
        back_kernel,
        out_shape=(
            jax.ShapeDtypeStruct((slots, *x.shape), kind),
            jax.ShapeDtypeStruct((56, width), F32),
        ),
        grid_spec=pltpu.PrefetchScalarGridSpec(
            num_scalar_prefetch=1,
            grid=(blocks,),
            in_specs=[
                pl.BlockSpec((48 * 48, LANES), half),
                pl.BlockSpec((48, RIM, LANES), lambda cb, place: (0, 0, place[0] * blocks + cb)),
                pl.BlockSpec((48, RIM, LANES), lambda cb, place: (0, 0, place[0] * blocks + cb)),
                pl.BlockSpec(x.shape, whole),
                pl.BlockSpec(cot.shape, whole),
                pl.BlockSpec((24, 24, LANES), lambda cb, place: (0, 0, place[0] * blocks + cb)),
                pl.BlockSpec((49, LANES), lambda cb, place: (0, cb)),
                pl.BlockSpec(mask.shape, lambda cb, place: (0, 0, 0)),
            ],
            out_specs=(
                pl.BlockSpec((1, *x.shape), lambda cb, place: (place[0] if slots == 2 else 0, 0, 0)),
                pl.BlockSpec((56, LANES), lambda cb, place: (0, cb)),
            ),
            scratch_shapes=[
                pltpu.VMEM((54, 64, LANES), F32),
                pltpu.VMEM((2, 49, 8, LANES), F32),
                pltpu.VMEM((49, 8, LANES), F32),
                pltpu.VMEM((24, 48, LANES), F32),
            ],
        ),
        **conv_params(90_000_000 * width, 25_000_000),
    )(place, grad, top, bot, x, cot, pool, taps, mask)


def join_kernel(place_ref, branch_ref, scale_ref, own_ref, other_ref, own_out, other_out, pool_out, pair_ref):
    rows, width = 48, own_ref.shape[1] // 4
    for g, (src, dst) in enumerate(((own_ref, own_out), (other_ref, other_out))):
        side = place_ref[0] if g == 0 else 1 - place_ref[0]
        at = pl.ds(pl.multiple_of(side * width, LANES), width)
        scale = scale_ref[:, at]
        for q in range(2):
            total = None
            for w in (2 * q, 2 * q + 1):
                field = src[:, w * width : (w + 1) * width].astype(F32)
                field = field + scale * branch_ref[w * rows : (w + 1) * rows, at]
                dst[0, :, w * width : (w + 1) * width] = field.astype(BF)
                total = field if total is None else total + field
            for n in range(width // LANES):
                pair_ref[q, n] = total[:, n * LANES : (n + 1) * LANES]
                even = pair_ref[q, n, pl.ds(0, 24, stride=2), :]
                odd = pair_ref[q, n, pl.ds(1, 24, stride=2), :]
                lane = pl.ds(pl.multiple_of(side * width + n * LANES, LANES), LANES)
                pool_out[q, :, lane] = (even + odd) * 0.25


def join_branch(branch, scale, own, other, place):
    width = own.shape[1] // 48
    raw = pl.BlockSpec((48, 4 * width), lambda i, place: (0, i))
    return pl.pallas_call(
        join_kernel,
        out_shape=(
            jax.ShapeDtypeStruct((2, *own.shape), BF),
            jax.ShapeDtypeStruct((1, *own.shape), BF),
            jax.ShapeDtypeStruct((24, 24, 2 * width), F32),
        ),
        grid_spec=pltpu.PrefetchScalarGridSpec(
            num_scalar_prefetch=1,
            grid=(12,),
            in_specs=[
                pl.BlockSpec((4 * 48, 2 * width), lambda i, place: (i, 0)),
                pl.BlockSpec((1, 2 * width), lambda i, place: (0, 0)),
                raw,
                raw,
            ],
            out_specs=(
                pl.BlockSpec((1, 48, 4 * width), lambda i, place: (place[0], 0, i)),
                pl.BlockSpec((1, 48, 4 * width), lambda i, place: (0, 0, i)),
                pl.BlockSpec((2, 24, 2 * width), lambda i, place: (i, 0, 0)),
            ),
            scratch_shapes=[pltpu.VMEM((2, width // LANES, 48, LANES), F32)],
        ),
        **conv_params(10_000_000, 40_000_000),
    )(place, branch, scale, own, other)


def scaled_kernel(place_ref, pool_ref, branch_ref, scale_ref, own_ref, other_ref, out_ref, sum_ref, pair_ref):
    rows, width = 48, own_ref.shape[1] // 4

    @pl.when(pl.program_id(0) == 0)
    def _():
        sum_ref[...] = jnp.zeros_like(sum_ref)

    for g, src in enumerate((own_ref, other_ref)):
        side = place_ref[0] if g == 0 else 1 - place_ref[0]
        at = pl.ds(pl.multiple_of(side * width, LANES), width)
        scale = scale_ref[:, at]
        for q in range(2):
            quarter = pool_ref[q, :, at] * 0.25
            for n in range(width // LANES):
                part = quarter[:, n * LANES : (n + 1) * LANES]
                pair_ref[q, n, pl.ds(0, 24, stride=2), :] = part
                pair_ref[q, n, pl.ds(1, 24, stride=2), :] = part
            spread = jnp.concatenate([pair_ref[q, n] for n in range(width // LANES)], axis=1)
            for w in (2 * q, 2 * q + 1):
                here = slice(w * rows, (w + 1) * rows)
                grad = src[:, w * width : (w + 1) * width].astype(F32) + spread
                part = grad * branch_ref[here, at]
                sum_ref[:, at] += jnp.sum(part.reshape(6, 8, width), axis=0)
                out_ref[here, at] = (grad * scale).astype(BF)


def scaled_grads(pool, branch, scale, own, other, place):
    width = own.shape[1] // 48
    raw = pl.BlockSpec((48, 4 * width), lambda i, place: (0, i))
    return pl.pallas_call(
        scaled_kernel,
        out_shape=(
            jax.ShapeDtypeStruct(branch.shape, BF),
            jax.ShapeDtypeStruct((8, 2 * width), F32),
        ),
        grid_spec=pltpu.PrefetchScalarGridSpec(
            num_scalar_prefetch=1,
            grid=(12,),
            in_specs=[
                pl.BlockSpec((2, 24, 2 * width), lambda i, place: (i, 0, 0)),
                pl.BlockSpec((4 * 48, 2 * width), lambda i, place: (i, 0)),
                pl.BlockSpec((1, 2 * width), lambda i, place: (0, 0)),
                raw,
                raw,
            ],
            out_specs=(
                pl.BlockSpec((4 * 48, 2 * width), lambda i, place: (i, 0)),
                pl.BlockSpec((8, 2 * width), lambda i, place: (0, 0)),
            ),
            scratch_shapes=[pltpu.VMEM((2, width // LANES, 48, LANES), F32)],
        ),
        **conv_params(10_000_000, 40_000_000),
    )(place, pool, branch, scale, own, other)


CHUNK = 256
PAIRS = 2
WIDE = PAIRS * LANES
NT = (((1,), (1,)), ((), ()))
TN = (((0,), (0,)), ((), ()))


def dot(left, right, dims):
    return lax.dot_general(left, right, dims, preferred_element_type=F32)


NN = (((1,), (0,)), ((), ()))


def lane_half(shape, side):
    lanes = lax.broadcasted_iota(jnp.int32, shape, len(shape) - 1)
    return (lanes < 64) if side == 0 else (lanes >= 64)


def fill_window(win_ref, before, own, after):
    count = own.shape[0]
    win_ref[0:count] = before[...]
    win_ref[count : 2 * count] = own[...]
    win_ref[2 * count : 3 * count] = after[...]
    win_ref[3 * count :] = jnp.zeros_like(win_ref[3 * count :])


def attend_kernel(first_ref, last_ref, q_ref, kb_ref, k_ref, ka_ref, vb_ref, v_ref, va_ref,
                  klab_ref, qlab_ref, out_ref, total_ref, kw_ref, vw_ref):
    fill_window(kw_ref, kb_ref, k_ref, ka_ref)
    fill_window(vw_ref, vb_ref, v_ref, va_ref)
    heads = [(pair, side) for pair in range(PAIRS) for side in range(2)]
    lanes = [slice(pair * LANES, (pair + 1) * LANES) for pair in range(PAIRS)]
    for n in range(3):
        rows = slice(n * 192, (n + 1) * 192)
        q = q_ref[rows, :] * jnp.asarray(0.125, BF)
        q_half = []
        for pair, side in heads:
            own = q[:, lanes[pair]]
            q_half.append(jnp.where(lane_half(own.shape, side), own, jnp.zeros_like(own)))
        q_lab = qlab_ref[n, 0:1, :]

        def chunk(c, carry):
            at = pl.ds(pl.multiple_of(c * CHUNK, CHUNK), CHUNK)
            same = klab_ref[at, 0:1] == q_lab
            new = []
            scores = [
                jnp.where(same, dot(kw_ref[at, lanes[pair]], q_half[i], NT), NEG)
                for i, (pair, side) in enumerate(heads)
            ]
            for i, (pair, side) in enumerate(heads):
                top, total, acc = carry[i]
                best = jnp.maximum(top, jnp.max(scores[i], axis=0, keepdims=True))
                p = jnp.exp(scores[i] - best)
                shrink = jnp.exp(top - best)
                total = total * shrink + jnp.sum(p, axis=0, keepdims=True)
                acc = acc * shrink + dot(vw_ref[at, lanes[pair]], p.astype(BF), TN)
                new.append((best, total, acc))
            return tuple(new)

        start = (jnp.full((1, 192), NEG, F32), jnp.zeros((1, 192), F32), jnp.zeros((LANES, 192), F32))
        done = lax.fori_loop(first_ref[n], last_ref[n], chunk, (start,) * len(heads))
        for pair in range(PAIRS):
            outs = []
            for side in range(2):
                top, total, acc = done[2 * pair + side]
                outs.append(acc * (1.0 / total))
                total_ref[pair, n, side : side + 1, :] = top + jnp.log(total)
            both = jnp.concatenate([outs[0][:64], outs[1][64:]], axis=0)
            out_ref[rows, lanes[pair]] = both.T.astype(BF)


def attend(q, k, v, around, qlab, klab, first, last):
    count, width = q.shape
    window = -(-3 * count // CHUNK) * CHUNK
    block = pl.BlockSpec((count, WIDE), lambda p, *_: (0, p))
    stats = pl.BlockSpec((PAIRS, 3, 2, 192), lambda p, *_: (p, 0, 0, 0))
    return pl.pallas_call(
        attend_kernel,
        out_shape=(
            jax.ShapeDtypeStruct(q.shape, BF),
            jax.ShapeDtypeStruct((width // LANES, 3, 2, 192), F32),
        ),
        grid_spec=pltpu.PrefetchScalarGridSpec(
            num_scalar_prefetch=2,
            grid=(width // WIDE,),
            in_specs=[block] * 7
            + [
                pl.BlockSpec(klab.shape, lambda p, *_: (0, 0)),
                pl.BlockSpec(qlab.shape, lambda p, *_: (0, 0, 0)),
            ],
            out_specs=(block, stats),
            scratch_shapes=[pltpu.VMEM((window, WIDE), BF), pltpu.VMEM((window, WIDE), BF)],
        ),
        **conv_params(40_000_000 * width, 20_000_000),
    )(first, last, q, around[0], k, around[1], around[2], v, around[3], klab, qlab)


def attend_back_kernel(first_ref, last_ref, q_ref, kb_ref, k_ref, ka_ref, vb_ref, v_ref, va_ref,
                       do_ref, o_ref, total_ref, klab_ref, qlab_ref,
                       dq_ref, dk_ref, dv_ref, before_ref, after_ref,
                       kw_ref, vw_ref, dkw_ref, dvw_ref):
    count = q_ref.shape[0]
    fill_window(kw_ref, kb_ref, k_ref, ka_ref)
    fill_window(vw_ref, vb_ref, v_ref, va_ref)
    dkw_ref[...] = jnp.zeros_like(dkw_ref)
    dvw_ref[...] = jnp.zeros_like(dvw_ref)
    heads = [(pair, side) for pair in range(PAIRS) for side in range(2)]
    lanes = [slice(pair * LANES, (pair + 1) * LANES) for pair in range(PAIRS)]
    for n in range(3):
        rows = slice(n * 192, (n + 1) * 192)
        q = q_ref[rows, :] * jnp.asarray(0.125, BF)
        do = do_ref[rows, :]
        halves = [lane_half((192, LANES), side) for side in range(2)]
        q_half = [jnp.where(halves[s], q[:, lanes[p]], jnp.zeros((), BF)) for p, s in heads]
        do_half = [jnp.where(halves[s], do[:, lanes[p]], jnp.zeros((), BF)) for p, s in heads]
        q_lab = qlab_ref[n, 0:1, :]
        flow = do.astype(F32) * o_ref[rows, :].astype(F32)
        delta = []
        for p in range(PAIRS):
            turned = flow[:, lanes[p]].T
            delta += [jnp.sum(turned[s * 64 : s * 64 + 64], axis=0, keepdims=True) for s in range(2)]

        def chunk(c, carry):
            at = pl.ds(pl.multiple_of(c * CHUNK, CHUNK), CHUNK)
            same = klab_ref[at, 0:1] == q_lab
            kcs = [kw_ref[at, lanes[pair]] for pair in range(PAIRS)]
            vcs = [vw_ref[at, lanes[pair]] for pair in range(PAIRS)]
            scores = [dot(kcs[p], q_half[i], NT) for i, (p, s) in enumerate(heads)]
            dps = [dot(vcs[p], do_half[i], NT) for i, (p, s) in enumerate(heads)]
            ps, dss = [], []
            for i, (p, s) in enumerate(heads):
                raised = jnp.where(same, scores[i] - total_ref[p, n, s : s + 1, :], NEG)
                ps.append(jnp.exp(raised))
            for i, (p, s) in enumerate(heads):
                dss.append((ps[i] * (dps[i] - delta[i])).astype(BF))
            low = [item.astype(BF) for item in ps]
            dqs = []
            for p in range(PAIRS):
                e, o = 2 * p, 2 * p + 1
                dvw_ref[at, lanes[p]] += dot(low[e], do_half[e], NN) + dot(low[o], do_half[o], NN)
                dkw_ref[at, lanes[p]] += dot(dss[e], q_half[e], NN) + dot(dss[o], q_half[o], NN)
                two = [dot(dss[e], kcs[p], TN), dot(dss[o], kcs[p], TN)]
                dqs.append(carry[p] + jnp.where(lane_half((192, LANES), 0), two[0], two[1]))
            return tuple(dqs)

        dqs = lax.fori_loop(
            first_ref[n], last_ref[n], chunk, tuple(jnp.zeros((192, LANES), F32) for _ in range(PAIRS))
        )
        for pair in range(PAIRS):
            dq_ref[rows, lanes[pair]] = (dqs[pair] * 0.125).astype(BF)
    dk_ref[...] = dkw_ref[count : 2 * count, :]
    dv_ref[...] = dvw_ref[count : 2 * count, :]
    before_ref[0] = dkw_ref[0:count, :].astype(BF)
    before_ref[1] = dvw_ref[0:count, :].astype(BF)
    after_ref[0] = dkw_ref[2 * count : 3 * count, :].astype(BF)
    after_ref[1] = dvw_ref[2 * count : 3 * count, :].astype(BF)


def attend_back(q, k, v, around, grad, out, total, qlab, klab, first, last):
    count, width = q.shape
    window = -(-3 * count // CHUNK) * CHUNK
    block = pl.BlockSpec((count, WIDE), lambda p, *_: (0, p))
    stats = pl.BlockSpec((PAIRS, 3, 2, 192), lambda p, *_: (p, 0, 0, 0))
    pair = pl.BlockSpec((2, count, WIDE), lambda p, *_: (0, 0, p))
    return pl.pallas_call(
        attend_back_kernel,
        out_shape=(
            jax.ShapeDtypeStruct(q.shape, BF),
            jax.ShapeDtypeStruct(q.shape, F32),
            jax.ShapeDtypeStruct(q.shape, F32),
            jax.ShapeDtypeStruct((2, count, width), BF),
            jax.ShapeDtypeStruct((2, count, width), BF),
        ),
        grid_spec=pltpu.PrefetchScalarGridSpec(
            num_scalar_prefetch=2,
            grid=(width // WIDE,),
            in_specs=[block] * 9
            + [
                stats,
                pl.BlockSpec(klab.shape, lambda p, *_: (0, 0)),
                pl.BlockSpec(qlab.shape, lambda p, *_: (0, 0, 0)),
            ],
            out_specs=(block, block, block, pair, pair),
            scratch_shapes=[
                pltpu.VMEM((window, WIDE), BF),
                pltpu.VMEM((window, WIDE), BF),
                pltpu.VMEM((window, WIDE), F32),
                pltpu.VMEM((window, WIDE), F32),
            ],
        ),
        **conv_params(55_000_000 * width, 20_000_000),
    )(first, last, q, around[0], k, around[1], around[2], v, around[3], grad, out, total, klab, qlab)


def on_device(
    lo_in,
    hi_in,
    image_ids,
    cn_kernel,
    cn_gain,
    cn_w1,
    cn_w2,
    cn_scale,
    ad_proj,
    ad_kernel,
    gate_w1,
    gate_w2,
    ln1_gain,
    qkv,
    out_proj,
    ln2_gain,
    fc1,
    fc2,
    d_lo_out,
    d_hi_out,
):
    micro_count, row_count, col_count, d_shard = lo_in.shape
    hi_rows = hi_in.shape[1]
    hi_cols = HCOLS
    c_shard = hi_in.shape[3] // hi_cols
    d_own, c_own = 2 * d_shard, 2 * c_shard
    tok_count = row_count * col_count
    pix_count = hi_rows * hi_cols
    mine = lax.axis_index("mb")
    row_start = lax.axis_index(TILE) * row_count
    head_count = d_own // HDIM

    fast = c_shard % LANES == 0 and lax.axis_size("tp") == 1
    hi_raw = hi_in.reshape(2, hi_rows, hi_cols * c_shard)
    hi_own, hi_other = swap_micro(hi_raw)
    up, down = rim_pair(hi_raw, RIM, 1)
    own_rims, other_rims = swap_micro(jnp.stack([up, down], axis=1))
    hid_shard, gh_shard, ff_shard = cn_w1.shape[1], gate_w1.shape[1], fc1.shape[1]
    mlp = gather_all(jnp.concatenate([cn_w1, cn_w2.T, ad_proj, gate_w1], axis=1))
    def apply(left, pair):
        return jnp.concatenate([matmul(left, pair[0]), matmul(left, pair[1])], axis=1)

    def apply_t(left, pair):
        width = pair[0].shape[1]
        return matmul_nt(left[:, :width], pair[0]) + matmul_nt(left[:, width:], pair[1])

    def cols(values):
        width = values.shape[1] // 2
        return [values[:, :width], values[:, width:]]

    canvas_ids = lax.dynamic_index_in_dim(image_ids, mine, 0, keepdims=False)
    small_ids = row_labels(canvas_ids, row_start, row_count, 1)
    lo_mid = small_ids[1 : 1 + row_count]
    hi_ids = row_labels(jnp.repeat(canvas_ids, 2), 2 * row_start, hi_rows, 3)
    hi_mid = hi_ids[3 : 3 + hi_rows]

    def both_shards(shard, axis):
        return in_order(shard, lax.ppermute(shard, "mb", SWAP), axis)

    other_kernel = lax.ppermute(cn_kernel, "mb", SWAP)
    conv_taps = in_order(cn_kernel, other_kernel, 1)

    own_place = mine.reshape(1).astype(jnp.int32)
    other_place = 1 - own_place
    seen = jnp.stack([(hi_ids[a : a + hi_rows] == hi_mid).astype(F32) for a in range(7)])
    mask = jnp.broadcast_to(seen[:, :, None], (7, hi_rows, LANES))
    own_taps, other_taps = cn_kernel.astype(F32), other_kernel.astype(F32)

    def natural(own, other):
        shape = (-1, hi_cols, c_shard)
        return in_order(own.reshape(shape), other.reshape(shape), 2)

    if fast:
        conv_flat = conv_forward(hi_own, *own_rims, own_taps, mask, own_place)
        conv_flat = conv_forward(hi_other, *other_rims, other_taps, mask, other_place, conv_flat)
    else:
        hi_field = natural(hi_own, hi_other)
        hi_pad = jnp.concatenate(
            [
                natural(own_rims[0], other_rims[0])[-3:],
                hi_field,
                natural(own_rims[1], other_rims[1])[:3],
            ]
        )
        conv_low = depthwise(hi_pad, conv_taps, hi_ids, hi_mid, 7, False).astype(BF)
        conv_flat = conv_low.transpose(1, 0, 2).reshape(pix_count, c_own)
    conv_full = features(conv_flat)
    normed, norm_pull = jax.vjp(layer_norm, conv_full.astype(F32), cn_gain.astype(F32))
    normed_low, mlp, gate_w2 = together(normed.astype(BF), mlp, gate_w2)
    mlp_in = [mlp[g, :, :hid_shard] for g in range(2)]
    mlp_out = [mlp[g, :, hid_shard : 2 * hid_shard] for g in range(2)]
    ad_matrix = [mlp[g, :, 2 * hid_shard : 2 * hid_shard + d_shard] for g in range(2)]
    gate_in = [mlp[g, :, 2 * hid_shard + d_shard :] for g in range(2)]
    vit = gather_all(
        jnp.concatenate(
            [
                gate_w2.T,
                qkv[0],
                qkv[1],
                qkv[2],
                out_proj.T,
                fc1,
                fc2.T,
            ],
            axis=1,
        )
    )
    cuts = np.cumsum([0, gh_shard, d_shard, d_shard, d_shard, d_shard, ff_shard, ff_shard])
    gate_out, q_w, k_w, v_w, out_w, ff_in, ff_out = [
        [vit[g, :, int(cuts[i]) : int(cuts[i + 1])] for g in range(2)] for i in range(7)
    ]

    inner_act, inner_slope = zip(*[gelu_pair(matmul(normed_low, mlp_in[g])) for g in range(2)])
    lo_in, d_lo_out, cn_scale, ad_kernel, first_act = together(
        lo_in, d_lo_out, cn_scale, ad_kernel, inner_act[0]
    )
    inner_act = (first_act, inner_act[1])
    lo_low = in_order(*swap_micro(lo_in.reshape(2, tok_count, d_shard)), 1)
    lo_field = lo_low.astype(F32)
    ad_taps = both_shards(ad_kernel, 1)
    hi_scale = both_shards(cn_scale, 0).astype(F32)
    branch = partial_sums(
        matmul_nt(inner_act[0], mlp_out[0]) + matmul_nt(inner_act[1], mlp_out[1])
    )
    if fast:
        hi_mine, hi_sent, pooled = join_branch(branch, hi_scale[None], hi_own, hi_other, own_place)
        pooled = pooled.transpose(1, 0, 2)
    else:
        branch_rows = branch.reshape(hi_cols, hi_rows, c_own).transpose(1, 0, 2)
        hi_sum = hi_field.astype(F32) + hi_scale * branch_rows
        pooled = jnp.mean(hi_sum.reshape(row_count, 2, col_count, 2, c_own), axis=(1, 3))
    pooled_full = features(pooled.reshape(tok_count, c_own).astype(BF))
    pooled_full, d_hi_out = together(pooled_full, d_hi_out)
    cot_own, cot_other = swap_micro(d_hi_out.reshape(2, hi_rows, hi_cols * c_shard))
    proj_low = apply(pooled_full, ad_matrix).astype(BF)
    proj_pad = rim_rows(proj_low.reshape(row_count, col_count, d_own), 1)
    local_conv = depthwise(proj_pad, ad_taps, small_ids, lo_mid, 3, False).reshape(
        tok_count, d_own
    )
    gate_hidden, gate_slope = gelu_pair(apply(pooled_full, gate_in))
    gate_val = jnp.tanh(partial_sums(apply_t(gate_hidden, gate_out)))
    mixed_one = lo_field + gate_val * local_conv
    mixed_full = features(mixed_one.astype(BF))
    norm_one, first_pull = jax.vjp(layer_norm, mixed_full.astype(F32), ln1_gain.astype(F32))
    norm_low = norm_one.astype(BF)
    key_rows = apply(norm_low, k_w).astype(BF)
    value_rows = apply(norm_low, v_w).astype(BF)
    query_in, key_rows, value_rows = together(norm_low, key_rows, value_rows)
    queries = apply(query_in, q_w).astype(BF)
    around = rim_pair(key_rows, tok_count, 0) + rim_pair(value_rows, tok_count, 0)
    near = row_labels(canvas_ids, row_start, row_count, row_count)
    key_tok = jnp.repeat(near, col_count)
    window = -(-3 * tok_count // CHUNK) * CHUNK
    key_tok = jnp.pad(key_tok, (0, window - 3 * tok_count), constant_values=-2)
    key_lab = jnp.broadcast_to(key_tok[:, None], (window, LANES))
    query_lab = jnp.broadcast_to(jnp.repeat(lo_mid, col_count).reshape(3, 1, 192), (3, 8, 192))
    edge = jnp.arange(3 * row_count)
    first_row = jnp.min(jnp.where(near[None] == lo_mid[::8][:, None], edge, 3 * row_count), axis=1)
    last_row = jnp.max(jnp.where(near[None] == lo_mid[7::8][:, None], edge, -1), axis=1) + 1
    first = (first_row * col_count // CHUNK).astype(jnp.int32)
    last = ((last_row * col_count + CHUNK - 1) // CHUNK).astype(jnp.int32)
    attended, log_total = attend(
        queries, key_rows, value_rows, around, query_lab, key_lab, first, last
    )
    mixed_two = mixed_one + partial_sums(apply_t(attended, out_w))
    if fast:
        hi_got = lax.ppermute(hi_sent, "mb", SWAP)
        mixed_two, hi_got = together(mixed_two, hi_got)
    mixed2_full = features(mixed_two.astype(BF))
    norm_two, second_pull = jax.vjp(layer_norm, mixed2_full.astype(F32), ln2_gain.astype(F32))
    norm2_low = norm_two.astype(BF)
    ff_hidden, ff_slope = gelu_pair(apply(norm2_low, ff_in))
    lo_result = (mixed_two + partial_sums(apply_t(ff_hidden, ff_out))).astype(BF)

    grad_low = in_order(*swap_micro(d_lo_out.reshape(2, tok_count, d_shard)), 1)
    grad_out = grad_low.astype(F32)
    ff_grad_full = features(grad_low)
    ff_pre_grad = (apply(ff_grad_full, ff_out) * ff_slope.astype(F32)).astype(BF)
    second_grad = partial_sums(apply_t(ff_pre_grad, ff_in)).astype(BF)
    back_two, grad_ln2 = second_pull(features(second_grad).astype(F32))
    p_ff = stacked_grads([norm2_low, ff_grad_full], [ff_pre_grad, ff_hidden])
    grad_two, cot_other = together(grad_out + own_slice(back_two), cot_other)
    att_grad_full = features(grad_two.astype(BF))
    att_grad = apply(att_grad_full, out_w).astype(BF)
    query_grad, key_own, value_own, to_before, to_after = attend_back(
        queries, key_rows, value_rows, around, att_grad, attended, log_total, query_lab, key_lab, first, last
    )
    devices = tile_count()
    steps = [(i, i + 1) for i in range(devices - 1)]
    from_before = lax.ppermute(to_after, TILE, steps)
    from_after = lax.ppermute(to_before, TILE, [(j, i) for i, j in steps])
    p_ff, from_before = together(p_ff, from_before)
    s_ff = reduce_tiles(p_ff)
    key_grad, value_grad = [
        (own + from_before[i].astype(F32) + from_after[i].astype(F32)).astype(BF)
        for i, own in enumerate((key_own, value_own))
    ]
    first_grad = partial_sums(
        apply_t(query_grad, q_w) + apply_t(key_grad, k_w) + apply_t(value_grad, v_w)
    ).astype(BF)
    back_one, grad_ln1 = first_pull(features(first_grad).astype(F32))
    grad_one = grad_two + own_slice(back_one)
    gate_pre_grad = (grad_one * local_conv * (1.0 - gate_val * gate_val)).astype(BF)
    gate_grad_full = features(gate_pre_grad)
    p_att = stacked_grads(
        [gate_grad_full, norm_low, att_grad_full],
        [gate_hidden, jnp.concatenate([query_grad, key_grad, value_grad], axis=1), attended],
    )
    hidden_grad = (apply(gate_grad_full, gate_out) * gate_slope.astype(F32)).astype(BF)
    local_grad = (grad_one * gate_val).astype(BF).reshape(row_count, col_count, d_own)
    local_pad = rim_rows(local_grad, 1)
    proj_grad = (
        depthwise(local_pad, ad_taps, small_ids, lo_mid, 3, True)
        .reshape(tok_count, d_own)
        .astype(BF)
    )
    grad_ad_kernel = tap_grads(proj_pad, local_grad, small_ids, lo_mid, 3)
    p_ad = matmul_tn(pooled_full, jnp.concatenate([proj_grad, hidden_grad], axis=1)).astype(BF)
    pooled_grad = partial_sums(apply_t(hidden_grad, gate_in) + apply_t(proj_grad, ad_matrix))
    pooled_grad, p_att, p_ad = together(pooled_grad, p_att, p_ad)
    s_att, s_ad = reduce_tiles(p_att), reduce_tiles(p_ad)
    pool_cols = pooled_grad.reshape(row_count, col_count, c_own).transpose(1, 0, 2)
    if fast:
        scaled_grad, scale_parts = scaled_grads(
            pool_cols, branch, hi_scale[None], cot_own, cot_other, own_place
        )
        grad_scale = jnp.sum(scale_parts, axis=0)
    else:
        spread_grad = jnp.repeat(jnp.repeat(pool_cols.transpose(1, 0, 2) * 0.25, 2, 0), 2, 1)
        hi_grad = natural(cot_own, cot_other).astype(F32) + spread_grad
        grad_cols = hi_grad.transpose(1, 0, 2).reshape(pix_count, c_own)
        grad_scale = jnp.sum(grad_cols * branch, axis=0)
        scaled_grad = (grad_cols * hi_scale).astype(BF)
    branch_full = lax.optimization_barrier(features(scaled_grad))
    first = mine == 0
    p_w2 = [matmul_tn(branch_full, act).astype(BF) for act in inner_act]
    branch_full, *p_w2 = together(branch_full, *p_w2)
    s_w2 = [reduce_tiles(item) for item in p_w2]
    grad_first = (matmul(branch_full, mlp_out[0]) * inner_slope[0].astype(F32)).astype(BF)
    w1_first = matmul_tn(normed_low, grad_first).astype(BF)
    branch_full, w1_first = together(branch_full, w1_first)
    core_first = core_sum(w1_first)
    grad_second = (matmul(branch_full, mlp_out[1]) * inner_slope[1].astype(F32)).astype(BF)
    w1_second = matmul_tn(normed_low, grad_second).astype(BF)
    grad_second, w1_second, s_ff = together(grad_second, w1_second, s_ff)
    core_second = core_sum(w1_second)
    normed_part = matmul_nt(grad_first, mlp_in[0])
    normed_part, core_first, core_second = together(normed_part, core_first, core_second)
    w1_own = jnp.where(first, core_first, core_second)
    w1_sent = jnp.where(first, core_second, core_first)
    piece = w1_sent.shape[1] // (3 * LANES) * LANES
    w1_got = [
        lax.ppermute(item, "mb", SWAP) for item in (w1_sent[:, :piece], w1_sent[:, piece:])
    ]
    normed_grad = partial_sums(normed_part + matmul_nt(grad_second, mlp_in[1])).astype(BF)
    normed_grad, w1_got[0] = together(normed_grad, w1_got[0])
    back_conv, grad_cn_gain = norm_pull(features(normed_grad).astype(F32))
    conv_grad = own_slice(back_conv).astype(BF)
    conv_cols = conv_grad.reshape(hi_cols, hi_rows, c_own)
    grad_up, grad_down = rim_pair(conv_cols, RIM, 1)
    if fast:
        ghi_sent, taps_other = conv_backward(
            conv_grad, grad_up, grad_down, hi_other, cot_other, pool_cols, other_taps, mask, other_place, 1, BF
        )
        conv_grad, ghi_sent, w1_got[1] = together(conv_grad, ghi_sent, w1_got[1])
        w1_sum = add_low(w1_own, jnp.concatenate(w1_got, axis=1))
        ghi_mine, taps_own = conv_backward(
            conv_grad, grad_up, grad_down, hi_own, cot_own, pool_cols, own_taps, mask, own_place, 2, F32
        )
        tap_sums = jnp.concatenate([taps_own, taps_other])
    else:
        conv_grad = conv_cols.transpose(1, 0, 2)
        conv_pad = jnp.concatenate(
            [grad_up.transpose(1, 0, 2)[-3:], conv_grad, grad_down.transpose(1, 0, 2)[:3]]
        )
        hi_back = hi_grad + depthwise(conv_pad, conv_taps, hi_ids, hi_mid, 7, True)
        grad_cn_kernel = tap_grads(hi_pad, conv_grad, hi_ids, hi_mid, 7)
        tap_sums = jnp.concatenate(halves(grad_cn_kernel))
        w1_sum = add_low(w1_own, jnp.concatenate(w1_got, axis=1))

    chips = lax.axis_size("chip")
    w1_sum = w1_sum.reshape(chips, w1_sum.shape[0] // chips, w1_sum.shape[1])
    if chips & (chips - 1):
        w1_sum = lax.psum_scatter(w1_sum, "chip", scatter_dimension=0, tiled=True)
    else:
        own, got = chip_step(w1_sum, 1)
        tap_sums, got, s_att, s_ad = together(tap_sums, got, s_att, s_ad)
        w1_sum, bit = add_low(own, got), 2
        while bit < chips:
            w1_sum, bit = add_low(*chip_step(w1_sum, bit)), 2 * bit

    own_terms, sent_terms = zip(*[halves(item) for item in (grad_scale, grad_ad_kernel)])
    others = (*own_terms, *sent_terms, grad_cn_gain, grad_ln1, grad_ln2)
    sizes = [int(item) for item in np.cumsum([0] + [item.size for item in others])]
    flat = jnp.concatenate([item.reshape(-1) for item in others])
    flat = jnp.pad(flat, (0, -sizes[-1] % (8 * c_shard))).reshape(-1, c_shard)
    tap_rows = tap_sums.shape[0] // 2
    small = jnp.concatenate([tap_sums, flat])
    devices = tile_count()
    bits = [1 << i for i in range(devices.bit_length() - 1)]
    doubling = devices == 1 << len(bits)
    small = sum_tiles(small, bits[:1]) if doubling else lax.psum(small, TILE)
    if fast:
        ghi_got = lax.ppermute(ghi_sent, "mb", SWAP)
        small, ghi_got, *s_w2 = together(small, ghi_got, *s_w2)
    if doubling:
        small = sum_tiles(small, bits[1:])
    got = lax.ppermute(small[tap_rows:], "mb", SWAP)
    g_kernel = (small[:tap_rows] + got[:tap_rows])[: cn_kernel.shape[0]]
    flat, got = small[2 * tap_rows :].reshape(-1), got[tap_rows:].reshape(-1)
    pieces = [
        (flat[sizes[i] : sizes[i + 1]] + got[sizes[j] : sizes[j + 1]]).reshape(others[i].shape)
        for i, j in ((0, 2), (1, 3), (4, 4), (5, 5), (6, 6))
    ]
    g_scale, g_taps, *gain_sums = pieces

    def leave(values, kind):
        own, sent = halves(values)
        other = lax.ppermute(sent.astype(BF), "mb", SWAP)
        return both_micro(own.astype(kind), other.astype(kind))

    lo_stack = leave(lo_result.reshape(row_count, col_count, d_own), BF)
    if fast:
        hi_stack, ghi_stack = [
            lax.dynamic_update_slice_in_dim(stack, got.astype(stack.dtype), 1 - mine, 0)
            for stack, got in ((hi_mine, hi_got), (ghi_mine, ghi_got))
        ]
    else:
        hi_stack = leave(hi_sum, BF)
        ghi_stack = leave(hi_back, F32)
    glo_stack = leave(grad_one.reshape(row_count, col_count, d_own), F32)

    (g_w2,) = settle(jnp.concatenate(s_w2, axis=1), (hid_shard,))
    hi_stack = hi_stack.reshape(2, hi_rows, 1, hi_cols * c_shard)
    ghi_stack, w1_sum = together(ghi_stack.reshape(2, hi_rows, -1, 128), w1_sum)
    ghi_stack = ghi_stack.reshape(2, hi_rows, 1, hi_cols * c_shard)
    g_w1 = all_columns(w1_sum.reshape(-1, w1_sum.shape[-1])).astype(F32)
    g_fc1, g_fc2 = settle(s_ff, (ff_shard, ff_shard))
    g_gate_w2, g_q, g_k, g_v, g_out = settle(s_att, (gh_shard, d_shard, d_shard, d_shard, d_shard))
    g_ad, g_gate_w1 = settle(s_ad, (d_shard, gh_shard))

    return (
        lo_stack,
        hi_stack,
        glo_stack,
        ghi_stack,
        g_kernel,
        gain_sums[0],
        g_w1,
        g_w2.T,
        g_scale,
        g_ad,
        g_taps,
        g_gate_w1,
        g_gate_w2.T,
        gain_sums[1],
        jnp.stack([g_q, g_k, g_v]),
        g_out.T,
        gain_sums[2],
        g_fc1,
        g_fc2.T,
    )


def solution(mesh):
    tiles, mps = mesh.shape["tile"], mesh.shape["mp"]
    fine = Mesh(mesh.devices.reshape(tiles // 2, 2, 2, mps // 2), (*TILE, "mb", "tp"))
    mp = ("mb", "tp")
    in_specs = (
        P(None, TILE, None, mp),
        P(None, TILE, mp, None),
        P(),
        P(None, mp),
        P(),
        P(TILE, mp),
        P(mp, TILE),
        P(mp),
        P(TILE, mp),
        P(None, mp),
        P(TILE, mp),
        P(mp, TILE),
        P(),
        P(None, TILE, mp),
        P(mp, TILE),
        P(),
        P(TILE, mp),
        P(mp, TILE),
        P(None, TILE, None, mp),
        P(None, TILE, mp, None),
    )
    out_specs = (
        P(None, TILE, None, mp),
        P(None, TILE, mp, None),
        P(None, TILE, None, mp),
        P(None, TILE, mp, None),
        P(None, mp),
        P(),
        P(TILE, mp),
        P(mp, TILE),
        P(mp),
        P(TILE, mp),
        P(None, mp),
        P(TILE, mp),
        P(mp, TILE),
        P(),
        P(None, TILE, mp),
        P(mp, TILE),
        P(),
        P(TILE, mp),
        P(mp, TILE),
    )
    return jax.shard_map(
        on_device, mesh=fine, in_specs=in_specs, out_specs=out_specs, check_vma=False
    )
```

```python
import functools

import jax
import jax.numpy as jnp
import numpy as np
from jax import lax
from jax.experimental import pallas as pl
from jax.experimental.pallas import tpu as pltpu
from jax.sharding import Mesh
from jax.sharding import PartitionSpec as P

HDIM = 64
IMG_ROWS = 24
HCOLS = 48

EPS = 1e-06
NEG = -1e30
BF = jnp.bfloat16
F32 = jnp.float32
TILE = ("chip", "core")
ALL = ("mb", *TILE)


def tile_count():
    return lax.axis_size("chip") * lax.axis_size("core")


def rim_pair(value, width, axis):
    devices, length = tile_count(), value.shape[axis]
    up = [(i, (i + 1) % devices) for i in range(devices - 1)]
    down = [(j, i) for i, j in up]
    before = lax.ppermute(lax.slice_in_dim(value, length - width, length, axis=axis), TILE, up)
    after = lax.ppermute(lax.slice_in_dim(value, 0, width, axis=axis), TILE, down)
    return before, after


def rim_rows(value, width):
    devices, length = tile_count(), value.shape[0]
    up = [(i, (i + 1) % devices) for i in range(devices - 1)]
    down = [(j, i) for i, j in up]
    before = lax.ppermute(value[length - width :], TILE, up)
    after = lax.ppermute(value[:width], TILE, down)
    return jnp.concatenate([before, value, after], axis=0)


def matmul(left, right):
    return jnp.dot(left, right, preferred_element_type=F32)


def matmul_tn(left, right):
    return lax.dot_general(left, right, (((0,), (0,)), ((), ())), preferred_element_type=F32)


def matmul_nt(left, right):
    return lax.dot_general(left, right, (((1,), (1,)), ((), ())), preferred_element_type=F32)


def layer_norm(values, gain_vec):
    average = jnp.mean(values, axis=-1, keepdims=True)
    centered = values - average
    variance = jnp.mean(centered * centered, axis=-1, keepdims=True)
    return centered * lax.rsqrt(variance + EPS) * gain_vec


def gelu_pair(values):
    cdf = 0.5 + 0.5 * lax.erf(values * 0.7071067811865476)
    slope = cdf + values * (0.3989422804014327 * jnp.exp(-0.5 * values * values))
    return (values * cdf).astype(BF), slope.astype(BF)


def features(values):
    parts = lax.axis_size("tp")
    if parts == 1:
        return values
    rows, width = values.shape
    full = lax.all_gather(values.reshape(rows, 2, width // 2), "tp", axis=2)
    return full.reshape(rows, parts * width)


def partial_sums(values):
    parts = lax.axis_size("tp")
    if parts == 1:
        return values
    rows, width = values.shape
    split = values.reshape(rows, 2, parts, width // (2 * parts))
    return lax.psum_scatter(split, "tp", scatter_dimension=2).reshape(rows, width // parts)


def own_slice(values):
    parts = lax.axis_size("tp")
    if parts == 1:
        return values
    rows, width = values.shape
    split = values.reshape(rows, 2, parts, width // (2 * parts))
    own = lax.dynamic_index_in_dim(split, lax.axis_index("tp"), 2, keepdims=False)
    return own.reshape(rows, width // parts)


SWAP = [(0, 1), (1, 0)]


def swap_micro(values):
    mine = lax.axis_index("mb")
    own = lax.dynamic_index_in_dim(values, mine, 0, keepdims=False)
    sent = lax.dynamic_index_in_dim(values, 1 - mine, 0, keepdims=False)
    return own, lax.ppermute(sent, "mb", SWAP)


def in_order(own, other, axis):
    first = lax.axis_index("mb") == 0
    return jnp.concatenate(
        [jnp.where(first, own, other), jnp.where(first, other, own)], axis=axis
    )


def both_micro(own, other):
    first = lax.axis_index("mb") == 0
    return jnp.stack([jnp.where(first, own, other), jnp.where(first, other, own)])


def halves(values):
    width = values.shape[-1] // 2
    mine = lax.axis_index("mb")
    own = lax.dynamic_slice_in_dim(values, mine * width, width, values.ndim - 1)
    sent = lax.dynamic_slice_in_dim(values, (1 - mine) * width, width, values.ndim - 1)
    return own, sent


def row_labels(labels, first_row, count_rows, margin):
    padded = jnp.pad(labels, (margin, margin), constant_values=-1)
    return lax.dynamic_slice_in_dim(padded, first_row, count_rows + 2 * margin, 0)


def depthwise(padded, kernel, ids_pad, ids_mid, tap_size, flipped):
    margin = tap_size // 2
    row_count = ids_mid.shape[0]
    col_count = padded.shape[1]
    widened = jnp.pad(padded, ((0, 0), (margin, margin), (0, 0)))
    summed = jnp.zeros((row_count, col_count, padded.shape[2]), F32)
    for a in range(tap_size):
        same_img = (ids_pad[a : a + row_count] == ids_mid)[:, None, None]
        shifted = jnp.where(same_img, widened[a : a + row_count].astype(F32), 0.0)
        for b in range(tap_size):
            tap_index = (
                (tap_size - 1 - a) * tap_size + (tap_size - 1 - b) if flipped else a * tap_size + b
            )
            summed = summed + kernel[tap_index].astype(F32) * shifted[:, b : b + col_count]
    return summed


def tap_grads(padded, grad_low, ids_pad, ids_mid, tap_size):
    margin = tap_size // 2
    row_count = ids_mid.shape[0]
    col_count = padded.shape[1]
    widened = jnp.pad(padded, ((0, 0), (margin, margin), (0, 0)))
    grad_vals = grad_low.astype(F32)
    results = []
    for a in range(tap_size):
        same_img = (ids_pad[a : a + row_count] == ids_mid)[:, None, None]
        shifted = jnp.where(same_img, widened[a : a + row_count].astype(F32), 0.0)
        for b in range(tap_size):
            results.append(jnp.sum(shifted[:, b : b + col_count] * grad_vals, axis=(0, 1)))
    return jnp.stack(results)


def stacked_kernel(cuts, *refs):
    count = len(cuts) - 1
    step = pl.program_id(0)
    for i in range(count):

        @pl.when((step >= cuts[i]) & (step < cuts[i + 1]))
        def _(i=i):
            refs[-1][...] = dot(refs[i][...], refs[count + i][...], NN).astype(BF)


def stacked_grads(lefts, rights):
    widths = [item.shape[1] for item in rights]
    step_width = next((size for size in (512, 256) if not any(width % size for width in widths)), 0)
    if not step_width:
        return jnp.concatenate(
            [matmul_tn(left, right).astype(BF) for left, right in zip(lefts, rights)], axis=1
        )
    tokens, rows = lefts[0].shape
    cuts = [int(item) for item in np.cumsum([0] + [width // step_width for width in widths])]

    def column(i):
        return lambda step: (0, jnp.clip(step - cuts[i], 0, cuts[i + 1] - cuts[i] - 1))

    return pl.pallas_call(
        functools.partial(stacked_kernel, cuts),
        out_shape=jax.ShapeDtypeStruct((rows, sum(widths)), BF),
        grid=(cuts[-1],),
        in_specs=[pl.BlockSpec((rows, tokens), lambda step: (0, 0)) for _ in lefts]
        + [pl.BlockSpec((tokens, step_width), column(i)) for i in range(len(rights))],
        out_specs=pl.BlockSpec((rows, step_width), lambda step: (0, step)),
        **conv_params(5 * tokens * rows * sum(widths), 2 * rows * sum(widths)),
    )(*[left.T for left in lefts], *rights)


def gather_all(shard):
    full = lax.all_gather(shard, ALL, axis=0)
    return full.reshape(2, -1, shard.shape[1])


def reduce_tiles(terms):
    return lax.psum_scatter(terms, TILE, scatter_dimension=0, tiled=True)


def core_sum(terms):
    width = terms.shape[1] // 2
    core = lax.axis_index("core")
    own = lax.dynamic_slice_in_dim(terms, core * width, width, 1)
    sent = lax.dynamic_slice_in_dim(terms, (1 - core) * width, width, 1)
    got = lax.ppermute(sent, "core", SWAP)
    return (own.astype(F32) + got.astype(F32)).astype(BF)


def add_low(own, got):
    return (own.astype(F32) + got.astype(F32)).astype(BF)


def chip_step(terms, bit):
    pairs = terms.reshape(terms.shape[0] // 2, 2, *terms.shape[1:])
    side = (lax.axis_index("chip") // bit) % 2
    own = lax.dynamic_index_in_dim(pairs, side, 1, keepdims=False)
    sent = lax.dynamic_index_in_dim(pairs, 1 - side, 1, keepdims=False)
    got = lax.ppermute(sent, "chip", [(i, i ^ bit) for i in range(lax.axis_size("chip"))])
    return own, got


def all_columns(both):
    rows = both.shape[0] // 2
    core = lax.axis_index("core")
    own = lax.dynamic_slice_in_dim(both, core * rows, rows, 0)
    sent = lax.dynamic_slice_in_dim(both, (1 - core) * rows, rows, 0)
    got = lax.ppermute(sent, "core", SWAP)
    first = core == 0
    return jnp.concatenate([jnp.where(first, own, got), jnp.where(first, got, own)], axis=1)


def settle(summed, widths):
    own, sent, start = [], [], 0
    for width in widths:
        mine, other = halves(summed[:, start : start + 2 * width])
        own.append(mine)
        sent.append(other)
        start += 2 * width
    got = lax.ppermute(jnp.concatenate(sent, axis=1), "mb", SWAP)
    cuts = [int(item) for item in np.cumsum([0] + list(widths))]
    return [
        item.astype(F32) + got[:, cuts[i] : cuts[i + 1]].astype(F32) for i, item in enumerate(own)
    ]


def pair_sum(values, axis, pairs):
    low = values.astype(BF)
    return low.astype(F32) + lax.ppermute(low, axis, pairs).astype(F32)


def sum_tiles(values, bits):
    devices = tile_count()
    for bit in bits:
        values = pair_sum(values, TILE, [(i, i ^ bit) for i in range(devices)])
    return values


def together(*values):
    return lax.optimization_barrier(values)


LANES = 128
RIM = 8
VMEM_LIMIT = 60 * 1024 * 1024


def conv_params(flops=0, moved=0):
    return dict(
        compiler_params=pltpu.CompilerParams(vmem_limit_bytes=VMEM_LIMIT),
        cost_estimate=pl.CostEstimate(flops=flops, bytes_accessed=moved, transcendentals=0),
    )


def masked_taps(taps_ref, mask_ref, km_ref, sub, flip):
    for a in range(7):
        seen = mask_ref[a, pl.ds(sub * 8, 8), :]
        for b in range(7):
            tap = 48 - (a * 7 + b) if flip else a * 7 + b
            km_ref[a * 7 + b] = taps_ref[tap : tap + 1, :] * seen


def conv_kernel(place_ref, x_ref, top_ref, bot_ref, taps_ref, mask_ref, out_ref, xs_ref, km_ref):
    rows, width = 48, x_ref.shape[1] // 48
    cb = pl.program_id(0)

    @pl.when(cb == 0)
    def _():
        for w in (0, 1, 2, 51, 52, 53):
            xs_ref[w] = jnp.zeros_like(xs_ref[w])

    def fill(w, carry):
        at = pl.ds(pl.multiple_of(w * width + cb * LANES, LANES), LANES)
        xs_ref[w + 3, 0:RIM, :] = top_ref[:, at].astype(F32)
        xs_ref[w + 3, RIM : RIM + rows, :] = x_ref[:, at].astype(F32)
        xs_ref[w + 3, RIM + rows :, :] = bot_ref[:, at].astype(F32)
        return carry

    lax.fori_loop(0, 48, fill, 0)

    def band(t, carry):
        for s in range(2):
            masked_taps(taps_ref, mask_ref, km_ref.at[s], t * 2 + s, False)

        def block(i, carry):
            w0 = i * 8
            accs = []
            for s in range(2):
                acc = [jnp.zeros((8, LANES), F32) for _ in range(8)]
                for a in range(7):
                    start = t * 16 + (s * 8 + RIM - 3 + a)
                    x = [xs_ref[w0 + j, pl.ds(start, 8), :] for j in range(14)]
                    for b in range(7):
                        k = km_ref[s, a * 7 + b]
                        for j in range(8):
                            acc[j] = acc[j] + k * x[j + b]
                accs.append(acc)
            for j in range(8):
                both = jnp.concatenate([accs[0][j], accs[1][j]], axis=0).astype(BF)
                out_ref[pl.ds(pl.multiple_of((w0 + j) * rows + t * 16, 16), 16), :] = both
            return carry

        lax.fori_loop(0, 6, block, 0)
        return carry

    lax.fori_loop(0, 3, band, 0)


def conv_forward(x, top, bot, taps, mask, place, into=None):
    width = x.shape[1] // 48
    blocks = width // LANES
    whole = lambda cb, place: (0, 0)
    half = lambda cb, place: (0, place[0] * blocks + cb)
    extra = [] if into is None else [into]
    kernel = conv_kernel if into is None else conv_kernel_into
    return pl.pallas_call(
        kernel,
        out_shape=jax.ShapeDtypeStruct((48 * 48, 2 * width), BF),
        grid_spec=pltpu.PrefetchScalarGridSpec(
            num_scalar_prefetch=1,
            grid=(blocks,),
            in_specs=[
                pl.BlockSpec(x.shape, whole),
                pl.BlockSpec(top.shape, whole),
                pl.BlockSpec(bot.shape, whole),
                pl.BlockSpec((49, LANES), lambda cb, place: (0, cb)),
                pl.BlockSpec(mask.shape, lambda cb, place: (0, 0, 0)),
            ]
            + [pl.BlockSpec(memory_space=pl.ANY)] * len(extra),
            out_specs=pl.BlockSpec((48 * 48, LANES), half),
            scratch_shapes=[
                pltpu.VMEM((54, 64, LANES), F32),
                pltpu.VMEM((2, 49, 8, LANES), F32),
            ],
        ),
        input_output_aliases={} if into is None else {6: 0},
        **conv_params(54_000_000 * width, 12_000_000),
    )(place, x, top, bot, taps, mask, *extra)


def conv_kernel_into(place_ref, x_ref, top_ref, bot_ref, taps_ref, mask_ref, into_ref, *rest):
    conv_kernel(place_ref, x_ref, top_ref, bot_ref, taps_ref, mask_ref, *rest)


def back_kernel(place_ref, g_ref, top_ref, bot_ref, x_ref, cot_ref, pool_ref, taps_ref, mask_ref,
                out_ref, tap_out_ref, gs_ref, km_ref, tacc_ref, sp_ref):
    rows, width = 48, x_ref.shape[1] // 48
    cb = pl.program_id(0)

    @pl.when(cb == 0)
    def _():
        for w in (0, 1, 2, 51, 52, 53):
            gs_ref[w] = jnp.zeros_like(gs_ref[w])

    tacc_ref[...] = jnp.zeros_like(tacc_ref)

    def fill(w, carry):
        gs_ref[w + 3, 0:RIM, :] = top_ref[w].astype(F32)
        own = pl.ds(pl.multiple_of(w * rows, rows), rows)
        gs_ref[w + 3, RIM : RIM + rows, :] = g_ref[own, :].astype(F32)
        gs_ref[w + 3, RIM + rows :, :] = bot_ref[w].astype(F32)
        return carry

    lax.fori_loop(0, 48, fill, 0)

    def spread(q, carry):
        quarter = pool_ref[q] * 0.25
        sp_ref[q, pl.ds(0, 24, stride=2), :] = quarter
        sp_ref[q, pl.ds(1, 24, stride=2), :] = quarter
        return carry

    lax.fori_loop(0, 24, spread, 0)

    def band(t, carry):
        for s in range(2):
            masked_taps(taps_ref, mask_ref, km_ref.at[s], t * 2 + s, True)

        def block(i, carry):
            w0 = i * 8
            ats = [
                pl.ds(pl.multiple_of((w0 + j) * width + cb * LANES, LANES), LANES) for j in range(8)
            ]
            band_rows = pl.ds(pl.multiple_of(t * 16, 16), 16)
            vals = [x_ref[band_rows, at].astype(F32) for at in ats]
            accs = []
            for s in range(2):
                acc = [jnp.zeros((8, LANES), F32) for _ in range(8)]
                v = [val[s * 8 : s * 8 + 8] for val in vals]
                for a in range(7):
                    start = t * 16 + (s * 8 + RIM - 3 + a)
                    g = [gs_ref[w0 + j, pl.ds(start, 8), :] for j in range(14)]
                    seen = mask_ref[a, pl.ds(t * 16 + s * 8, 8), :]
                    vm = [item * seen for item in v]
                    for b in range(7):
                        k = km_ref[s, a * 7 + b]
                        tap = None
                        for j in range(8):
                            acc[j] = acc[j] + k * g[j + b]
                            term = vm[j] * g[j + b]
                            tap = term if tap is None else tap + term
                        tacc_ref[48 - (a * 7 + b)] += tap
                accs.append(acc)
            for j in range(8):
                both = jnp.concatenate([accs[0][j], accs[1][j]], axis=0)
                total = both + cot_ref[band_rows, ats[j]].astype(F32)
                total = total + sp_ref[i * 4 + j // 2, band_rows, :]
                out_ref[0, band_rows, ats[j]] = total.astype(out_ref.dtype)
            return carry

        lax.fori_loop(0, 6, block, 0)
        return carry

    lax.fori_loop(0, 3, band, 0)
    tap_out_ref[0:49, :] = jnp.sum(tacc_ref[...], axis=1)


def conv_backward(grad, top, bot, x, cot, pool, taps, mask, place, slots, kind):
    width = x.shape[1] // 48
    blocks = width // LANES
    whole = lambda cb, place: (0, 0)
    half = lambda cb, place: (0, place[0] * blocks + cb)
    return pl.pallas_call(
        back_kernel,
        out_shape=(
            jax.ShapeDtypeStruct((slots, *x.shape), kind),
            jax.ShapeDtypeStruct((56, width), F32),
        ),
        grid_spec=pltpu.PrefetchScalarGridSpec(
            num_scalar_prefetch=1,
            grid=(blocks,),
            in_specs=[
                pl.BlockSpec((48 * 48, LANES), half),
                pl.BlockSpec((48, RIM, LANES), lambda cb, place: (0, 0, place[0] * blocks + cb)),
                pl.BlockSpec((48, RIM, LANES), lambda cb, place: (0, 0, place[0] * blocks + cb)),
                pl.BlockSpec(x.shape, whole),
                pl.BlockSpec(cot.shape, whole),
                pl.BlockSpec((24, 24, LANES), lambda cb, place: (0, 0, place[0] * blocks + cb)),
                pl.BlockSpec((49, LANES), lambda cb, place: (0, cb)),
                pl.BlockSpec(mask.shape, lambda cb, place: (0, 0, 0)),
            ],
            out_specs=(
                pl.BlockSpec((1, *x.shape), lambda cb, place: (place[0] if slots == 2 else 0, 0, 0)),
                pl.BlockSpec((56, LANES), lambda cb, place: (0, cb)),
            ),
            scratch_shapes=[
                pltpu.VMEM((54, 64, LANES), F32),
                pltpu.VMEM((2, 49, 8, LANES), F32),
                pltpu.VMEM((49, 8, LANES), F32),
                pltpu.VMEM((24, 48, LANES), F32),
            ],
        ),
        **conv_params(90_000_000 * width, 25_000_000),
    )(place, grad, top, bot, x, cot, pool, taps, mask)


def join_kernel(place_ref, branch_ref, scale_ref, own_ref, other_ref, own_out, other_out, pool_out, pair_ref):
    rows, width = 48, own_ref.shape[1] // 4
    for g, (src, dst) in enumerate(((own_ref, own_out), (other_ref, other_out))):
        side = place_ref[0] if g == 0 else 1 - place_ref[0]
        at = pl.ds(pl.multiple_of(side * width, LANES), width)
        scale = scale_ref[:, at]
        for q in range(2):
            total = None
            for w in (2 * q, 2 * q + 1):
                field = src[:, w * width : (w + 1) * width].astype(F32)
                field = field + scale * branch_ref[w * rows : (w + 1) * rows, at]
                dst[0, :, w * width : (w + 1) * width] = field.astype(BF)
                total = field if total is None else total + field
            for n in range(width // LANES):
                pair_ref[q, n] = total[:, n * LANES : (n + 1) * LANES]
                even = pair_ref[q, n, pl.ds(0, 24, stride=2), :]
                odd = pair_ref[q, n, pl.ds(1, 24, stride=2), :]
                lane = pl.ds(pl.multiple_of(side * width + n * LANES, LANES), LANES)
                pool_out[q, :, lane] = (even + odd) * 0.25


def join_branch(branch, scale, own, other, place):
    width = own.shape[1] // 48
    raw = pl.BlockSpec((48, 4 * width), lambda i, place: (0, i))
    return pl.pallas_call(
        join_kernel,
        out_shape=(
            jax.ShapeDtypeStruct((2, *own.shape), BF),
            jax.ShapeDtypeStruct((1, *own.shape), BF),
            jax.ShapeDtypeStruct((24, 24, 2 * width), F32),
        ),
        grid_spec=pltpu.PrefetchScalarGridSpec(
            num_scalar_prefetch=1,
            grid=(12,),
            in_specs=[
                pl.BlockSpec((4 * 48, 2 * width), lambda i, place: (i, 0)),
                pl.BlockSpec((1, 2 * width), lambda i, place: (0, 0)),
                raw,
                raw,
            ],
            out_specs=(
                pl.BlockSpec((1, 48, 4 * width), lambda i, place: (place[0], 0, i)),
                pl.BlockSpec((1, 48, 4 * width), lambda i, place: (0, 0, i)),
                pl.BlockSpec((2, 24, 2 * width), lambda i, place: (i, 0, 0)),
            ),
            scratch_shapes=[pltpu.VMEM((2, width // LANES, 48, LANES), F32)],
        ),
        **conv_params(10_000_000, 40_000_000),
    )(place, branch, scale, own, other)


def scaled_kernel(place_ref, pool_ref, branch_ref, scale_ref, own_ref, other_ref, out_ref, sum_ref, pair_ref):
    rows, width = 48, own_ref.shape[1] // 4

    @pl.when(pl.program_id(0) == 0)
    def _():
        sum_ref[...] = jnp.zeros_like(sum_ref)

    for g, src in enumerate((own_ref, other_ref)):
        side = place_ref[0] if g == 0 else 1 - place_ref[0]
        at = pl.ds(pl.multiple_of(side * width, LANES), width)
        scale = scale_ref[:, at]
        for q in range(2):
            quarter = pool_ref[q, :, at] * 0.25
            for n in range(width // LANES):
                part = quarter[:, n * LANES : (n + 1) * LANES]
                pair_ref[q, n, pl.ds(0, 24, stride=2), :] = part
                pair_ref[q, n, pl.ds(1, 24, stride=2), :] = part
            spread = jnp.concatenate([pair_ref[q, n] for n in range(width // LANES)], axis=1)
            for w in (2 * q, 2 * q + 1):
                here = slice(w * rows, (w + 1) * rows)
                grad = src[:, w * width : (w + 1) * width].astype(F32) + spread
                part = grad * branch_ref[here, at]
                sum_ref[:, at] += jnp.sum(part.reshape(6, 8, width), axis=0)
                out_ref[here, at] = (grad * scale).astype(BF)


def scaled_grads(pool, branch, scale, own, other, place):
    width = own.shape[1] // 48
    raw = pl.BlockSpec((48, 4 * width), lambda i, place: (0, i))
    return pl.pallas_call(
        scaled_kernel,
        out_shape=(
            jax.ShapeDtypeStruct(branch.shape, BF),
            jax.ShapeDtypeStruct((8, 2 * width), F32),
        ),
        grid_spec=pltpu.PrefetchScalarGridSpec(
            num_scalar_prefetch=1,
            grid=(12,),
            in_specs=[
                pl.BlockSpec((2, 24, 2 * width), lambda i, place: (i, 0, 0)),
                pl.BlockSpec((4 * 48, 2 * width), lambda i, place: (i, 0)),
                pl.BlockSpec((1, 2 * width), lambda i, place: (0, 0)),
                raw,
                raw,
            ],
            out_specs=(
                pl.BlockSpec((4 * 48, 2 * width), lambda i, place: (i, 0)),
                pl.BlockSpec((8, 2 * width), lambda i, place: (0, 0)),
            ),
            scratch_shapes=[pltpu.VMEM((2, width // LANES, 48, LANES), F32)],
        ),
        **conv_params(10_000_000, 40_000_000),
    )(place, pool, branch, scale, own, other)


CHUNK = 256
PAIRS = 2
WIDE = PAIRS * LANES
NT = (((1,), (1,)), ((), ()))
TN = (((0,), (0,)), ((), ()))


def dot(left, right, dims):
    return lax.dot_general(left, right, dims, preferred_element_type=F32)


NN = (((1,), (0,)), ((), ()))


def lane_half(shape, side):
    lanes = lax.broadcasted_iota(jnp.int32, shape, len(shape) - 1)
    return (lanes < 64) if side == 0 else (lanes >= 64)


def fill_window(win_ref, before, own, after):
    count = own.shape[0]
    win_ref[0:count] = before[...]
    win_ref[count : 2 * count] = own[...]
    win_ref[2 * count : 3 * count] = after[...]
    win_ref[3 * count :] = jnp.zeros_like(win_ref[3 * count :])


def attend_kernel(first_ref, last_ref, q_ref, kb_ref, k_ref, ka_ref, vb_ref, v_ref, va_ref,
                  klab_ref, qlab_ref, out_ref, total_ref, kw_ref, vw_ref):
    fill_window(kw_ref, kb_ref, k_ref, ka_ref)
    fill_window(vw_ref, vb_ref, v_ref, va_ref)
    heads = [(pair, side) for pair in range(PAIRS) for side in range(2)]
    lanes = [slice(pair * LANES, (pair + 1) * LANES) for pair in range(PAIRS)]
    for n in range(3):
        rows = slice(n * 192, (n + 1) * 192)
        q = q_ref[rows, :] * jnp.asarray(0.125, BF)
        q_half = []
        for pair, side in heads:
            own = q[:, lanes[pair]]
            q_half.append(jnp.where(lane_half(own.shape, side), own, jnp.zeros_like(own)))
        q_lab = qlab_ref[n, 0:1, :]

        def chunk(c, carry):
            at = pl.ds(pl.multiple_of(c * CHUNK, CHUNK), CHUNK)
            same = klab_ref[at, 0:1] == q_lab
            new = []
            scores = [
                jnp.where(same, dot(kw_ref[at, lanes[pair]], q_half[i], NT), NEG)
                for i, (pair, side) in enumerate(heads)
            ]
            for i, (pair, side) in enumerate(heads):
                top, total, acc = carry[i]
                best = jnp.maximum(top, jnp.max(scores[i], axis=0, keepdims=True))
                p = jnp.exp(scores[i] - best)
                shrink = jnp.exp(top - best)
                total = total * shrink + jnp.sum(p, axis=0, keepdims=True)
                acc = acc * shrink + dot(vw_ref[at, lanes[pair]], p.astype(BF), TN)
                new.append((best, total, acc))
            return tuple(new)

        start = (jnp.full((1, 192), NEG, F32), jnp.zeros((1, 192), F32), jnp.zeros((LANES, 192), F32))
        done = lax.fori_loop(first_ref[n], last_ref[n], chunk, (start,) * len(heads))
        for pair in range(PAIRS):
            outs = []
            for side in range(2):
                top, total, acc = done[2 * pair + side]
                outs.append(acc * (1.0 / total))
                total_ref[pair, n, side : side + 1, :] = top + jnp.log(total)
            both = jnp.concatenate([outs[0][:64], outs[1][64:]], axis=0)
            out_ref[rows, lanes[pair]] = both.T.astype(BF)


def attend(q, k, v, around, qlab, klab, first, last):
    count, width = q.shape
    window = -(-3 * count // CHUNK) * CHUNK
    block = pl.BlockSpec((count, WIDE), lambda p, *_: (0, p))
    stats = pl.BlockSpec((PAIRS, 3, 2, 192), lambda p, *_: (p, 0, 0, 0))
    return pl.pallas_call(
        attend_kernel,
        out_shape=(
            jax.ShapeDtypeStruct(q.shape, BF),
            jax.ShapeDtypeStruct((width // LANES, 3, 2, 192), F32),
        ),
        grid_spec=pltpu.PrefetchScalarGridSpec(
            num_scalar_prefetch=2,
            grid=(width // WIDE,),
            in_specs=[block] * 7
            + [
                pl.BlockSpec(klab.shape, lambda p, *_: (0, 0)),
                pl.BlockSpec(qlab.shape, lambda p, *_: (0, 0, 0)),
            ],
            out_specs=(block, stats),
            scratch_shapes=[pltpu.VMEM((window, WIDE), BF), pltpu.VMEM((window, WIDE), BF)],
        ),
        **conv_params(40_000_000 * width, 20_000_000),
    )(first, last, q, around[0], k, around[1], around[2], v, around[3], klab, qlab)


def attend_back_kernel(first_ref, last_ref, q_ref, kb_ref, k_ref, ka_ref, vb_ref, v_ref, va_ref,
                       do_ref, o_ref, total_ref, klab_ref, qlab_ref,
                       dq_ref, dk_ref, dv_ref, before_ref, after_ref,
                       kw_ref, vw_ref, dkw_ref, dvw_ref):
    count = q_ref.shape[0]
    fill_window(kw_ref, kb_ref, k_ref, ka_ref)
    fill_window(vw_ref, vb_ref, v_ref, va_ref)
    dkw_ref[...] = jnp.zeros_like(dkw_ref)
    dvw_ref[...] = jnp.zeros_like(dvw_ref)
    heads = [(pair, side) for pair in range(PAIRS) for side in range(2)]
    lanes = [slice(pair * LANES, (pair + 1) * LANES) for pair in range(PAIRS)]
    for n in range(3):
        rows = slice(n * 192, (n + 1) * 192)
        q = q_ref[rows, :] * jnp.asarray(0.125, BF)
        do = do_ref[rows, :]
        halves = [lane_half((192, LANES), side) for side in range(2)]
        q_half = [jnp.where(halves[s], q[:, lanes[p]], jnp.zeros((), BF)) for p, s in heads]
        do_half = [jnp.where(halves[s], do[:, lanes[p]], jnp.zeros((), BF)) for p, s in heads]
        q_lab = qlab_ref[n, 0:1, :]
        flow = do.astype(F32) * o_ref[rows, :].astype(F32)
        delta = []
        for p in range(PAIRS):
            turned = flow[:, lanes[p]].T
            delta += [jnp.sum(turned[s * 64 : s * 64 + 64], axis=0, keepdims=True) for s in range(2)]

        def chunk(c, carry):
            at = pl.ds(pl.multiple_of(c * CHUNK, CHUNK), CHUNK)
            same = klab_ref[at, 0:1] == q_lab
            kcs = [kw_ref[at, lanes[pair]] for pair in range(PAIRS)]
            vcs = [vw_ref[at, lanes[pair]] for pair in range(PAIRS)]
            scores = [dot(kcs[p], q_half[i], NT) for i, (p, s) in enumerate(heads)]
            dps = [dot(vcs[p], do_half[i], NT) for i, (p, s) in enumerate(heads)]
            ps, dss = [], []
            for i, (p, s) in enumerate(heads):
                raised = jnp.where(same, scores[i] - total_ref[p, n, s : s + 1, :], NEG)
                ps.append(jnp.exp(raised))
            for i, (p, s) in enumerate(heads):
                dss.append((ps[i] * (dps[i] - delta[i])).astype(BF))
            low = [item.astype(BF) for item in ps]
            dqs = []
            for p in range(PAIRS):
                e, o = 2 * p, 2 * p + 1
                dvw_ref[at, lanes[p]] += dot(low[e], do_half[e], NN) + dot(low[o], do_half[o], NN)
                dkw_ref[at, lanes[p]] += dot(dss[e], q_half[e], NN) + dot(dss[o], q_half[o], NN)
                two = [dot(dss[e], kcs[p], TN), dot(dss[o], kcs[p], TN)]
                dqs.append(carry[p] + jnp.where(lane_half((192, LANES), 0), two[0], two[1]))
            return tuple(dqs)

        dqs = lax.fori_loop(
            first_ref[n], last_ref[n], chunk, tuple(jnp.zeros((192, LANES), F32) for _ in range(PAIRS))
        )
        for pair in range(PAIRS):
            dq_ref[rows, lanes[pair]] = (dqs[pair] * 0.125).astype(BF)
    dk_ref[...] = dkw_ref[count : 2 * count, :]
    dv_ref[...] = dvw_ref[count : 2 * count, :]
    before_ref[0] = dkw_ref[0:count, :].astype(BF)
    before_ref[1] = dvw_ref[0:count, :].astype(BF)
    after_ref[0] = dkw_ref[2 * count : 3 * count, :].astype(BF)
    after_ref[1] = dvw_ref[2 * count : 3 * count, :].astype(BF)


def attend_back(q, k, v, around, grad, out, total, qlab, klab, first, last):
    count, width = q.shape
    window = -(-3 * count // CHUNK) * CHUNK
    block = pl.BlockSpec((count, WIDE), lambda p, *_: (0, p))
    stats = pl.BlockSpec((PAIRS, 3, 2, 192), lambda p, *_: (p, 0, 0, 0))
    pair = pl.BlockSpec((2, count, WIDE), lambda p, *_: (0, 0, p))
    return pl.pallas_call(
        attend_back_kernel,
        out_shape=(
            jax.ShapeDtypeStruct(q.shape, BF),
            jax.ShapeDtypeStruct(q.shape, F32),
            jax.ShapeDtypeStruct(q.shape, F32),
            jax.ShapeDtypeStruct((2, count, width), BF),
            jax.ShapeDtypeStruct((2, count, width), BF),
        ),
        grid_spec=pltpu.PrefetchScalarGridSpec(
            num_scalar_prefetch=2,
            grid=(width // WIDE,),
            in_specs=[block] * 9
            + [
                stats,
                pl.BlockSpec(klab.shape, lambda p, *_: (0, 0)),
                pl.BlockSpec(qlab.shape, lambda p, *_: (0, 0, 0)),
            ],
            out_specs=(block, block, block, pair, pair),
            scratch_shapes=[
                pltpu.VMEM((window, WIDE), BF),
                pltpu.VMEM((window, WIDE), BF),
                pltpu.VMEM((window, WIDE), F32),
                pltpu.VMEM((window, WIDE), F32),
            ],
        ),
        **conv_params(55_000_000 * width, 20_000_000),
    )(first, last, q, around[0], k, around[1], around[2], v, around[3], grad, out, total, klab, qlab)


def on_device(
    lo_in,
    hi_in,
    image_ids,
    cn_kernel,
    cn_gain,
    cn_w1,
    cn_w2,
    cn_scale,
    ad_proj,
    ad_kernel,
    gate_w1,
    gate_w2,
    ln1_gain,
    qkv,
    out_proj,
    ln2_gain,
    fc1,
    fc2,
    d_lo_out,
    d_hi_out,
):
    micro_count, row_count, col_count, d_shard = lo_in.shape
    hi_rows = hi_in.shape[1]
    hi_cols = HCOLS
    c_shard = hi_in.shape[3] // hi_cols
    d_own, c_own = 2 * d_shard, 2 * c_shard
    tok_count = row_count * col_count
    pix_count = hi_rows * hi_cols
    mine = lax.axis_index("mb")
    row_start = lax.axis_index(TILE) * row_count
    head_count = d_own // HDIM

    fast = c_shard % LANES == 0 and lax.axis_size("tp") == 1
    hi_raw = hi_in.reshape(2, hi_rows, hi_cols * c_shard)
    hi_own, hi_other = swap_micro(hi_raw)
    up, down = rim_pair(hi_raw, RIM, 1)
    own_rims, other_rims = swap_micro(jnp.stack([up, down], axis=1))
    hid_shard, gh_shard, ff_shard = cn_w1.shape[1], gate_w1.shape[1], fc1.shape[1]
    mlp = gather_all(jnp.concatenate([cn_w1, cn_w2.T, ad_proj, gate_w1], axis=1))
    def apply(left, pair):
        return jnp.concatenate([matmul(left, pair[0]), matmul(left, pair[1])], axis=1)

    def apply_t(left, pair):
        width = pair[0].shape[1]
        return matmul_nt(left[:, :width], pair[0]) + matmul_nt(left[:, width:], pair[1])

    def cols(values):
        width = values.shape[1] // 2
        return [values[:, :width], values[:, width:]]

    canvas_ids = lax.dynamic_index_in_dim(image_ids, mine, 0, keepdims=False)
    small_ids = row_labels(canvas_ids, row_start, row_count, 1)
    lo_mid = small_ids[1 : 1 + row_count]
    hi_ids = row_labels(jnp.repeat(canvas_ids, 2), 2 * row_start, hi_rows, 3)
    hi_mid = hi_ids[3 : 3 + hi_rows]

    def both_shards(shard, axis):
        return in_order(shard, lax.ppermute(shard, "mb", SWAP), axis)

    other_kernel = lax.ppermute(cn_kernel, "mb", SWAP)
    conv_taps = in_order(cn_kernel, other_kernel, 1)

    own_place = mine.reshape(1).astype(jnp.int32)
    other_place = 1 - own_place
    seen = jnp.stack([(hi_ids[a : a + hi_rows] == hi_mid).astype(F32) for a in range(7)])
    mask = jnp.broadcast_to(seen[:, :, None], (7, hi_rows, LANES))
    own_taps, other_taps = cn_kernel.astype(F32), other_kernel.astype(F32)

    def natural(own, other):
        shape = (-1, hi_cols, c_shard)
        return in_order(own.reshape(shape), other.reshape(shape), 2)

    if fast:
        conv_flat = conv_forward(hi_own, *own_rims, own_taps, mask, own_place)
        conv_flat = conv_forward(hi_other, *other_rims, other_taps, mask, other_place, conv_flat)
    else:
        hi_field = natural(hi_own, hi_other)
        hi_pad = jnp.concatenate(
            [
                natural(own_rims[0], other_rims[0])[-3:],
                hi_field,
                natural(own_rims[1], other_rims[1])[:3],
            ]
        )
        conv_low = depthwise(hi_pad, conv_taps, hi_ids, hi_mid, 7, False).astype(BF)
        conv_flat = conv_low.transpose(1, 0, 2).reshape(pix_count, c_own)
    conv_full = features(conv_flat)
    normed, norm_pull = jax.vjp(layer_norm, conv_full.astype(F32), cn_gain.astype(F32))
    normed_low, mlp, gate_w2 = together(normed.astype(BF), mlp, gate_w2)
    mlp_in = [mlp[g, :, :hid_shard] for g in range(2)]
    mlp_out = [mlp[g, :, hid_shard : 2 * hid_shard] for g in range(2)]
    ad_matrix = [mlp[g, :, 2 * hid_shard : 2 * hid_shard + d_shard] for g in range(2)]
    gate_in = [mlp[g, :, 2 * hid_shard + d_shard :] for g in range(2)]
    vit = gather_all(
        jnp.concatenate(
            [
                gate_w2.T,
                qkv[0],
                qkv[1],
                qkv[2],
                out_proj.T,
                fc1,
                fc2.T,
            ],
            axis=1,
        )
    )
    cuts = np.cumsum([0, gh_shard, d_shard, d_shard, d_shard, d_shard, ff_shard, ff_shard])
    gate_out, q_w, k_w, v_w, out_w, ff_in, ff_out = [
        [vit[g, :, int(cuts[i]) : int(cuts[i + 1])] for g in range(2)] for i in range(7)
    ]

    inner_act, inner_slope = zip(*[gelu_pair(matmul(normed_low, mlp_in[g])) for g in range(2)])
    lo_in, d_lo_out, cn_scale, ad_kernel, first_act = together(
        lo_in, d_lo_out, cn_scale, ad_kernel, inner_act[0]
    )
    inner_act = (first_act, inner_act[1])
    lo_low = in_order(*swap_micro(lo_in.reshape(2, tok_count, d_shard)), 1)
    lo_field = lo_low.astype(F32)
    ad_taps = both_shards(ad_kernel, 1)
    hi_scale = both_shards(cn_scale, 0).astype(F32)
    branch = partial_sums(
        matmul_nt(inner_act[0], mlp_out[0]) + matmul_nt(inner_act[1], mlp_out[1])
    )
    if fast:
        hi_mine, hi_sent, pooled = join_branch(branch, hi_scale[None], hi_own, hi_other, own_place)
        pooled = pooled.transpose(1, 0, 2)
    else:
        branch_rows = branch.reshape(hi_cols, hi_rows, c_own).transpose(1, 0, 2)
        hi_sum = hi_field.astype(F32) + hi_scale * branch_rows
        pooled = jnp.mean(hi_sum.reshape(row_count, 2, col_count, 2, c_own), axis=(1, 3))
    pooled_full = features(pooled.reshape(tok_count, c_own).astype(BF))
    pooled_full, d_hi_out = together(pooled_full, d_hi_out)
    cot_own, cot_other = swap_micro(d_hi_out.reshape(2, hi_rows, hi_cols * c_shard))
    proj_low = apply(pooled_full, ad_matrix).astype(BF)
    proj_pad = rim_rows(proj_low.reshape(row_count, col_count, d_own), 1)
    local_conv = depthwise(proj_pad, ad_taps, small_ids, lo_mid, 3, False).reshape(
        tok_count, d_own
    )
    gate_hidden, gate_slope = gelu_pair(apply(pooled_full, gate_in))
    gate_val = jnp.tanh(partial_sums(apply_t(gate_hidden, gate_out)))
    mixed_one = lo_field + gate_val * local_conv
    mixed_full = features(mixed_one.astype(BF))
    norm_one, first_pull = jax.vjp(layer_norm, mixed_full.astype(F32), ln1_gain.astype(F32))
    norm_low = norm_one.astype(BF)
    key_rows = apply(norm_low, k_w).astype(BF)
    value_rows = apply(norm_low, v_w).astype(BF)
    query_in, key_rows, value_rows = together(norm_low, key_rows, value_rows)
    queries = apply(query_in, q_w).astype(BF)
    around = rim_pair(key_rows, tok_count, 0) + rim_pair(value_rows, tok_count, 0)
    near = row_labels(canvas_ids, row_start, row_count, row_count)
    key_tok = jnp.repeat(near, col_count)
    window = -(-3 * tok_count // CHUNK) * CHUNK
    key_tok = jnp.pad(key_tok, (0, window - 3 * tok_count), constant_values=-2)
    key_lab = jnp.broadcast_to(key_tok[:, None], (window, LANES))
    query_lab = jnp.broadcast_to(jnp.repeat(lo_mid, col_count).reshape(3, 1, 192), (3, 8, 192))
    edge = jnp.arange(3 * row_count)
    first_row = jnp.min(jnp.where(near[None] == lo_mid[::8][:, None], edge, 3 * row_count), axis=1)
    last_row = jnp.max(jnp.where(near[None] == lo_mid[7::8][:, None], edge, -1), axis=1) + 1
    first = (first_row * col_count // CHUNK).astype(jnp.int32)
    last = ((last_row * col_count + CHUNK - 1) // CHUNK).astype(jnp.int32)
    attended, log_total = attend(
        queries, key_rows, value_rows, around, query_lab, key_lab, first, last
    )
    mixed_two = mixed_one + partial_sums(apply_t(attended, out_w))
    if fast:
        hi_got = lax.ppermute(hi_sent, "mb", SWAP)
        mixed_two, hi_got = together(mixed_two, hi_got)
    mixed2_full = features(mixed_two.astype(BF))
    norm_two, second_pull = jax.vjp(layer_norm, mixed2_full.astype(F32), ln2_gain.astype(F32))
    norm2_low = norm_two.astype(BF)
    ff_hidden, ff_slope = gelu_pair(apply(norm2_low, ff_in))
    lo_result = (mixed_two + partial_sums(apply_t(ff_hidden, ff_out))).astype(BF)

    grad_low = in_order(*swap_micro(d_lo_out.reshape(2, tok_count, d_shard)), 1)
    grad_out = grad_low.astype(F32)
    ff_grad_full = features(grad_low)
    ff_pre_grad = (apply(ff_grad_full, ff_out) * ff_slope.astype(F32)).astype(BF)
    second_grad = partial_sums(apply_t(ff_pre_grad, ff_in)).astype(BF)
    back_two, grad_ln2 = second_pull(features(second_grad).astype(F32))
    p_ff = stacked_grads([norm2_low, ff_grad_full], [ff_pre_grad, ff_hidden])
    grad_two, cot_other = together(grad_out + own_slice(back_two), cot_other)
    att_grad_full = features(grad_two.astype(BF))
    att_grad = apply(att_grad_full, out_w).astype(BF)
    query_grad, key_own, value_own, to_before, to_after = attend_back(
        queries, key_rows, value_rows, around, att_grad, attended, log_total, query_lab, key_lab, first, last
    )
    devices = tile_count()
    steps = [(i, i + 1) for i in range(devices - 1)]
    from_before = lax.ppermute(to_after, TILE, steps)
    from_after = lax.ppermute(to_before, TILE, [(j, i) for i, j in steps])
    p_ff, lo_result, from_before, from_after = together(p_ff, lo_result, from_before, from_after)
    s_ff = reduce_tiles(p_ff)
    key_grad, value_grad = [
        (own + from_before[i].astype(F32) + from_after[i].astype(F32)).astype(BF)
        for i, own in enumerate((key_own, value_own))
    ]
    first_grad = partial_sums(
        apply_t(query_grad, q_w) + apply_t(key_grad, k_w) + apply_t(value_grad, v_w)
    ).astype(BF)
    back_one, grad_ln1 = first_pull(features(first_grad).astype(F32))
    grad_one = grad_two + own_slice(back_one)
    gate_pre_grad = (grad_one * local_conv * (1.0 - gate_val * gate_val)).astype(BF)
    gate_grad_full = features(gate_pre_grad)
    p_att = stacked_grads(
        [gate_grad_full, norm_low, att_grad_full],
        [gate_hidden, jnp.concatenate([query_grad, key_grad, value_grad], axis=1), attended],
    )
    hidden_grad = (apply(gate_grad_full, gate_out) * gate_slope.astype(F32)).astype(BF)
    local_grad = (grad_one * gate_val).astype(BF).reshape(row_count, col_count, d_own)
    local_pad = rim_rows(local_grad, 1)
    proj_grad = (
        depthwise(local_pad, ad_taps, small_ids, lo_mid, 3, True)
        .reshape(tok_count, d_own)
        .astype(BF)
    )
    grad_ad_kernel = tap_grads(proj_pad, local_grad, small_ids, lo_mid, 3)
    p_ad = matmul_tn(pooled_full, jnp.concatenate([proj_grad, hidden_grad], axis=1)).astype(BF)
    pooled_grad = partial_sums(apply_t(hidden_grad, gate_in) + apply_t(proj_grad, ad_matrix))
    pooled_grad, p_att, p_ad = together(pooled_grad, p_att, p_ad)
    s_att, s_ad = reduce_tiles(p_att), reduce_tiles(p_ad)
    pool_cols = pooled_grad.reshape(row_count, col_count, c_own).transpose(1, 0, 2)
    if fast:
        scaled_grad, scale_parts = scaled_grads(
            pool_cols, branch, hi_scale[None], cot_own, cot_other, own_place
        )
        grad_scale = jnp.sum(scale_parts, axis=0)
    else:
        spread_grad = jnp.repeat(jnp.repeat(pool_cols.transpose(1, 0, 2) * 0.25, 2, 0), 2, 1)
        hi_grad = natural(cot_own, cot_other).astype(F32) + spread_grad
        grad_cols = hi_grad.transpose(1, 0, 2).reshape(pix_count, c_own)
        grad_scale = jnp.sum(grad_cols * branch, axis=0)
        scaled_grad = (grad_cols * hi_scale).astype(BF)
    branch_full = lax.optimization_barrier(features(scaled_grad))
    first = mine == 0
    p_w2 = [matmul_tn(branch_full, act).astype(BF) for act in inner_act]
    branch_full, *p_w2 = together(branch_full, *p_w2)
    s_w2 = [reduce_tiles(item) for item in p_w2]
    grad_first = (matmul(branch_full, mlp_out[0]) * inner_slope[0].astype(F32)).astype(BF)
    w1_first = matmul_tn(normed_low, grad_first).astype(BF)
    branch_full, w1_first = together(branch_full, w1_first)
    core_first = core_sum(w1_first)
    grad_second = (matmul(branch_full, mlp_out[1]) * inner_slope[1].astype(F32)).astype(BF)
    w1_second = matmul_tn(normed_low, grad_second).astype(BF)
    grad_second, w1_second, s_ff = together(grad_second, w1_second, s_ff)
    core_second = core_sum(w1_second)
    normed_part = matmul_nt(grad_first, mlp_in[0])
    normed_part, core_first, core_second = together(normed_part, core_first, core_second)
    w1_own = jnp.where(first, core_first, core_second)
    w1_sent = jnp.where(first, core_second, core_first)
    piece = w1_sent.shape[1] // (3 * LANES) * LANES
    w1_got = [
        lax.ppermute(item, "mb", SWAP) for item in (w1_sent[:, :piece], w1_sent[:, piece:])
    ]
    normed_grad = partial_sums(normed_part + matmul_nt(grad_second, mlp_in[1])).astype(BF)
    normed_grad, w1_got[0] = together(normed_grad, w1_got[0])
    back_conv, grad_cn_gain = norm_pull(features(normed_grad).astype(F32))
    conv_grad = own_slice(back_conv).astype(BF)
    conv_cols = conv_grad.reshape(hi_cols, hi_rows, c_own)
    grad_up, grad_down = rim_pair(conv_cols, RIM, 1)
    if fast:
        ghi_sent, taps_other = conv_backward(
            conv_grad, grad_up, grad_down, hi_other, cot_other, pool_cols, other_taps, mask, other_place, 1, BF
        )
        conv_grad, ghi_sent, w1_got[1] = together(conv_grad, ghi_sent, w1_got[1])
        w1_sum = add_low(w1_own, jnp.concatenate(w1_got, axis=1))
        ghi_mine, taps_own = conv_backward(
            conv_grad, grad_up, grad_down, hi_own, cot_own, pool_cols, own_taps, mask, own_place, 2, F32
        )
        tap_sums = jnp.concatenate([taps_own, taps_other])
    else:
        conv_grad = conv_cols.transpose(1, 0, 2)
        conv_pad = jnp.concatenate(
            [grad_up.transpose(1, 0, 2)[-3:], conv_grad, grad_down.transpose(1, 0, 2)[:3]]
        )
        hi_back = hi_grad + depthwise(conv_pad, conv_taps, hi_ids, hi_mid, 7, True)
        grad_cn_kernel = tap_grads(hi_pad, conv_grad, hi_ids, hi_mid, 7)
        tap_sums = jnp.concatenate(halves(grad_cn_kernel))
        w1_sum = add_low(w1_own, jnp.concatenate(w1_got, axis=1))

    chips = lax.axis_size("chip")
    w1_sum = w1_sum.reshape(chips, w1_sum.shape[0] // chips, w1_sum.shape[1])
    if chips & (chips - 1):
        w1_sum = lax.psum_scatter(w1_sum, "chip", scatter_dimension=0, tiled=True)
    else:
        own, got = chip_step(w1_sum, 1)
        tap_sums, got, s_att, s_ad = together(tap_sums, got, s_att, s_ad)
        w1_sum, bit = add_low(own, got), 2
        while bit < chips:
            w1_sum, bit = add_low(*chip_step(w1_sum, bit)), 2 * bit

    own_terms, sent_terms = zip(*[halves(item) for item in (grad_scale, grad_ad_kernel)])
    others = (*own_terms, *sent_terms, grad_cn_gain, grad_ln1, grad_ln2)
    sizes = [int(item) for item in np.cumsum([0] + [item.size for item in others])]
    flat = jnp.concatenate([item.reshape(-1) for item in others])
    flat = jnp.pad(flat, (0, -sizes[-1] % (8 * c_shard))).reshape(-1, c_shard)
    tap_rows = tap_sums.shape[0] // 2
    small = jnp.concatenate([tap_sums, flat])
    devices = tile_count()
    bits = [1 << i for i in range(devices.bit_length() - 1)]
    doubling = devices == 1 << len(bits)
    small = sum_tiles(small, bits[:-1]) if doubling else lax.psum(small, TILE)
    if fast:
        ghi_got = lax.ppermute(ghi_sent, "mb", SWAP)
        small, ghi_got, *s_w2 = together(small, ghi_got, *s_w2)
    if doubling:
        small = sum_tiles(small, bits[-1:])
    got = lax.ppermute(small[tap_rows:], "mb", SWAP)
    g_kernel = (small[:tap_rows] + got[:tap_rows])[: cn_kernel.shape[0]]
    flat, got = small[2 * tap_rows :].reshape(-1), got[tap_rows:].reshape(-1)
    pieces = [
        (flat[sizes[i] : sizes[i + 1]] + got[sizes[j] : sizes[j + 1]]).reshape(others[i].shape)
        for i, j in ((0, 2), (1, 3), (4, 4), (5, 5), (6, 6))
    ]
    g_scale, g_taps, *gain_sums = pieces

    def leave(values, kind):
        own, sent = halves(values)
        other = lax.ppermute(sent.astype(BF), "mb", SWAP)
        return both_micro(own.astype(kind), other.astype(kind))

    lo_stack = leave(lo_result.reshape(row_count, col_count, d_own), BF)
    if fast:
        hi_stack, ghi_stack = [
            lax.dynamic_update_slice_in_dim(stack, got.astype(stack.dtype), 1 - mine, 0)
            for stack, got in ((hi_mine, hi_got), (ghi_mine, ghi_got))
        ]
    else:
        hi_stack = leave(hi_sum, BF)
        ghi_stack = leave(hi_back, F32)
    glo_stack = leave(grad_one.reshape(row_count, col_count, d_own), F32)

    (g_w2,) = settle(jnp.concatenate(s_w2, axis=1), (hid_shard,))
    hi_stack = hi_stack.reshape(2, hi_rows, 1, hi_cols * c_shard)
    ghi_stack, w1_sum = together(ghi_stack.reshape(2, hi_rows, -1, 128), w1_sum)
    ghi_stack = ghi_stack.reshape(2, hi_rows, 1, hi_cols * c_shard)
    g_w1 = all_columns(w1_sum.reshape(-1, w1_sum.shape[-1])).astype(F32)
    g_fc1, g_fc2 = settle(s_ff, (ff_shard, ff_shard))
    g_gate_w2, g_q, g_k, g_v, g_out = settle(s_att, (gh_shard, d_shard, d_shard, d_shard, d_shard))
    g_ad, g_gate_w1 = settle(s_ad, (d_shard, gh_shard))

    return (
        lo_stack,
        hi_stack,
        glo_stack,
        ghi_stack,
        g_kernel,
        gain_sums[0],
        g_w1,
        g_w2.T,
        g_scale,
        g_ad,
        g_taps,
        g_gate_w1,
        g_gate_w2.T,
        gain_sums[1],
        jnp.stack([g_q, g_k, g_v]),
        g_out.T,
        gain_sums[2],
        g_fc1,
        g_fc2.T,
    )


def solution(mesh):
    tiles, mps = mesh.shape["tile"], mesh.shape["mp"]
    fine = Mesh(mesh.devices.reshape(tiles // 2, 2, 2, mps // 2), (*TILE, "mb", "tp"))
    mp = ("mb", "tp")
    in_specs = (
        P(None, TILE, None, mp),
        P(None, TILE, mp, None),
        P(),
        P(None, mp),
        P(),
        P(TILE, mp),
        P(mp, TILE),
        P(mp),
        P(TILE, mp),
        P(None, mp),
        P(TILE, mp),
        P(mp, TILE),
        P(),
        P(None, TILE, mp),
        P(mp, TILE),
        P(),
        P(TILE, mp),
        P(mp, TILE),
        P(None, TILE, None, mp),
        P(None, TILE, mp, None),
    )
    out_specs = (
        P(None, TILE, None, mp),
        P(None, TILE, mp, None),
        P(None, TILE, None, mp),
        P(None, TILE, mp, None),
        P(None, mp),
        P(),
        P(TILE, mp),
        P(mp, TILE),
        P(mp),
        P(TILE, mp),
        P(None, mp),
        P(TILE, mp),
        P(mp, TILE),
        P(),
        P(None, TILE, mp),
        P(mp, TILE),
        P(),
        P(TILE, mp),
        P(mp, TILE),
    )
    return jax.shard_map(
        on_device, mesh=fine, in_specs=in_specs, out_specs=out_specs, check_vma=False
    )
```
